256 devices in a mesh: gx: 16 (over z_lo, x), gy: 4 (over z_hi, core), gz: 4 (over y).
Axes of the slice: x: 4, y: 4, z: 8 (z_hi: 2, z_lo: 4; z = z_hi * 4 + z_lo), core: 2. Of those that a mesh axis runs over, the one named last changes fastest.
Arguments:
- residual: float32 [128, 128, 8192], P('gy', 'gz', 'gx'), may hold values from -11 to 11, as said below
Outputs:
- correction: float32 [128, 128, 8192], P('gy', 'gz', 'gx')
The draws below stay inside these ranges and needn't reach their ends.
Inputs may be any that keep to these rules, and one draw needn't show every extreme that they name: `residual`: independent from node to node.
All inputs are finite; a program needn't handle non-finite values.
Results may differ from the reference program's by a relative error of at most 0.0001.
Values sent between devices are 32-bit elements; how exact they have to be, the bound alone decides.
A program may use at most 128 MiB of HBM per device.

```python
import jax
import jax.numpy as jnp
import numpy as np
from jax import lax

ORDER = 7
MID_ORDER = 3
SMOOTH_STEPS = 2
COARSE_STEPS = 4
LINE_NODES = 8
GLOBAL_X = 1024
GLOBAL_Y = 16
GLOBAL_Z = 16


def draw_residual(key, part):
    key = jax.random.fold_in(key, 17)
    first_key, second_key = jax.random.split(key)
    shape_all = (GLOBAL_Y * LINE_NODES, GLOBAL_Z * LINE_NODES, GLOBAL_X * LINE_NODES)
    spread = jnp.exp(jax.random.uniform(second_key, shape_all, jnp.float32, -1.0, 1.0))
    roughness = jnp.clip(jax.random.normal(first_key, shape_all, jnp.float32), -4.0, 4.0)
    return roughness * spread


def setup_inputs(seed: int = 0) -> dict:
    streams_of = jax.random.split(jax.random.key(seed), 2)
    residual = draw_residual(jax.random.fold_in(streams_of[1], 71), 0)
    return {"residual": residual}


HIGHEST_PREC = lax.Precision.HIGHEST


def legendre_pair(degree, points):
    previous = np.ones(points.shape)
    current = points.copy()
    for level in range(1, degree):
        following = ((2 * level + 1) * points * current - level * previous) / (level + 1)
        previous = current
        current = following
    return current, previous


def gll_table(degree):
    points = np.cos(np.pi * np.arange(degree + 1) / degree)
    for sweep in range(100):
        current, previous = legendre_pair(degree, points)
        points = points - (points * current - previous) / ((degree + 1) * current)
    points = points[::-1].copy()
    current, previous = legendre_pair(degree, points)
    weights = 2.0 / (degree * (degree + 1) * current ** 2)
    return points, weights


def lagrange_matrix(targets, points):
    point_count = len(points)
    matrix = np.ones((len(targets), point_count))
    for column in range(point_count):
        for partner in range(point_count):
            if partner != column:
                matrix[:, column] *= (targets - points[partner]) / (points[column] - points[partner])
    return matrix


def line_stiffness(degree):
    points, weights = gll_table(degree)
    point_count = len(points)
    barycentric = np.array([1.0 / np.prod([points[column] - points[partner] for partner in range(point_count) if partner != column]) for column in range(point_count)])
    derivative = np.zeros((point_count, point_count))
    for target in range(point_count):
        for column in range(point_count):
            if target != column:
                derivative[target, column] = barycentric[column] / barycentric[target] / (points[target] - points[column])
        derivative[target, target] = -np.sum(derivative[target])
    return derivative.T @ (weights[:, None] * derivative), weights


def assembled_patterns(degree):
    stiffness, weights = line_stiffness(degree)
    indices = np.arange(len(weights))
    diag_pat = stiffness[indices, indices].copy()
    weight_pat = weights.copy()
    row_pat = np.abs(stiffness).sum(axis=1)
    for pattern in (diag_pat, weight_pat, row_pat):
        shared = pattern[0] + pattern[-1]
        pattern[0] = shared
        pattern[-1] = shared
    return diag_pat, weight_pat, row_pat


def three_terms(special, weight_pat):
    return (special[:, None, None] * weight_pat[None, :, None] * weight_pat[None, None, :]
            + weight_pat[:, None, None] * special[None, :, None] * weight_pat[None, None, :]
            + weight_pat[:, None, None] * weight_pat[None, :, None] * special[None, None, :])


def chebyshev_bound(degree):
    diag_pat, weight_pat, row_pat = assembled_patterns(degree)
    return float(np.max(three_terms(row_pat, weight_pat) / three_terms(diag_pat, weight_pat)))


def pattern_vector(pattern, length):
    return jnp.asarray(np.tile(pattern, length // len(pattern)), jnp.float32)


def inverse_diagonal(target_shape, degree):
    diag_pat, weight_pat, row_pat = assembled_patterns(degree)
    diag_a = pattern_vector(diag_pat, target_shape[0])[:, None, None]
    diag_b = pattern_vector(diag_pat, target_shape[1])[None, :, None]
    diag_p = pattern_vector(diag_pat, target_shape[2])[None, None, :]
    weight_a = pattern_vector(weight_pat, target_shape[0])[:, None, None]
    weight_b = pattern_vector(weight_pat, target_shape[1])[None, :, None]
    weight_p = pattern_vector(weight_pat, target_shape[2])[None, None, :]
    total = diag_a * weight_b * weight_p + weight_a * diag_b * weight_p + weight_a * weight_b * diag_p
    return 1.0 / total


def wall_mask(length, position, parts):
    rows = jnp.arange(length)
    start_wall = (rows == 0) & (position == 0)
    end_wall = (rows == length - 1) & (position == parts - 1)
    return jnp.where(start_wall | end_wall, 0.0, 1.0).astype(jnp.float32)


def edge_masks(length, direction, degree):
    position = jnp.arange(length) % (degree + 1)
    target = [1, 1, 1]
    target[direction] = length
    head_mask = (position == 0).astype(jnp.float32).reshape(target)
    tail_mask = (position == degree).astype(jnp.float32).reshape(target)
    return head_mask, tail_mask


def local_stiffness(vector, degree):
    per_elem = degree + 1
    stiffness_np, weights_np = line_stiffness(degree)
    stiffness = jnp.asarray(stiffness_np, jnp.float32)
    size_a, size_b, size_pipe = vector.shape
    weight_a = pattern_vector(weights_np, size_a)[:, None, None]
    weight_b = pattern_vector(weights_np, size_b)[None, :, None]
    weight_p = pattern_vector(weights_np, size_pipe)[None, None, :]
    along_a = jnp.einsum('ajbc,Jj->aJbc', vector.reshape(size_a // per_elem, per_elem, size_b, size_pipe), stiffness, precision=HIGHEST_PREC).reshape(vector.shape)
    along_b = jnp.einsum('abjc,Jj->abJc', vector.reshape(size_a, size_b // per_elem, per_elem, size_pipe), stiffness, precision=HIGHEST_PREC).reshape(vector.shape)
    along_pipe = jnp.einsum('abcj,Jj->abcJ', vector.reshape(size_a, size_b, size_pipe // per_elem, per_elem), stiffness, precision=HIGHEST_PREC).reshape(vector.shape)
    return along_a * weight_b * weight_p + along_b * weight_a * weight_p + along_pipe * weight_a * weight_b


def transfer(vector, matrix_np):
    matrix = jnp.asarray(matrix_np, jnp.float32)
    out_nodes, in_nodes = matrix_np.shape
    size_a, size_b, size_pipe = vector.shape
    moved = jnp.einsum('ajbc,Jj->aJbc', vector.reshape(size_a // in_nodes, in_nodes, size_b, size_pipe), matrix, precision=HIGHEST_PREC)
    size_a = size_a // in_nodes * out_nodes
    moved = moved.reshape(size_a, size_b, size_pipe)
    moved = jnp.einsum('abjc,Jj->abJc', moved.reshape(size_a, size_b // in_nodes, in_nodes, size_pipe), matrix, precision=HIGHEST_PREC)
    size_b = size_b // in_nodes * out_nodes
    moved = moved.reshape(size_a, size_b, size_pipe)
    moved = jnp.einsum('abcj,Jj->abcJ', moved.reshape(size_a, size_b, size_pipe // in_nodes, in_nodes), matrix, precision=HIGHEST_PREC)
    return moved.reshape(size_a, size_b, size_pipe // in_nodes * out_nodes)


def assemble_global(vector, degree):
    combined = vector
    for direction, periodic in ((2, True), (0, False), (1, False)):
        length = combined.shape[direction]
        if periodic:
            preceding = jnp.roll(combined, 1, axis=direction)
            following = jnp.roll(combined, -1, axis=direction)
        else:
            zero_slab = jnp.zeros_like(lax.slice_in_dim(combined, 0, 1, axis=direction))
            preceding = jnp.concatenate([zero_slab, lax.slice_in_dim(combined, 0, length - 1, axis=direction)], axis=direction)
            following = jnp.concatenate([lax.slice_in_dim(combined, 1, length, axis=direction), zero_slab], axis=direction)
        head_mask, tail_mask = edge_masks(length, direction, degree)
        combined = combined + head_mask * preceding + tail_mask * following
    wall = wall_mask(combined.shape[0], 0, 1)[:, None, None] * wall_mask(combined.shape[1], 0, 1)[None, :, None]
    return combined * wall


def chebyshev(local_residual, steps, degree, inverse_diag):
    upper_bound = chebyshev_bound(degree)
    lower_bound = upper_bound / 10.0
    center = 0.5 * (upper_bound + lower_bound)
    halfwidth = 0.5 * (upper_bound - lower_bound)
    scaled = center / halfwidth
    ratio_now = 1.0 / scaled
    assembled = assemble_global(local_residual, degree)
    update = inverse_diag * assembled / center
    solution = update
    for iteration in range(1, steps):
        local_residual = local_residual - local_stiffness(update, degree)
        assembled = assemble_global(local_residual, degree)
        ratio_next = 1.0 / (2.0 * scaled - ratio_now)
        update = (ratio_next * ratio_now) * update + (2.0 * ratio_next / halfwidth) * (inverse_diag * assembled)
        solution = solution + update
        ratio_now = ratio_next
    return solution, local_residual, update


def reference(residual):
    fine_points = gll_table(ORDER)[0]
    mid_points = gll_table(MID_ORDER)[0]
    low_points = gll_table(1)[0]
    lift_mid = lagrange_matrix(fine_points, mid_points)
    lift_low = lagrange_matrix(mid_points, low_points)
    fine_sol, fine_res, fine_last = chebyshev(residual, SMOOTH_STEPS, ORDER, inverse_diagonal(residual.shape, ORDER))
    fine_res = fine_res - local_stiffness(fine_last, ORDER)
    mid_rhs = transfer(fine_res, lift_mid.T)
    mid_inverse = inverse_diagonal(mid_rhs.shape, MID_ORDER)
    mid_sol, mid_res, mid_last = chebyshev(mid_rhs, SMOOTH_STEPS, MID_ORDER, mid_inverse)
    mid_res = mid_res - local_stiffness(mid_last, MID_ORDER)
    low_rhs = transfer(mid_res, lift_low.T)
    low_sol = chebyshev(low_rhs, COARSE_STEPS, 1, inverse_diagonal(low_rhs.shape, 1))[0]
    mid_lift = transfer(low_sol, lift_low)
    mid_res = mid_res - local_stiffness(mid_lift, MID_ORDER)
    mid_post = chebyshev(mid_res, SMOOTH_STEPS, MID_ORDER, mid_inverse)[0]
    mid_total = mid_sol + mid_lift + mid_post
    fine_lift = transfer(mid_total, lift_mid)
    fine_res = fine_res - local_stiffness(fine_lift, ORDER)
    fine_post = chebyshev(fine_res, SMOOTH_STEPS, ORDER, inverse_diagonal(residual.shape, ORDER))[0]
    return fine_sol + fine_lift + fine_post
```

```python
import itertools

import jax
import jax.numpy as jnp
import numpy as np
from jax import lax
from jax.experimental import pallas as pl
from jax.experimental.pallas import tpu as pltpu
from jax.sharding import PartitionSpec as P

ORDER = 7
MID_ORDER = 3
COARSE_STEPS = 4


def legendre_pair(degree, points):
    previous = np.ones(points.shape)
    current = points.copy()
    for level in range(1, degree):
        following = ((2 * level + 1) * points * current - level * previous) / (level + 1)
        previous = current
        current = following
    return (current, previous)


def gll_table(degree):
    points = np.cos(np.pi * np.arange(degree + 1) / degree)
    for sweep in range(100):
        current, previous = legendre_pair(degree, points)
        points = points - (points * current - previous) / ((degree + 1) * current)
    points = points[::-1].copy()
    current, previous = legendre_pair(degree, points)
    weights = 2.0 / (degree * (degree + 1) * current**2)
    return (points, weights)


def lagrange_matrix(targets, points):
    point_count = len(points)
    matrix = np.ones((len(targets), point_count))
    for column in range(point_count):
        for partner in range(point_count):
            if partner != column:
                matrix[:, column] *= (targets - points[partner]) / (
                    points[column] - points[partner]
                )
    return matrix


def line_stiffness(degree):
    points, weights = gll_table(degree)
    point_count = len(points)
    barycentric = np.array(
        [
            1.0
            / np.prod(
                [
                    points[column] - points[partner]
                    for partner in range(point_count)
                    if partner != column
                ]
            )
            for column in range(point_count)
        ]
    )
    derivative = np.zeros((point_count, point_count))
    for target in range(point_count):
        for column in range(point_count):
            if target != column:
                derivative[target, column] = (
                    barycentric[column] / barycentric[target] / (points[target] - points[column])
                )
        derivative[target, target] = -np.sum(derivative[target])
    return (derivative.T @ (weights[:, None] * derivative), weights)


def assembled_patterns(degree):
    stiffness, weights = line_stiffness(degree)
    indices = np.arange(len(weights))
    diag_pat = stiffness[indices, indices].copy()
    weight_pat = weights.copy()
    row_pat = np.abs(stiffness).sum(axis=1)
    for pattern in (diag_pat, weight_pat, row_pat):
        shared = pattern[0] + pattern[-1]
        pattern[0] = shared
        pattern[-1] = shared
    return (diag_pat, weight_pat, row_pat)


def three_terms(special, weight_pat):
    return (
        special[:, None, None] * weight_pat[None, :, None] * weight_pat[None, None, :]
        + weight_pat[:, None, None] * special[None, :, None] * weight_pat[None, None, :]
        + weight_pat[:, None, None] * weight_pat[None, :, None] * special[None, None, :]
    )


def chebyshev_bound(degree):
    diag_pat, weight_pat, row_pat = assembled_patterns(degree)
    return float(np.max(three_terms(row_pat, weight_pat) / three_terms(diag_pat, weight_pat)))


class Level:
    def __init__(self, q):
        stiffness, weights = line_stiffness(q)
        diag_pat, weight_pat, row_pat = assembled_patterns(q)
        self.q = self.n = q
        self.half = half = (q + 1) // 2
        self.mass = weight_pat
        self.gain = gain = stiffness / weight_pat[:, None]
        self.even = 0.5 * (gain[:half, :half] + gain[:half, ::-1][:, :half])
        self.odd = 0.5 * (gain[:half, :half] - gain[:half, ::-1][:, :half])
        self.alpha = diag_pat / weight_pat
        upper = chebyshev_bound(q)
        lower = upper / 10.0
        self.center = 0.5 * (upper + lower)
        self.halfwidth = 0.5 * (upper - lower)

    def inverse(self, a, b, c):
        return 1.0 / (self.alpha[a] + self.alpha[b] + self.alpha[c])

    def factors(self, steps):
        scaled = self.center / self.halfwidth
        ratio = 1.0 / scaled
        found = []
        for step in range(1, steps):
            following = 1.0 / (2.0 * scaled - ratio)
            found.append((following * ratio, 2.0 * following / self.halfwidth))
            ratio = following
        return found


FINE, MID, LOW = Level(ORDER), Level(MID_ORDER), Level(1)
ALL_DIMS = "abc"
SUBSETS = ("a", "b", "c", "ab", "ac", "bc", "abc")
TAB = 33
BLOCKS = [o for o in itertools.product((-1, 0, 1), repeat=3) if any(o)]


def table():
    rows = []
    for a in range(7):
        inverse = [FINE.inverse(a, b, c) for b in range(4) for c in range(4)]
        scale = [
            1.0 / (FINE.mass[a] * FINE.mass[b] * FINE.mass[c]) for b in range(4) for c in range(4)
        ]
        rows += inverse + scale + [FINE.gain[a, 7]]
    return np.asarray(rows, np.float32)


def combo(b, c):
    return min(b, 7 - b) * 4 + min(c, 7 - c)


def node(dim, m, i, k):
    return {"a": (m, i, k), "b": (i, m, k), "c": (i, k, m)}[dim]


def face_vregs(n, dim):
    return 1 if dim == "c" else n * -(-n // 4)


def plan():
    slots, size, count = {}, 0, 0

    def add(key, length):
        nonlocal size, count
        slots[key] = (size, length, count)
        size += length
        count += 1

    for name, n in (
        ("f1", 7), ("f2", 7), ("f3", 7), ("f4", 7),
        ("m1", 3), ("m2", 3), ("m4", 3),
    ):
        for dim in ALL_DIMS:
            for way in (1, -1):
                add((name, dim, way), face_vregs(n, dim))
    for name, n, way in (("S7", 7, 1), ("S3", 3, 1), ("S1", 1, 1), ("C3", 3, -1), ("C7", 7, -1)):
        for dims in SUBSETS:
            add((name, dims, way), face_vregs(n, dims) if len(dims) == 1 else n ** (3 - len(dims)))
    for offset in BLOCKS:
        add(offset, 1)
    return slots, -(-size // 8) * 8, count


SLOTS, BUF_VREGS, MESSAGES = plan()


def total(terms):
    out = None
    for term in terms:
        if term is not None:
            out = term if out is None else out + term
    return out


def mix(coefs, values):
    return total(
        None if abs(coef) < 1e-13 else float(coef) * value for coef, value in zip(coefs, values)
    )


def kernel(sizes, tab, x, out, tr, u, rho, d, xs, w1, w2, ha, pk, sbuf, rbuf, ssem, rsem):
    nx, ny, nz = sizes
    gx, gy, gz = lax.axis_index("gx"), lax.axis_index("gy"), lax.axis_index("gz")
    rows = lax.broadcasted_iota(jnp.int32, (8, 128), 0)
    lanes = lax.broadcasted_iota(jnp.int32, (8, 128), 1)
    odd_row, odd_lane = rows % 2 == 1, lanes % 2 == 1
    first = {"a": rows < 2, "b": (rows % 2 == 0) & (lanes % 2 == 0), "c": lanes < 2}
    last = {"a": rows >= 6, "b": odd_row & odd_lane, "c": lanes >= 126}
    wall_a = jnp.where(first["a"] & (gy == 0), 0.0, 1.0).astype(jnp.float32)
    wall_b = jnp.where(first["b"] & (gz == 0), 0.0, 1.0).astype(jnp.float32)

    def spin(v, row, lane):
        if row % 8:
            v = pltpu.roll(v, row % 8, 0)
        if lane % 128:
            v = pltpu.roll(v, lane % 128, 1)
        return v

    def up(dim, v):
        if dim == "a":
            return jnp.where(rows >= 2, spin(v, 2, 0), 0.0)
        if dim == "b":
            w = jnp.where(odd_lane, jnp.where(odd_row, spin(v, 1, 0), 0.0), v)
            return jnp.where(odd_lane, spin(w, 0, 1), spin(w, 0, -1))
        t = jnp.where(lanes < 8, spin(v, 0, 10), spin(v, 0, 8))
        return jnp.where(lanes < 2, 0.0, t)

    def down(dim, v):
        if dim == "a":
            return jnp.where(rows < 6, spin(v, -2, 0), 0.0)
        if dim == "b":
            w = jnp.where(odd_lane, v, jnp.where(odd_row, 0.0, spin(v, -1, 0)))
            return jnp.where(odd_lane, spin(w, 0, 1), spin(w, 0, -1))
        t = jnp.where(lanes >= 120, spin(v, 0, -10), spin(v, 0, -8))
        return jnp.where(lanes >= 126, 0.0, t)

    def pack(dim, way, vs):
        acc = None
        for j, v in enumerate(vs):
            if dim == "a":
                v, mask = spin(v, 2 * j + (2 if way > 0 else 0), 0), rows // 2 == j
            elif dim == "b":
                js, jl = j % 2, j // 2
                back = 1 if way > 0 else 0
                v, mask = spin(v, js - back, jl - back), (rows % 2 == js) & (lanes % 2 == jl)
            else:
                v, mask = spin(v, 0, 2 * j + (2 if way > 0 else 0)), lanes // 2 == j
            acc = v if acc is None else jnp.where(mask, v, acc)
        return acc

    def unpack(dim, way, w, j):
        if dim == "a":
            w = spin(w, -2 * j if way > 0 else 6 - 2 * j, 0)
        elif dim == "b":
            js, jl = j % 2, j // 2
            w = spin(w, -js, -jl) if way > 0 else spin(w, 1 - js, 1 - jl)
        else:
            w = spin(w, 0, -2 * j if way > 0 else 126 - 2 * j)
        return jnp.where((first if way > 0 else last)[dim], w, 0.0)

    def move(dims, way, v):
        row = (2 if "a" in dims else 0) - (1 if "b" in dims else 0)
        lane = (2 if "c" in dims else 0) - (1 if "b" in dims else 0)
        mask = None
        for dim in dims:
            part = (first if way > 0 else last)[dim]
            mask = part if mask is None else mask & part
        return jnp.where(mask, spin(v, way * row, way * lane), 0.0)

    def guarded(key, way, run):
        name, dims, _ = key
        if name in ("f1", "f2", "f3", "f4", "S7", "C7") and "a" in dims:
            pl.when(gy < ny - 1 if way > 0 else gy > 0)(run)
        else:
            run()

    def device_at(da, db, dc):
        return {
            "gx": lax.rem(gx + dc + nx, nx) if dc else gx,
            "gy": lax.rem(gy + da + ny, ny) if da else gy,
            "gz": lax.rem(gz + db + nz, nz) if db else gz,
        }

    def remote(src, dst, index, device):
        return pltpu.make_async_remote_copy(
            src_ref=src,
            dst_ref=dst,
            send_sem=ssem.at[index],
            recv_sem=rsem.at[index],
            device_id=device,
            device_id_type=pl.DeviceIdType.MESH,
        )

    def copy_of(key):
        name, dims, way = key
        offset, length, index = SLOTS[key]
        part = pl.ds(offset * 8, length * 8)
        device = device_at(*(way if dim in dims else 0 for dim in ALL_DIMS))
        return remote(sbuf.at[part], rbuf.at[part], index, device)

    pending = []

    def send(key):
        guarded(key, key[2], lambda: copy_of(key).start())
        pending.append(key)

    def receive(key):
        guarded(key, -key[2], lambda: copy_of(key).wait_recv())

    def drain(keep=None):
        for key in list(pending):
            if key[0] != keep:
                guarded(key, key[2], lambda: copy_of(key).wait_send())
                pending.remove(key)

    def tile(ref, index):
        start = index * 8
        if not isinstance(index, int):
            start = pl.multiple_of(start, 8)
        return ref[pl.ds(start, 8), :]

    def put(ref, index, value):
        start = index * 8
        if not isinstance(index, int):
            start = pl.multiple_of(start, 8)
        ref[pl.ds(start, 8), :] = value

    def at7(t):
        return (t[0] * 7 + t[1]) * 7 + t[2]

    def at8(t):
        return (t[0] * 8 + t[1]) * 8 + t[2]

    def loop(count, body):
        def step(i, carry):
            body(i)
            return carry

        lax.fori_loop(0, count, step, 0)

    def line(lv, dim, v):
        q, half = lv.q, lv.half
        full = list(v) + [down(dim, v[0])]
        e = [full[j] + full[q - j] for j in range(half)]
        o = [full[j] - full[q - j] for j in range(half)]
        y = [None] * (q + 1)
        for i in range(half):
            ev, od = mix(lv.even[i], e), mix(lv.odd[i], o)
            y[i] = od if ev is None else ev + od
            y[q - i] = -od if ev is None else ev - od
        own = jnp.where(first[dim], float(lv.gain[q, q]), 0.0)
        y[0] = y[0] + up(dim, y[q]) + own * v[0]
        return y[:q]

    def partial_end(lv, v):
        return mix(lv.gain[lv.q, : lv.q], v)

    def lower_line(hi, lo, v):
        jmat = lagrange_matrix(gll_table(hi.q)[0], gll_table(lo.q)[0])
        r = jmat.T * hi.mass[None, :] / lo.mass[:, None]
        inner = range(1, hi.half)
        e = [v[n] + v[hi.q - n] for n in inner]
        o = [v[n] - v[hi.q - n] for n in inner]
        y = [None] * (lo.q + 1)
        for m in range(lo.half):
            ev = mix([0.5 * (r[m, n] + r[m, hi.q - n]) for n in inner], e)
            od = mix([0.5 * (r[m, n] - r[m, hi.q - n]) for n in inner], o)
            y[m], y[lo.q - m] = ev + od, ev - od
        y[0] = y[0] + float(r[0, 0]) * v[0]
        return y

    def raise_line(hi, lo, v):
        jmat = lagrange_matrix(gll_table(hi.q)[0], gll_table(lo.q)[0])
        e = [v[m] + v[lo.q - m] for m in range(lo.half)]
        o = [v[m] - v[lo.q - m] for m in range(lo.half)]
        y = [None] * (hi.q + 1)
        y[0] = v[0]
        for n in range(1, hi.half):
            ev = mix([0.5 * (jmat[n, m] + jmat[n, lo.q - m]) for m in range(lo.half)], e)
            od = mix([0.5 * (jmat[n, m] - jmat[n, lo.q - m]) for m in range(lo.half)], o)
            y[n], y[hi.q - n] = ev + od, ev - od
        return y[: hi.q]


    def store_face(name, dim, way, n, get):
        offset = SLOTS[(name, dim, way)][0]
        if dim == "c":
            acc = None
            for i in range(n):
                w = pack(dim, way, [get(i, k) for k in range(n)])
                acc = w if acc is None else jnp.where(lanes // 8 == i, spin(w, 0, 8 * i), acc)
            put(sbuf, offset, acc)
        else:
            for i in range(n):
                put(sbuf, offset + i, pack(dim, way, [get(i, k) for k in range(n)]))
        send((name, dim, way))

    def load_face(name, dim, way, n):
        offset = SLOTS[(name, dim, way)][0]
        receive((name, dim, way))
        if dim == "c":
            w = tile(rbuf, offset)
            return [[unpack(dim, way, spin(w, 0, -8 * i), k) for k in range(n)] for i in range(n)]
        return [
            [unpack(dim, way, tile(rbuf, offset + i), k) for k in range(n)] for i in range(n)
        ]

    def small_apply(lv, name, dv):
        n = lv.n
        for dim in ALL_DIMS:
            store_face(name, dim, -1, n, lambda i, k: dv[node(dim, 0, i, k)])
            store_face(
                name, dim, 1, n,
                lambda i, k: partial_end(lv, [dv[node(dim, m, i, k)] for m in range(n)]),
            )
        y = {}
        for dim in ALL_DIMS:
            for i in range(n):
                for k in range(n):
                    got = line(lv, dim, [dv[node(dim, m, i, k)] for m in range(n)])
                    for m in range(n):
                        t = node(dim, m, i, k)
                        y[t] = got[m] if t not in y else y[t] + got[m]
        drain(name)
        for dim in ALL_DIMS:
            before = load_face(name, dim, -1, n)
            after = load_face(name, dim, 1, n)
            for i in range(n):
                for k in range(n):
                    for m in range(n):
                        t = node(dim, m, i, k)
                        y[t] = y[t] + float(lv.gain[m, lv.q]) * before[i][k]
                    t = node(dim, 0, i, k)
                    y[t] = y[t] + after[i][k]
        return y

    def masked(t, v):
        if t[0] == 0:
            v = v * wall_a
        if t[1] == 0:
            v = v * wall_b
        return v

    def small_sum(lv, name, closed):
        n, q = lv.n, lv.q
        for dim in ALL_DIMS:
            for i in range(q + 1):
                for k in range(q + 1):
                    low, high = node(dim, 0, i, k), node(dim, q, i, k)
                    closed[low] = closed[low] + up(dim, closed[high])
        for dim in ALL_DIMS:
            store_face(name, dim, 1, n, lambda i, k: closed[node(dim, q, i, k)])
        for dims in SUBSETS[3:]:
            key = (name, dims, 1)
            for j, t in enumerate(plane(dims, n, q)):
                put(sbuf, SLOTS[key][0] + j, closed[t])
            send(key)
        drain(name)
        r = {t: closed[t] for t in itertools.product(range(n), repeat=3)}
        for dim in ALL_DIMS:
            got = load_face(name, dim, 1, n)
            for i in range(n):
                for k in range(n):
                    t = node(dim, 0, i, k)
                    r[t] = r[t] + got[i][k]
        for dims in SUBSETS[3:]:
            key = (name, dims, 1)
            receive(key)
            for j, t in enumerate(plane(dims, n, 0)):
                r[t] = r[t] + move(dims, 1, tile(rbuf, SLOTS[key][0] + j))
        return {t: masked(t, v) for t, v in r.items()}

    def plane(dims, n, end):
        ranges = [[end] if dim in dims else range(n) for dim in ALL_DIMS]
        return list(itertools.product(*ranges))

    def small_close(lv, name, v):
        n, q = lv.n, lv.q
        for dim in ALL_DIMS:
            store_face(name, dim, -1, n, lambda i, k: v[node(dim, 0, i, k)])
        for dims in SUBSETS[3:]:
            key = (name, dims, -1)
            for j, t in enumerate(plane(dims, n, 0)):
                put(sbuf, SLOTS[key][0] + j, v[t])
            send(key)
        drain(name)
        halo = {}
        for dim in ALL_DIMS:
            got = load_face(name, dim, -1, n)
            for i in range(n):
                for k in range(n):
                    halo[(dim, node(dim, q, i, k))] = got[i][k]
        for dims in SUBSETS[3:]:
            key = (name, dims, -1)
            receive(key)
            for j, t in enumerate(plane(dims, n, q)):
                halo[(dims, t)] = move(dims, -1, tile(rbuf, SLOTS[key][0] + j))
        return closure(lv, dict(v), halo)

    def closure(lv, field, halo):
        n, q = lv.n, lv.q

        def value(have, t):
            ends = "".join(dim for dim, i in zip(ALL_DIMS, t) if i == q and dim not in have)
            if not ends:
                return halo[(have, t)] if have else field[t]
            dim = ends[0]
            low = tuple(0 if d == dim else i for d, i in zip(ALL_DIMS, t))
            with_dim = "".join(d for d in ALL_DIMS if d in have or d == dim)
            return down(dim, value(have, low)) + value(with_dim, t)

        return {t: value("", t) for t in itertools.product(range(q + 1), repeat=3)}

    def first_step(lv, r):
        return {t: float(lv.inverse(*t) / lv.center) * v for t, v in r.items()}

    def next_step(lv, factor, dv, r):
        keep, gain = factor
        return {t: float(keep) * dv[t] + float(gain * lv.inverse(*t)) * r[t] for t in r}

    def subtract(r, y):
        return {t: masked(t, r[t] - y[t]) for t in r}

    def add(*fields):
        return {t: total(f[t] for f in fields) for t in fields[0]}

    def zero_block(i):
        rbuf[pl.ds(pl.multiple_of(i * 64, 64), 64), :] = jnp.zeros((64, 128), jnp.float32)

    loop(BUF_VREGS // 8, zero_block)

    for offset in BLOCKS:
        pl.semaphore_signal(
            pltpu.get_barrier_semaphore(),
            inc=1,
            device_id=device_at(*offset),
            device_id_type=pl.DeviceIdType.MESH,
        )

    def butterfly(vs):
        for bit in (1, 2, 4):
            new = list(vs)
            low = (lanes // bit) % 2 == 0
            for i in range(8):
                if not i & bit:
                    lo, hi = vs[i], vs[i + bit]
                    new[i] = jnp.where(low, lo, spin(hi, 0, bit))
                    new[i + bit] = jnp.where(low, spin(lo, 0, -bit), hi)
            vs = new
        return vs

    def enter(i):
        an, ael = lax.rem(i, 8), lax.div(i, 8)
        for b_hi in range(2):
            vs = [
                x[i, pl.ds((2 * b_hi + g % 2) * 8, 8), pl.ds((g // 2) * 128, 128)] for g in range(8)
            ]
            for cn, v in enumerate(butterfly(vs)):
                put(tr, (an * 8 + cn) * 8 + ael * 2 + b_hi, v)

    loop(32, enter)

    def by_nodes(an, bn, cn):
        return pl.ds((an * 8 + cn) * 64 + bn, 8, stride=8)

    def slab(a):
        v = {(b, c): tr[by_nodes(a, b, c), :] for b in range(8) for c in range(8)}
        for c in range(8):
            v[(0, c)] = v[(0, c)] + up("b", v[(7, c)])
        for b in range(8):
            v[(b, 0)] = v[(b, 0)] + up("c", v[(b, 7)])
        for (b, c), value in v.items():
            put(u, at8((a, b, c)), value)

    loop(8, slab)

    def join(b):
        for c in range(8):
            t = at8((0, b, c))
            put(u, t, tile(u, t) + up("a", tile(u, at8((7, b, c)))))

    loop(8, join)

    pl.semaphore_wait(pltpu.get_barrier_semaphore(), len(BLOCKS))

    def fine_face(name, dim, way, get):
        offset = SLOTS[(name, dim, way)][0]

        def row(i):
            vs = [get(i, k) for k in range(7)]
            if dim == "c":
                put(pk, i, pack(dim, way, vs))
            else:
                put(sbuf, offset + 2 * i, pack(dim, way, vs[:4]))
                put(sbuf, offset + 2 * i + 1, pack(dim, way, vs[4:]))

        loop(7, row)
        if dim == "c":
            acc = tile(pk, 0)
            for i in range(1, 7):
                acc = jnp.where(lanes // 16 == i, spin(tile(pk, i), 0, 16 * i), acc)
            put(sbuf, offset, acc)
        send((name, dim, way))

    def spread_c(name, way, base):
        w = tile(rbuf, SLOTS[(name, "c", way)][0])
        for i in range(7):
            put(pk, base + i, spin(w, 0, -16 * i))

    def fine_row(name, dim, way, i, base):
        if dim == "c":
            w = tile(pk, base + i)
            return [unpack(dim, way, w, k) for k in range(7)]
        offset = SLOTS[(name, dim, way)][0]
        lo, hi = tile(rbuf, offset + 2 * i), tile(rbuf, offset + 2 * i + 1)
        return [unpack(dim, way, lo if k < 4 else hi, k % 4) for k in range(7)]

    for dim in ALL_DIMS:
        fine_face("S7", dim, 1, lambda i, k: tile(u, at8(node(dim, 7, i, k))))
    for dims in SUBSETS[3:]:
        key = ("S7", dims, 1)
        for j, t in enumerate(plane(dims, 7, 7)):
            put(sbuf, SLOTS[key][0] + j, tile(u, at8(t)))
        send(key)
    for dim in ALL_DIMS:
        receive(("S7", dim, 1))
        if dim == "c":
            spread_c("S7", 1, 0)

        def add_face(i):
            got = fine_row("S7", dim, 1, i, 0)
            for k in range(7):
                t = at8(node(dim, 0, i, k))
                put(u, t, tile(u, t) + got[k])

        loop(7, add_face)
    for dims in SUBSETS[3:]:
        key = ("S7", dims, 1)
        receive(key)
        for j, t in enumerate(plane(dims, 7, 0)):
            put(u, at8(t), tile(u, at8(t)) + move(dims, 1, tile(rbuf, SLOTS[key][0] + j)))

    def first_fine(a):
        wall = jnp.where(a == 0, wall_a, 1.0)
        for b in range(7):
            for c in range(7):
                scale = tab[a * TAB + 16 + combo(b, c)]
                r = tile(u, at8((a, b, c))) * scale * wall
                if b == 0:
                    r = r * wall_b
                put(rho, at7((a, b, c)), r)
                put(d, at7((a, b, c)), (tab[a * TAB + combo(b, c)] * (1.0 / FINE.center)) * r)

    loop(7, first_fine)

    def fine_apply(name, after):
        for dim in ALL_DIMS:
            fine_face(name, dim, -1, lambda i, k: tile(d, at7(node(dim, 0, i, k))))
            fine_face(
                name, dim, 1,
                lambda i, k: partial_end(FINE, [tile(d, at7(node(dim, m, i, k))) for m in range(7)]),
            )

        def lines(dim, i):
            for k in range(7):
                at = [at7(node(dim, m, i, k)) for m in range(7)]
                got = line(FINE, dim, [tile(d, t) for t in at])
                for t, y in zip(at, got):
                    put(rho, t, tile(rho, t) - y)

        loop(7, lambda i: lines("a", i))

        def cross(i):
            lines("b", i)
            lines("c", i)

        loop(7, cross)

        drain(name)
        for dim in ALL_DIMS:
            for way in (1, -1):
                receive((name, dim, way))
        spread_c(name, 1, 0)
        spread_c(name, -1, 7)

        def side_a(i):
            got = fine_row(name, "a", -1, i, 0)
            add0 = fine_row(name, "a", 1, i, 0)
            for k in range(7):
                put(ha, i * 7 + k, got[k])
                t = at7((0, i, k))
                put(rho, t, tile(rho, t) - add0[k])

        loop(7, side_a)

        def finish(a):
            wall = jnp.where(a == 0, wall_a, 1.0)
            gain_a = tab[a * TAB + 32]
            b_before = fine_row(name, "b", -1, a, 0)
            b_after = fine_row(name, "b", 1, a, 0)
            c_before = fine_row(name, "c", -1, a, 7)
            c_after = fine_row(name, "c", 1, a, 0)
            for b in range(7):
                for c in range(7):
                    t = at7((a, b, c))
                    r = tile(rho, t) - gain_a * tile(ha, b * 7 + c)
                    r = r - float(FINE.gain[b, 7]) * b_before[c]
                    r = r - float(FINE.gain[c, 7]) * c_before[b]
                    if b == 0:
                        r = r - b_after[c]
                    if c == 0:
                        r = r - c_after[b]
                    r = r * wall
                    if b == 0:
                        r = r * wall_b
                    put(rho, t, r)
                    if after is not None:
                        after(a, b, c, r)

        loop(7, finish)

    fine_keep, fine_gain = FINE.factors(2)[0]

    def fine_next(a, b, c, r):
        t = at7((a, b, c))
        h = tab[a * TAB + combo(b, c)]
        return float(fine_keep) * tile(d, t) + (h * float(fine_gain)) * r

    def after_first(a, b, c, r):
        new = fine_next(a, b, c, r)
        t = at7((a, b, c))
        put(xs, at8((a, b, c)), tile(d, t) + new)
        put(d, t, new)

    def after_lift(a, b, c, r):
        t, s = at7((a, b, c)), at8((a, b, c))
        put(xs, s, tile(xs, s) + tile(d, t))
        put(d, t, (tab[a * TAB + combo(b, c)] * (1.0 / FINE.center)) * r)

    def after_post(a, b, c, r):
        t, s = at7((a, b, c)), at8((a, b, c))
        put(xs, s, tile(xs, s) + tile(d, t) + fine_next(a, b, c, r))

    fine_apply("f1", after_first)
    fine_apply("f2", None)

    def lower_a(b):
        for c in range(7):
            got = lower_line(FINE, MID, [tile(rho, at7((m, b, c))) for m in range(7)])
            for m in range(4):
                put(w1, (m * 7 + b) * 7 + c, got[m])

    loop(7, lower_a)

    def lower_b(a):
        for c in range(7):
            got = lower_line(FINE, MID, [tile(w1, (a * 7 + m) * 7 + c) for m in range(7)])
            for m in range(4):
                put(w2, (a * 4 + m) * 7 + c, got[m])

    loop(4, lower_b)
    closed = {}
    for a in range(4):
        for b in range(4):
            got = lower_line(FINE, MID, [tile(w2, (a * 4 + b) * 7 + m) for m in range(7)])
            for m in range(4):
                closed[(a, b, m)] = got[m]
    r3 = small_sum(MID, "S3", closed)

    mid_factor = MID.factors(2)[0]
    d3 = first_step(MID, r3)
    r3 = subtract(r3, small_apply(MID, "m1", d3))
    e3 = next_step(MID, mid_factor, d3, r3)
    x3 = add(d3, e3)
    r3 = subtract(r3, small_apply(MID, "m2", e3))

    closed = r3
    for dim in ALL_DIMS:
        new = {}
        others = sorted({tuple(i for dd, i in zip(ALL_DIMS, t) if dd != dim) for t in closed})
        for i, k in others:
            got = lower_line(MID, LOW, [closed[node(dim, m, i, k)] for m in range(3)])
            for m in range(2):
                new[node(dim, m, i, k)] = got[m]
        closed = new
    r1 = small_sum(LOW, "S1", closed)
    here = (0, 0, 0)
    origin = SLOTS[BLOCKS[0]][0]
    put(sbuf, origin, r1[here])

    def block_copy(offset):
        place, _, index = SLOTS[offset]
        src, dst = sbuf.at[pl.ds(origin * 8, 8)], rbuf.at[pl.ds(place * 8, 8)]
        return remote(src, dst, index, device_at(*offset))

    for offset in BLOCKS:
        block_copy(offset).start()
    drain()
    r = {here: r1[here]}
    for offset in BLOCKS:
        block_copy(offset).wait_recv()
        r[tuple(-o for o in offset)] = tile(rbuf, SLOTS[offset][0])

    def up_full(dim, v, before):
        if dim == "a":
            return spin(jnp.where(last["a"], before, v), 2, 0)
        if dim == "b":
            w = jnp.where(odd_lane, jnp.where(odd_row, spin(v, 1, 0), spin(before, -1, 0)), v)
            return jnp.where(odd_lane, spin(w, 0, 1), spin(w, 0, -1))
        t = jnp.where(lanes < 8, spin(v, 0, 10), spin(v, 0, 8))
        return jnp.where(lanes < 2, spin(before, 0, 2), t)

    def down_full(dim, v, after):
        if dim == "a":
            return spin(jnp.where(first["a"], after, v), -2, 0)
        if dim == "b":
            w = jnp.where(odd_lane, v, jnp.where(odd_row, spin(after, 1, 0), spin(v, -1, 0)))
            return jnp.where(odd_lane, spin(w, 0, 1), spin(w, 0, -1))
        t = jnp.where(lanes >= 120, spin(v, 0, -10), spin(v, 0, -8))
        return jnp.where(lanes >= 126, spin(after, 0, -2), t)

    def beside(dim, o, step):
        return tuple(i + step if d == dim else i for d, i in zip(ALL_DIMS, o))

    def both_sides(dim, f, o):
        before, after = f.get(beside(dim, o, -1), f[o]), f.get(beside(dim, o, 1), f[o])
        return up_full(dim, f[o], before) + down_full(dim, f[o], after)

    walls_a, walls_b = {}, {}
    for step in (-1, 0, 1):
        at_a, at_b = lax.rem(gy + step + ny, ny) == 0, lax.rem(gz + step + nz, nz) == 0
        walls_a[step] = jnp.where(first["a"] & at_a, 0.0, 1.0).astype(jnp.float32)
        walls_b[step] = jnp.where(first["b"] & at_b, 0.0, 1.0).astype(jnp.float32)

    own_low = 3.0 * float(LOW.gain[0, 0] + LOW.gain[1, 1])
    side_low = float(LOW.gain[0, 1])
    inverse_low = float(LOW.inverse(0, 0, 0))
    dl = {o: (inverse_low / LOW.center) * v for o, v in r.items()}
    x1 = dict(dl)
    for keep, gain in LOW.factors(COARSE_STEPS):
        new = {}
        for o in r:
            sides = total(both_sides(dim, dl, o) for dim in ALL_DIMS)
            left = r[o] - (own_low * dl[o] + side_low * sides)
            new[o] = left * (walls_a[o[0]] * walls_b[o[1]])
        r = new
        dl = {o: float(keep) * dl[o] + float(gain * inverse_low) * r[o] for o in r}
        x1 = add(x1, dl)

    def corners(f, dims):
        for dim in dims:
            new = {}
            for o, v in f.items():
                new[o] = v if o[ALL_DIMS.index(dim)] == 0 else None
            for o in f:
                if new[o] is None:
                    low = beside(dim, o, -1)
                    new[o] = down_full(dim, f[low], f[o])
            f = new
        return f

    def lift_low(f, dims):
        for dim in dims:
            new = {}
            rest = sorted({tuple(i for d, i in zip(ALL_DIMS, t) if d != dim) for t in f})
            for i, k in rest:
                got = raise_line(MID, LOW, [f[node(dim, m, i, k)] for m in range(2)])
                for m in range(3):
                    new[node(dim, m, i, k)] = got[m]
            f = new
        return f

    ends = list(itertools.product((0, 1), repeat=3))
    c3 = lift_low(corners({o: x1[o] for o in ends}, ALL_DIMS), "cba")
    y = {t: None for t in c3}
    for dim in ALL_DIMS:
        at = ALL_DIMS.index(dim)
        rest = ALL_DIMS.replace(dim, "")
        f = {}
        for o in ends:
            if o[at] == 0:
                f[o] = (x1[o] - 0.5 * both_sides(dim, x1, o)) * float(1.0 / MID.mass[0])
        for t, v in lift_low(corners(f, rest), rest).items():
            y[t] = v if y[t] is None else y[t] + v
    r3 = {t: masked(t, v if y[t] is None else v - y[t]) for t, v in r3.items()}
    d3 = first_step(MID, r3)
    r3 = subtract(r3, small_apply(MID, "m4", d3))
    e3 = next_step(MID, mid_factor, d3, r3)
    t3 = small_close(MID, "C3", add(x3, c3, d3, e3))

    for a in range(4):
        for b in range(4):
            got = raise_line(FINE, MID, [t3[(a, b, m)] for m in range(4)])
            for m in range(7):
                put(w2, (a * 4 + b) * 7 + m, got[m])

    def raise_b(a):
        for c in range(7):
            got = raise_line(FINE, MID, [tile(w2, (a * 4 + m) * 7 + c) for m in range(4)])
            for m in range(7):
                put(w1, (a * 7 + m) * 7 + c, got[m])

    loop(4, raise_b)

    def raise_a(b):
        for c in range(7):
            got = raise_line(FINE, MID, [tile(w1, (m * 7 + b) * 7 + c) for m in range(4)])
            for m in range(7):
                put(d, at7((m, b, c)), got[m])

    loop(7, raise_a)
    fine_apply("f3", after_lift)
    fine_apply("f4", after_post)

    for dim in ALL_DIMS:
        fine_face("C7", dim, -1, lambda i, k: tile(xs, at8(node(dim, 0, i, k))))
    for dims in SUBSETS[3:]:
        key = ("C7", dims, -1)
        for j, t in enumerate(plane(dims, 7, 0)):
            put(sbuf, SLOTS[key][0] + j, tile(xs, at8(t)))
        send(key)
    for dims in SUBSETS:
        receive(("C7", dims, -1))
    spread_c("C7", -1, 0)

    def edge(dims, j):
        return move(dims, -1, tile(rbuf, SLOTS[("C7", dims, -1)][0] + j))

    for dim in ALL_DIMS:

        def end_face(i):
            got = fine_row("C7", dim, -1, i, 0)
            for k in range(7):
                value = down(dim, tile(xs, at8(node(dim, 0, i, k)))) + got[k]
                put(xs, at8(node(dim, 7, i, k)), value)

        loop(7, end_face)

    hb = fine_row("C7", "b", -1, 0, 0)
    hc_a = fine_row("C7", "c", -1, 0, 0)
    hc_b = [fine_row("C7", "c", -1, i, 0)[0] for i in range(7)]
    for k in range(7):
        value = down("b", tile(xs, at8((7, 0, k)))) + down("a", hb[k]) + edge("ab", k)
        put(xs, at8((7, 7, k)), value)
        value = down("c", tile(xs, at8((7, k, 0)))) + down("a", hc_a[k]) + edge("ac", k)
        put(xs, at8((7, k, 7)), value)
        value = down("c", tile(xs, at8((k, 7, 0)))) + down("b", hc_b[k]) + edge("bc", k)
        put(xs, at8((k, 7, 7)), value)
    value = down("c", tile(xs, at8((7, 7, 0)))) + down("b", down("a", hc_a[0]))
    value = value + down("b", edge("ac", 0)) + down("a", edge("bc", 0)) + edge("abc", 0)
    put(xs, at8((7, 7, 7)), value)

    def leave_nodes(a):
        for b in range(8):
            for c in range(8):
                tr[by_nodes(a, b, c), :] = tile(xs, at8((a, b, c)))

    loop(8, leave_nodes)

    def leave(i):
        an, ael = lax.rem(i, 8), lax.div(i, 8)
        for b_hi in range(2):
            vs = butterfly([tile(tr, (an * 8 + cn) * 8 + ael * 2 + b_hi) for cn in range(8)])
            for g, v in enumerate(vs):
                out[i, pl.ds((2 * b_hi + g % 2) * 8, 8), pl.ds((g // 2) * 128, 128)] = v

    loop(32, leave)
    drain()
    for offset in BLOCKS:
        block_copy(offset).wait_send()


def solution(mesh):
    sizes = tuple(mesh.shape[axis] for axis in ("gx", "gy", "gz"))

    def body(*refs):
        kernel(sizes, *refs)

    def local(residual):
        vmem = lambda count: pltpu.VMEM((count * 8, 128), jnp.float32)
        return pl.pallas_call(
            body,
            out_shape=jax.ShapeDtypeStruct(residual.shape, jnp.float32),
            in_specs=[
                pl.BlockSpec(memory_space=pltpu.SMEM),
                pl.BlockSpec(memory_space=pltpu.VMEM),
            ],
            out_specs=pl.BlockSpec(memory_space=pltpu.VMEM),
            scratch_shapes=[
                vmem(512),
                vmem(512),
                vmem(343),
                vmem(343),
                vmem(512),
                vmem(196),
                vmem(112),
                vmem(49),
                vmem(16),
                vmem(BUF_VREGS),
                vmem(BUF_VREGS),
                pltpu.SemaphoreType.DMA((MESSAGES,)),
                pltpu.SemaphoreType.DMA((MESSAGES,)),
            ],
            compiler_params=pltpu.CompilerParams(
                collective_id=0, has_side_effects=True, vmem_limit_bytes=40 * 1024 * 1024
            ),
        )(jnp.asarray(table()), residual)

    return jax.shard_map(
        local,
        mesh=mesh,
        in_specs=(P("gy", "gz", "gx"),),
        out_specs=P("gy", "gz", "gx"),
        check_vma=False,
    )
```

```python
import itertools

import jax
import jax.numpy as jnp
import numpy as np
from jax import lax
from jax.experimental import pallas as pl
from jax.experimental.pallas import tpu as pltpu
from jax.sharding import PartitionSpec as P

ORDER = 7
MID_ORDER = 3
COARSE_STEPS = 4


def legendre_pair(degree, points):
    previous = np.ones(points.shape)
    current = points.copy()
    for level in range(1, degree):
        following = ((2 * level + 1) * points * current - level * previous) / (level + 1)
        previous = current
        current = following
    return (current, previous)


def gll_table(degree):
    points = np.cos(np.pi * np.arange(degree + 1) / degree)
    for sweep in range(100):
        current, previous = legendre_pair(degree, points)
        points = points - (points * current - previous) / ((degree + 1) * current)
    points = points[::-1].copy()
    current, previous = legendre_pair(degree, points)
    weights = 2.0 / (degree * (degree + 1) * current**2)
    return (points, weights)


def lagrange_matrix(targets, points):
    point_count = len(points)
    matrix = np.ones((len(targets), point_count))
    for column in range(point_count):
        for partner in range(point_count):
            if partner != column:
                matrix[:, column] *= (targets - points[partner]) / (
                    points[column] - points[partner]
                )
    return matrix


def line_stiffness(degree):
    points, weights = gll_table(degree)
    point_count = len(points)
    barycentric = np.array(
        [
            1.0
            / np.prod(
                [
                    points[column] - points[partner]
                    for partner in range(point_count)
                    if partner != column
                ]
            )
            for column in range(point_count)
        ]
    )
    derivative = np.zeros((point_count, point_count))
    for target in range(point_count):
        for column in range(point_count):
            if target != column:
                derivative[target, column] = (
                    barycentric[column] / barycentric[target] / (points[target] - points[column])
                )
        derivative[target, target] = -np.sum(derivative[target])
    return (derivative.T @ (weights[:, None] * derivative), weights)


def assembled_patterns(degree):
    stiffness, weights = line_stiffness(degree)
    indices = np.arange(len(weights))
    diag_pat = stiffness[indices, indices].copy()
    weight_pat = weights.copy()
    row_pat = np.abs(stiffness).sum(axis=1)
    for pattern in (diag_pat, weight_pat, row_pat):
        shared = pattern[0] + pattern[-1]
        pattern[0] = shared
        pattern[-1] = shared
    return (diag_pat, weight_pat, row_pat)


def three_terms(special, weight_pat):
    return (
        special[:, None, None] * weight_pat[None, :, None] * weight_pat[None, None, :]
        + weight_pat[:, None, None] * special[None, :, None] * weight_pat[None, None, :]
        + weight_pat[:, None, None] * weight_pat[None, :, None] * special[None, None, :]
    )


def chebyshev_bound(degree):
    diag_pat, weight_pat, row_pat = assembled_patterns(degree)
    return float(np.max(three_terms(row_pat, weight_pat) / three_terms(diag_pat, weight_pat)))


class Level:
    def __init__(self, q):
        stiffness, weights = line_stiffness(q)
        diag_pat, weight_pat, row_pat = assembled_patterns(q)
        self.q = self.n = q
        self.half = half = (q + 1) // 2
        self.mass = weight_pat
        self.gain = gain = stiffness / weight_pat[:, None]
        self.even = 0.5 * (gain[:half, :half] + gain[:half, ::-1][:, :half])
        self.odd = 0.5 * (gain[:half, :half] - gain[:half, ::-1][:, :half])
        self.alpha = diag_pat / weight_pat
        upper = chebyshev_bound(q)
        lower = upper / 10.0
        self.center = 0.5 * (upper + lower)
        self.halfwidth = 0.5 * (upper - lower)

    def inverse(self, a, b, c):
        return 1.0 / (self.alpha[a] + self.alpha[b] + self.alpha[c])

    def factors(self, steps):
        scaled = self.center / self.halfwidth
        ratio = 1.0 / scaled
        found = []
        for step in range(1, steps):
            following = 1.0 / (2.0 * scaled - ratio)
            found.append((following * ratio, 2.0 * following / self.halfwidth))
            ratio = following
        return found


FINE, MID, LOW = Level(ORDER), Level(MID_ORDER), Level(1)
ALL_DIMS = "abc"
SUBSETS = ("a", "b", "c", "ab", "ac", "bc", "abc")
BLOCKS = [o for o in itertools.product((-1, 0, 1), repeat=3) if any(o)]


def node(dim, m, i, k):
    return {"a": (m, i, k), "b": (i, m, k), "c": (i, k, m)}[dim]


def face_vregs(n, dim):
    return 1 if dim == "c" else n * -(-n // 4)


def plan():
    slots, size, count = {}, 0, 0

    def add(key, length):
        nonlocal size, count
        slots[key] = (size, length, count)
        size += length
        count += 1

    for name, n in (
        ("f1", 7), ("f2", 7), ("f3", 7), ("f4", 7),
        ("m1", 3), ("m2", 3), ("m4", 3),
    ):
        for dim in ALL_DIMS:
            for way in (1, -1):
                add((name, dim, way), face_vregs(n, dim))
    for name, n, way in (("S7", 7, 1), ("S3", 3, 1), ("S1", 1, 1), ("C3", 3, -1), ("C7", 7, -1)):
        for dims in SUBSETS:
            add((name, dims, way), face_vregs(n, dims) if len(dims) == 1 else n ** (3 - len(dims)))
    for offset in BLOCKS:
        add(offset, 1)
    return slots, -(-size // 8) * 8, count


SLOTS, BUF_VREGS, MESSAGES = plan()


def total(terms):
    out = None
    for term in terms:
        if term is not None:
            out = term if out is None else out + term
    return out


def mix(coefs, values):
    return total(
        None if abs(coef) < 1e-13 else float(coef) * value for coef, value in zip(coefs, values)
    )


def kernel(sizes, x, out, tr, u, rho, d, ya, yb, yc, xs, w1, w2, ha, pk, sbuf, rbuf, ssem, rsem):
    nx, ny, nz = sizes
    gx, gy, gz = lax.axis_index("gx"), lax.axis_index("gy"), lax.axis_index("gz")
    rows = lax.broadcasted_iota(jnp.int32, (8, 128), 0)
    lanes = lax.broadcasted_iota(jnp.int32, (8, 128), 1)
    odd_row, odd_lane = rows % 2 == 1, lanes % 2 == 1
    first = {"a": rows < 2, "b": (rows % 2 == 0) & (lanes % 2 == 0), "c": lanes < 2}
    last = {"a": rows >= 6, "b": odd_row & odd_lane, "c": lanes >= 126}
    wall_a = jnp.where(first["a"] & (gy == 0), 0.0, 1.0).astype(jnp.float32)
    wall_b = jnp.where(first["b"] & (gz == 0), 0.0, 1.0).astype(jnp.float32)

    def spin(v, row, lane):
        if row % 8:
            v = pltpu.roll(v, row % 8, 0)
        if lane % 128:
            v = pltpu.roll(v, lane % 128, 1)
        return v

    def up(dim, v):
        if dim == "a":
            return jnp.where(rows >= 2, spin(v, 2, 0), 0.0)
        if dim == "b":
            w = jnp.where(odd_lane, jnp.where(odd_row, spin(v, 1, 0), 0.0), v)
            return jnp.where(odd_lane, spin(w, 0, 1), spin(w, 0, -1))
        t = jnp.where(lanes < 8, spin(v, 0, 10), spin(v, 0, 8))
        return jnp.where(lanes < 2, 0.0, t)

    def down(dim, v):
        if dim == "a":
            return jnp.where(rows < 6, spin(v, -2, 0), 0.0)
        if dim == "b":
            w = jnp.where(odd_lane, v, jnp.where(odd_row, 0.0, spin(v, -1, 0)))
            return jnp.where(odd_lane, spin(w, 0, 1), spin(w, 0, -1))
        t = jnp.where(lanes >= 120, spin(v, 0, -10), spin(v, 0, -8))
        return jnp.where(lanes >= 126, 0.0, t)

    def pack(dim, way, vs):
        acc = None
        for j, v in enumerate(vs):
            if dim == "a":
                v, mask = spin(v, 2 * j + (2 if way > 0 else 0), 0), rows // 2 == j
            elif dim == "b":
                js, jl = j % 2, j // 2
                back = 1 if way > 0 else 0
                v, mask = spin(v, js - back, jl - back), (rows % 2 == js) & (lanes % 2 == jl)
            else:
                v, mask = spin(v, 0, 2 * j + (2 if way > 0 else 0)), lanes // 2 == j
            acc = v if acc is None else jnp.where(mask, v, acc)
        return acc

    def unpack(dim, way, w, j):
        if dim == "a":
            w = spin(w, -2 * j if way > 0 else 6 - 2 * j, 0)
        elif dim == "b":
            js, jl = j % 2, j // 2
            w = spin(w, -js, -jl) if way > 0 else spin(w, 1 - js, 1 - jl)
        else:
            w = spin(w, 0, -2 * j if way > 0 else 126 - 2 * j)
        return jnp.where((first if way > 0 else last)[dim], w, 0.0)

    def move(dims, way, v):
        row = (2 if "a" in dims else 0) - (1 if "b" in dims else 0)
        lane = (2 if "c" in dims else 0) - (1 if "b" in dims else 0)
        mask = None
        for dim in dims:
            part = (first if way > 0 else last)[dim]
            mask = part if mask is None else mask & part
        return jnp.where(mask, spin(v, way * row, way * lane), 0.0)

    def guarded(key, way, run):
        name, dims, _ = key
        if name in ("f1", "f2", "f3", "f4", "S7", "C7") and "a" in dims:
            pl.when(gy < ny - 1 if way > 0 else gy > 0)(run)
        else:
            run()

    def device_at(da, db, dc):
        return {
            "gx": lax.rem(gx + dc + nx, nx) if dc else gx,
            "gy": lax.rem(gy + da + ny, ny) if da else gy,
            "gz": lax.rem(gz + db + nz, nz) if db else gz,
        }

    def remote(src, dst, index, device):
        return pltpu.make_async_remote_copy(
            src_ref=src,
            dst_ref=dst,
            send_sem=ssem.at[index],
            recv_sem=rsem.at[index],
            device_id=device,
            device_id_type=pl.DeviceIdType.MESH,
        )

    def copy_of(key):
        name, dims, way = key
        offset, length, index = SLOTS[key]
        part = pl.ds(offset * 8, length * 8)
        device = device_at(*(way if dim in dims else 0 for dim in ALL_DIMS))
        return remote(sbuf.at[part], rbuf.at[part], index, device)

    pending = []

    def send(key):
        guarded(key, key[2], lambda: copy_of(key).start())
        pending.append(key)

    def receive(key):
        guarded(key, -key[2], lambda: copy_of(key).wait_recv())

    def drain(keep=None):
        for key in list(pending):
            if key[0] != keep:
                guarded(key, key[2], lambda: copy_of(key).wait_send())
                pending.remove(key)

    def tile(ref, index):
        start = index * 8
        if not isinstance(index, int):
            start = pl.multiple_of(start, 8)
        return ref[pl.ds(start, 8), :]

    def put(ref, index, value):
        start = index * 8
        if not isinstance(index, int):
            start = pl.multiple_of(start, 8)
        ref[pl.ds(start, 8), :] = value

    def sub(ref, base, length):
        start = base * 8
        if not isinstance(base, int):
            start = pl.multiple_of(start, 8)
        return ref.at[pl.ds(start, length * 8)]

    def line_view(ref, dim, i):
        if dim == "a":
            return sub(ref, i * 7, 301), lambda m, k: m * 49 + k
        return sub(ref, i * 49, 49), (lambda m, k: m * 7 + k) if dim == "b" else (
            lambda m, k: k * 7 + m
        )

    def by_class(i, values):
        picked = jnp.where((i == 2) | (i == 5), values[2], values[3])
        picked = jnp.where((i == 1) | (i == 6), values[1], picked)
        return jnp.where(i == 0, values[0], picked)

    def splat(value):
        return jnp.full((8, 128), value, jnp.float32)

    def inverse_slab(a):
        alpha = splat(by_class(a, [float(v) for v in FINE.alpha[:4]]))
        found = {}
        for b in range(4):
            for c in range(b, 4):
                found[(b, c)] = 1.0 / (alpha + float(FINE.alpha[b] + FINE.alpha[c]))
        return lambda b, c: found[tuple(sorted((min(b, 7 - b), min(c, 7 - c))))]

    def at7(t):
        return (t[0] * 7 + t[1]) * 7 + t[2]

    def at8(t):
        return (t[0] * 8 + t[1]) * 8 + t[2]

    def loop(count, body):
        def step(i, carry):
            body(i)
            return carry

        lax.fori_loop(0, count, step, 0)

    def line(lv, dim, v):
        q, half = lv.q, lv.half
        full = list(v) + [down(dim, v[0])]
        e = [full[j] + full[q - j] for j in range(half)]
        o = [full[j] - full[q - j] for j in range(half)]
        y = [None] * (q + 1)
        for i in range(half):
            ev, od = mix(lv.even[i], e), mix(lv.odd[i], o)
            y[i] = od if ev is None else ev + od
            y[q - i] = -od if ev is None else ev - od
        own = jnp.where(first[dim], float(lv.gain[q, q]), 0.0)
        y[0] = y[0] + up(dim, y[q]) + own * v[0]
        return y[:q]

    def partial_end(lv, v):
        return mix(lv.gain[lv.q, : lv.q], v)

    def lower_line(hi, lo, v):
        jmat = lagrange_matrix(gll_table(hi.q)[0], gll_table(lo.q)[0])
        r = jmat.T * hi.mass[None, :] / lo.mass[:, None]
        inner = range(1, hi.half)
        e = [v[n] + v[hi.q - n] for n in inner]
        o = [v[n] - v[hi.q - n] for n in inner]
        y = [None] * (lo.q + 1)
        for m in range(lo.half):
            ev = mix([0.5 * (r[m, n] + r[m, hi.q - n]) for n in inner], e)
            od = mix([0.5 * (r[m, n] - r[m, hi.q - n]) for n in inner], o)
            y[m], y[lo.q - m] = ev + od, ev - od
        y[0] = y[0] + float(r[0, 0]) * v[0]
        return y

    def raise_line(hi, lo, v):
        jmat = lagrange_matrix(gll_table(hi.q)[0], gll_table(lo.q)[0])
        e = [v[m] + v[lo.q - m] for m in range(lo.half)]
        o = [v[m] - v[lo.q - m] for m in range(lo.half)]
        y = [None] * (hi.q + 1)
        y[0] = v[0]
        for n in range(1, hi.half):
            ev = mix([0.5 * (jmat[n, m] + jmat[n, lo.q - m]) for m in range(lo.half)], e)
            od = mix([0.5 * (jmat[n, m] - jmat[n, lo.q - m]) for m in range(lo.half)], o)
            y[n], y[hi.q - n] = ev + od, ev - od
        return y[: hi.q]


    def store_face(name, dim, way, n, get):
        offset = SLOTS[(name, dim, way)][0]
        if dim == "c":
            acc = None
            for i in range(n):
                w = pack(dim, way, [get(i, k) for k in range(n)])
                acc = w if acc is None else jnp.where(lanes // 8 == i, spin(w, 0, 8 * i), acc)
            put(sbuf, offset, acc)
        else:
            for i in range(n):
                put(sbuf, offset + i, pack(dim, way, [get(i, k) for k in range(n)]))
        send((name, dim, way))

    def load_face(name, dim, way, n):
        offset = SLOTS[(name, dim, way)][0]
        receive((name, dim, way))
        if dim == "c":
            w = tile(rbuf, offset)
            return [[unpack(dim, way, spin(w, 0, -8 * i), k) for k in range(n)] for i in range(n)]
        return [
            [unpack(dim, way, tile(rbuf, offset + i), k) for k in range(n)] for i in range(n)
        ]

    def small_apply(lv, name, dv):
        n = lv.n
        for dim in ALL_DIMS:
            store_face(name, dim, -1, n, lambda i, k: dv[node(dim, 0, i, k)])
            store_face(
                name, dim, 1, n,
                lambda i, k: partial_end(lv, [dv[node(dim, m, i, k)] for m in range(n)]),
            )
        y = {}
        for dim in ALL_DIMS:
            for i in range(n):
                for k in range(n):
                    got = line(lv, dim, [dv[node(dim, m, i, k)] for m in range(n)])
                    for m in range(n):
                        t = node(dim, m, i, k)
                        y[t] = got[m] if t not in y else y[t] + got[m]
        drain(name)
        for dim in ALL_DIMS:
            before = load_face(name, dim, -1, n)
            after = load_face(name, dim, 1, n)
            for i in range(n):
                for k in range(n):
                    for m in range(n):
                        t = node(dim, m, i, k)
                        y[t] = y[t] + float(lv.gain[m, lv.q]) * before[i][k]
                    t = node(dim, 0, i, k)
                    y[t] = y[t] + after[i][k]
        return y

    def masked(t, v):
        if t[0] == 0:
            v = v * wall_a
        if t[1] == 0:
            v = v * wall_b
        return v

    def small_sum(lv, name, closed):
        n, q = lv.n, lv.q
        for dim in ALL_DIMS:
            for i in range(q + 1):
                for k in range(q + 1):
                    low, high = node(dim, 0, i, k), node(dim, q, i, k)
                    closed[low] = closed[low] + up(dim, closed[high])
        for dim in ALL_DIMS:
            store_face(name, dim, 1, n, lambda i, k: closed[node(dim, q, i, k)])
        for dims in SUBSETS[3:]:
            key = (name, dims, 1)
            for j, t in enumerate(plane(dims, n, q)):
                put(sbuf, SLOTS[key][0] + j, closed[t])
            send(key)
        drain(name)
        r = {t: closed[t] for t in itertools.product(range(n), repeat=3)}
        for dim in ALL_DIMS:
            got = load_face(name, dim, 1, n)
            for i in range(n):
                for k in range(n):
                    t = node(dim, 0, i, k)
                    r[t] = r[t] + got[i][k]
        for dims in SUBSETS[3:]:
            key = (name, dims, 1)
            receive(key)
            for j, t in enumerate(plane(dims, n, 0)):
                r[t] = r[t] + move(dims, 1, tile(rbuf, SLOTS[key][0] + j))
        return {t: masked(t, v) for t, v in r.items()}

    def plane(dims, n, end):
        ranges = [[end] if dim in dims else range(n) for dim in ALL_DIMS]
        return list(itertools.product(*ranges))

    def small_close(lv, name, v):
        n, q = lv.n, lv.q
        for dim in ALL_DIMS:
            store_face(name, dim, -1, n, lambda i, k: v[node(dim, 0, i, k)])
        for dims in SUBSETS[3:]:
            key = (name, dims, -1)
            for j, t in enumerate(plane(dims, n, 0)):
                put(sbuf, SLOTS[key][0] + j, v[t])
            send(key)
        drain(name)
        halo = {}
        for dim in ALL_DIMS:
            got = load_face(name, dim, -1, n)
            for i in range(n):
                for k in range(n):
                    halo[(dim, node(dim, q, i, k))] = got[i][k]
        for dims in SUBSETS[3:]:
            key = (name, dims, -1)
            receive(key)
            for j, t in enumerate(plane(dims, n, q)):
                halo[(dims, t)] = move(dims, -1, tile(rbuf, SLOTS[key][0] + j))
        return closure(lv, dict(v), halo)

    def closure(lv, field, halo):
        n, q = lv.n, lv.q

        def value(have, t):
            ends = "".join(dim for dim, i in zip(ALL_DIMS, t) if i == q and dim not in have)
            if not ends:
                return halo[(have, t)] if have else field[t]
            dim = ends[0]
            low = tuple(0 if d == dim else i for d, i in zip(ALL_DIMS, t))
            with_dim = "".join(d for d in ALL_DIMS if d in have or d == dim)
            return down(dim, value(have, low)) + value(with_dim, t)

        return {t: value("", t) for t in itertools.product(range(q + 1), repeat=3)}

    def first_step(lv, r):
        return {t: float(lv.inverse(*t) / lv.center) * v for t, v in r.items()}

    def next_step(lv, factor, dv, r):
        keep, gain = factor
        return {t: float(keep) * dv[t] + float(gain * lv.inverse(*t)) * r[t] for t in r}

    def subtract(r, y):
        return {t: masked(t, r[t] - y[t]) for t in r}

    def add(*fields):
        return {t: total(f[t] for f in fields) for t in fields[0]}

    def zero_block(i):
        rbuf[pl.ds(pl.multiple_of(i * 64, 64), 64), :] = jnp.zeros((64, 128), jnp.float32)

    loop(BUF_VREGS // 8, zero_block)

    for offset in BLOCKS:
        pl.semaphore_signal(
            pltpu.get_barrier_semaphore(),
            inc=1,
            device_id=device_at(*offset),
            device_id_type=pl.DeviceIdType.MESH,
        )

    def butterfly(vs):
        for bit in (1, 2, 4):
            new = list(vs)
            low = (lanes // bit) % 2 == 0
            for i in range(8):
                if not i & bit:
                    lo, hi = vs[i], vs[i + bit]
                    new[i] = jnp.where(low, lo, spin(hi, 0, bit))
                    new[i + bit] = jnp.where(low, spin(lo, 0, -bit), hi)
            vs = new
        return vs

    def enter(an):
        to = sub(tr, an * 64, 64)
        for ael in range(4):
            for b_hi in range(2):
                vs = [
                    x[ael * 8 + an, pl.ds((2 * b_hi + g % 2) * 8, 8), pl.ds((g // 2) * 128, 128)]
                    for g in range(8)
                ]
                for cn, v in enumerate(butterfly(vs)):
                    put(to, cn * 8 + ael * 2 + b_hi, v)

    loop(8, enter)

    def by_nodes(bn, cn):
        return pl.ds(cn * 64 + bn, 8, stride=8)

    def slab(a):
        at = sub(tr, a * 64, 64)
        to = sub(u, a * 64, 64)
        v = {(b, c): at[by_nodes(b, c), :] for b in range(8) for c in range(8)}
        for c in range(8):
            v[(0, c)] = v[(0, c)] + up("b", v[(7, c)])
        for b in range(8):
            v[(b, 0)] = v[(b, 0)] + up("c", v[(b, 7)])
        for (b, c), value in v.items():
            put(to, b * 8 + c, value)

    loop(8, slab)

    for b in range(8):
        for c in range(8):
            t = at8((0, b, c))
            put(u, t, tile(u, t) + up("a", tile(u, at8((7, b, c)))))

    pl.semaphore_wait(pltpu.get_barrier_semaphore(), len(BLOCKS))

    def face_row(name, dim, way, i, vs):
        offset = SLOTS[(name, dim, way)][0]
        if dim == "c":
            put(pk, i if way > 0 else i + 7, pack(dim, way, vs))
        else:
            to = sub(sbuf, offset + 2 * i, 2)
            put(to, 0, pack(dim, way, vs[:4]))
            put(to, 1, pack(dim, way, vs[4:]))

    def send_face(name, dim, way):
        if dim == "c":
            base = 0 if way > 0 else 7
            acc = tile(pk, base)
            for i in range(1, 7):
                acc = jnp.where(lanes // 16 == i, spin(tile(pk, base + i), 0, 16 * i), acc)
            put(sbuf, SLOTS[(name, dim, way)][0], acc)
        send((name, dim, way))

    def spread_c(name, way, base):
        w = tile(rbuf, SLOTS[(name, "c", way)][0])
        for i in range(7):
            put(pk, base + i, spin(w, 0, -16 * i))

    def fine_row(name, dim, way, i, base):
        if dim == "c":
            w = tile(pk, base + i)
            return [unpack(dim, way, w, k) for k in range(7)]
        offset = SLOTS[(name, dim, way)][0]
        at = sub(rbuf, offset + 2 * i, 2)
        lo, hi = tile(at, 0), tile(at, 1)
        return [unpack(dim, way, lo if k < 4 else hi, k % 4) for k in range(7)]

    for dim in ALL_DIMS:
        for i in range(7):
            face_row("S7", dim, 1, i, [tile(u, at8(node(dim, 7, i, k))) for k in range(7)])
        send_face("S7", dim, 1)
    for dims in SUBSETS[3:]:
        key = ("S7", dims, 1)
        for j, t in enumerate(plane(dims, 7, 7)):
            put(sbuf, SLOTS[key][0] + j, tile(u, at8(t)))
        send(key)
    for dims in ("c", "b", "a", "bc", "ac", "ab", "abc"):
        key = ("S7", dims, 1)
        receive(key)
        if dims == "c":
            spread_c("S7", 1, 0)
        elif dims == "a":
            for i in range(7):
                got = fine_row("S7", "a", 1, i, 0)
                for k in range(7):
                    t = at8((0, i, k))
                    put(u, t, tile(u, t) + got[k])
        elif len(dims) > 1:
            for j, t in enumerate(plane(dims, 7, 0)):
                put(u, at8(t), tile(u, at8(t)) + move(dims, 1, tile(rbuf, SLOTS[key][0] + j)))

    def first_fine(a):
        wall = jnp.where(a == 0, wall_a, 1.0)
        from_u, to_rho, to_d = sub(u, a * 64, 64), sub(rho, a * 49, 49), sub(d, a * 49, 49)
        mass_a = by_class(a, [float(1.0 / v) for v in FINE.mass[:4]])
        inverse = inverse_slab(a)
        b_after = fine_row("S7", "b", 1, a, 0)
        c_after = fine_row("S7", "c", 1, a, 0)
        for b in range(7):
            for c in range(7):
                r = tile(from_u, b * 8 + c)
                if b == 0:
                    r = r + b_after[c]
                if c == 0:
                    r = r + c_after[b]
                r = r * (float(1.0 / (FINE.mass[b] * FINE.mass[c])) * mass_a) * wall
                if b == 0:
                    r = r * wall_b
                put(to_rho, b * 7 + c, r)
                put(to_d, b * 7 + c, (inverse(b, c) * float(1.0 / FINE.center)) * r)

    loop(7, first_fine)

    def fine_apply(name, after):
        for dims in ("a", "bc"):

            def faces(i):
                for dim in dims:
                    at, place = line_view(d, dim, i)
                    vs = [[tile(at, place(m, k)) for m in range(7)] for k in range(7)]
                    face_row(name, dim, -1, i, [v[0] for v in vs])
                    face_row(name, dim, 1, i, [partial_end(FINE, v) for v in vs])

            loop(7, faces)
            for dim in dims:
                send_face(name, dim, -1)
                send_face(name, dim, 1)

        def lines(i):
            for dim, y in zip(ALL_DIMS, (ya, yb, yc)):
                at, place = line_view(d, dim, i)
                to, _ = line_view(y, dim, i)
                for k in range(7):
                    got = line(FINE, dim, [tile(at, place(m, k)) for m in range(7)])
                    for m in range(7):
                        put(to, place(m, k), got[m])

        loop(7, lines)

        drain(name)
        for dim in "cba":
            for way in (1, -1):
                receive((name, dim, way))
        spread_c(name, 1, 0)
        spread_c(name, -1, 7)
        for i in range(7):
            got = fine_row(name, "a", -1, i, 0)
            add0 = fine_row(name, "a", 1, i, 0)
            for k in range(7):
                put(ha, i * 7 + k, got[k])
                t = at7((0, i, k))
                put(ya, t, tile(ya, t) + add0[k])

        def finish(a):
            wall = jnp.where(a == 0, wall_a, 1.0)
            gain_a = float(FINE.gain[6, 7])
            for m in range(6):
                gain_a = jnp.where(a == m, float(FINE.gain[m, 7]), gain_a)
            gain_a = splat(gain_a)
            inverse = inverse_slab(a)
            b_before = fine_row(name, "b", -1, a, 0)
            b_after = fine_row(name, "b", 1, a, 0)
            c_before = fine_row(name, "c", -1, a, 7)
            c_after = fine_row(name, "c", 1, a, 0)
            at_rho, at_d, at_x = sub(rho, a * 49, 49), sub(d, a * 49, 49), sub(xs, a * 64, 64)
            at_y = [sub(y, a * 49, 49) for y in (ya, yb, yc)]
            for b in range(7):
                for c in range(7):
                    t, t8 = b * 7 + c, b * 8 + c
                    y = total(tile(part, t) for part in at_y) + gain_a * tile(ha, t)
                    y = y + float(FINE.gain[b, 7]) * b_before[c]
                    y = y + float(FINE.gain[c, 7]) * c_before[b]
                    if b == 0:
                        y = y + b_after[c]
                    if c == 0:
                        y = y + c_after[b]
                    r = (tile(at_rho, t) - y) * wall
                    if b == 0:
                        r = r * wall_b
                    put(at_rho, t, r)
                    if after is None:
                        continue
                    old = tile(at_d, t)
                    if after == "lift":
                        put(at_x, t8, tile(at_x, t8) + old)
                        put(at_d, t, (inverse(b, c) * float(1.0 / FINE.center)) * r)
                        continue
                    new = float(fine_keep) * old + (inverse(b, c) * float(fine_gain)) * r
                    if after == "first":
                        put(at_x, t8, old + new)
                        put(at_d, t, new)
                    else:
                        put(at_x, t8, tile(at_x, t8) + old + new)

        loop(7, finish)

    fine_keep, fine_gain = FINE.factors(2)[0]
    fine_apply("f1", "first")
    fine_apply("f2", None)

    def lower_a(b):
        at, place = line_view(rho, "a", b)
        to = sub(w1, b * 7, 154)
        for c in range(7):
            got = lower_line(FINE, MID, [tile(at, place(m, c)) for m in range(7)])
            for m in range(4):
                put(to, m * 49 + c, got[m])

    loop(7, lower_a)

    def lower_b(a):
        at, to = sub(w1, a * 49, 49), sub(w2, a * 28, 28)
        for c in range(7):
            got = lower_line(FINE, MID, [tile(at, m * 7 + c) for m in range(7)])
            for m in range(4):
                put(to, m * 7 + c, got[m])

    loop(4, lower_b)
    closed = {}
    for a in range(4):
        for b in range(4):
            got = lower_line(FINE, MID, [tile(w2, (a * 4 + b) * 7 + m) for m in range(7)])
            for m in range(4):
                closed[(a, b, m)] = got[m]
    r3 = small_sum(MID, "S3", closed)

    mid_factor = MID.factors(2)[0]
    d3 = first_step(MID, r3)
    r3 = subtract(r3, small_apply(MID, "m1", d3))
    e3 = next_step(MID, mid_factor, d3, r3)
    x3 = add(d3, e3)
    r3 = subtract(r3, small_apply(MID, "m2", e3))

    closed = r3
    for dim in ALL_DIMS:
        new = {}
        others = sorted({tuple(i for dd, i in zip(ALL_DIMS, t) if dd != dim) for t in closed})
        for i, k in others:
            got = lower_line(MID, LOW, [closed[node(dim, m, i, k)] for m in range(3)])
            for m in range(2):
                new[node(dim, m, i, k)] = got[m]
        closed = new
    r1 = small_sum(LOW, "S1", closed)
    here = (0, 0, 0)
    origin = SLOTS[BLOCKS[0]][0]
    put(sbuf, origin, r1[here])

    def block_copy(offset):
        place, _, index = SLOTS[offset]
        src, dst = sbuf.at[pl.ds(origin * 8, 8)], rbuf.at[pl.ds(place * 8, 8)]
        return remote(src, dst, index, device_at(*offset))

    for offset in BLOCKS:
        block_copy(offset).start()
    drain()
    r = {here: r1[here]}
    for offset in BLOCKS:
        block_copy(offset).wait_recv()
        r[tuple(-o for o in offset)] = tile(rbuf, SLOTS[offset][0])

    def up_full(dim, v, before):
        if dim == "a":
            return spin(jnp.where(last["a"], before, v), 2, 0)
        if dim == "b":
            w = jnp.where(odd_lane, jnp.where(odd_row, spin(v, 1, 0), spin(before, -1, 0)), v)
            return jnp.where(odd_lane, spin(w, 0, 1), spin(w, 0, -1))
        t = jnp.where(lanes < 8, spin(v, 0, 10), spin(v, 0, 8))
        return jnp.where(lanes < 2, spin(before, 0, 2), t)

    def down_full(dim, v, after):
        if dim == "a":
            return spin(jnp.where(first["a"], after, v), -2, 0)
        if dim == "b":
            w = jnp.where(odd_lane, v, jnp.where(odd_row, spin(after, 1, 0), spin(v, -1, 0)))
            return jnp.where(odd_lane, spin(w, 0, 1), spin(w, 0, -1))
        t = jnp.where(lanes >= 120, spin(v, 0, -10), spin(v, 0, -8))
        return jnp.where(lanes >= 126, spin(after, 0, -2), t)

    def beside(dim, o, step):
        return tuple(i + step if d == dim else i for d, i in zip(ALL_DIMS, o))

    def both_sides(dim, f, o):
        before, after = f.get(beside(dim, o, -1), f[o]), f.get(beside(dim, o, 1), f[o])
        return up_full(dim, f[o], before) + down_full(dim, f[o], after)

    walls_a, walls_b = {}, {}
    for step in (-1, 0, 1):
        at_a, at_b = lax.rem(gy + step + ny, ny) == 0, lax.rem(gz + step + nz, nz) == 0
        walls_a[step] = jnp.where(first["a"] & at_a, 0.0, 1.0).astype(jnp.float32)
        walls_b[step] = jnp.where(first["b"] & at_b, 0.0, 1.0).astype(jnp.float32)

    own_low = 3.0 * float(LOW.gain[0, 0] + LOW.gain[1, 1])
    side_low = float(LOW.gain[0, 1])
    inverse_low = float(LOW.inverse(0, 0, 0))
    dl = {o: (inverse_low / LOW.center) * v for o, v in r.items()}
    x1 = dict(dl)
    for keep, gain in LOW.factors(COARSE_STEPS):
        new = {}
        for o in r:
            sides = total(both_sides(dim, dl, o) for dim in ALL_DIMS)
            left = r[o] - (own_low * dl[o] + side_low * sides)
            new[o] = left * (walls_a[o[0]] * walls_b[o[1]])
        r = new
        dl = {o: float(keep) * dl[o] + float(gain * inverse_low) * r[o] for o in r}
        x1 = add(x1, dl)

    def corners(f, dims):
        for dim in dims:
            new = {}
            for o, v in f.items():
                new[o] = v if o[ALL_DIMS.index(dim)] == 0 else None
            for o in f:
                if new[o] is None:
                    low = beside(dim, o, -1)
                    new[o] = down_full(dim, f[low], f[o])
            f = new
        return f

    def lift_low(f, dims):
        for dim in dims:
            new = {}
            rest = sorted({tuple(i for d, i in zip(ALL_DIMS, t) if d != dim) for t in f})
            for i, k in rest:
                got = raise_line(MID, LOW, [f[node(dim, m, i, k)] for m in range(2)])
                for m in range(3):
                    new[node(dim, m, i, k)] = got[m]
            f = new
        return f

    ends = list(itertools.product((0, 1), repeat=3))
    c3 = lift_low(corners({o: x1[o] for o in ends}, ALL_DIMS), "cba")
    y = {t: None for t in c3}
    for dim in ALL_DIMS:
        at = ALL_DIMS.index(dim)
        rest = ALL_DIMS.replace(dim, "")
        f = {}
        for o in ends:
            if o[at] == 0:
                f[o] = (x1[o] - 0.5 * both_sides(dim, x1, o)) * float(1.0 / MID.mass[0])
        for t, v in lift_low(corners(f, rest), rest).items():
            y[t] = v if y[t] is None else y[t] + v
    r3 = {t: masked(t, v if y[t] is None else v - y[t]) for t, v in r3.items()}
    d3 = first_step(MID, r3)
    r3 = subtract(r3, small_apply(MID, "m4", d3))
    e3 = next_step(MID, mid_factor, d3, r3)
    t3 = small_close(MID, "C3", add(x3, c3, d3, e3))

    for a in range(4):
        for b in range(4):
            got = raise_line(FINE, MID, [t3[(a, b, m)] for m in range(4)])
            for m in range(7):
                put(w2, (a * 4 + b) * 7 + m, got[m])

    def raise_b(a):
        at, to = sub(w2, a * 28, 28), sub(w1, a * 49, 49)
        for c in range(7):
            got = raise_line(FINE, MID, [tile(at, m * 7 + c) for m in range(4)])
            for m in range(7):
                put(to, m * 7 + c, got[m])

    loop(4, raise_b)

    def raise_a(b):
        at = sub(w1, b * 7, 154)
        to, place = line_view(d, "a", b)
        for c in range(7):
            got = raise_line(FINE, MID, [tile(at, m * 49 + c) for m in range(4)])
            for m in range(7):
                put(to, place(m, c), got[m])

    loop(7, raise_a)
    fine_apply("f3", "lift")
    fine_apply("f4", "post")

    for dim in ALL_DIMS:
        for i in range(7):
            face_row("C7", dim, -1, i, [tile(xs, at8(node(dim, 0, i, k))) for k in range(7)])
        send_face("C7", dim, -1)
    for dims in SUBSETS[3:]:
        key = ("C7", dims, -1)
        for j, t in enumerate(plane(dims, 7, 0)):
            put(sbuf, SLOTS[key][0] + j, tile(xs, at8(t)))
        send(key)
    for dims in SUBSETS:
        receive(("C7", dims, -1))
    spread_c("C7", -1, 0)

    def edge(dims, j):
        return move(dims, -1, tile(rbuf, SLOTS[("C7", dims, -1)][0] + j))

    for dim in ALL_DIMS:
        for i in range(7):
            got = fine_row("C7", dim, -1, i, 0)
            for k in range(7):
                value = down(dim, tile(xs, at8(node(dim, 0, i, k)))) + got[k]
                put(xs, at8(node(dim, 7, i, k)), value)

    hb = fine_row("C7", "b", -1, 0, 0)
    hc_a = fine_row("C7", "c", -1, 0, 0)
    hc_b = [fine_row("C7", "c", -1, i, 0)[0] for i in range(7)]
    for k in range(7):
        value = down("b", tile(xs, at8((7, 0, k)))) + down("a", hb[k]) + edge("ab", k)
        put(xs, at8((7, 7, k)), value)
        value = down("c", tile(xs, at8((7, k, 0)))) + down("a", hc_a[k]) + edge("ac", k)
        put(xs, at8((7, k, 7)), value)
        value = down("c", tile(xs, at8((k, 7, 0)))) + down("b", hc_b[k]) + edge("bc", k)
        put(xs, at8((k, 7, 7)), value)
    value = down("c", tile(xs, at8((7, 7, 0)))) + down("b", down("a", hc_a[0]))
    value = value + down("b", edge("ac", 0)) + down("a", edge("bc", 0)) + edge("abc", 0)
    put(xs, at8((7, 7, 7)), value)

    def leave_nodes(a):
        at, to = sub(xs, a * 64, 64), sub(tr, a * 64, 64)
        for b in range(8):
            for c in range(8):
                to[by_nodes(b, c), :] = tile(at, b * 8 + c)

    loop(8, leave_nodes)

    def leave(an):
        at = sub(tr, an * 64, 64)
        for ael in range(4):
            for b_hi in range(2):
                vs = butterfly([tile(at, cn * 8 + ael * 2 + b_hi) for cn in range(8)])
                for g, v in enumerate(vs):
                    b_at, c_at = pl.ds((2 * b_hi + g % 2) * 8, 8), pl.ds((g // 2) * 128, 128)
                    out[ael * 8 + an, b_at, c_at] = v

    loop(8, leave)
    drain()
    for offset in BLOCKS:
        block_copy(offset).wait_send()


def solution(mesh):
    sizes = tuple(mesh.shape[axis] for axis in ("gx", "gy", "gz"))

    def body(*refs):
        kernel(sizes, *refs)

    def local(residual):
        vmem = lambda count: pltpu.VMEM((count * 8, 128), jnp.float32)
        return pl.pallas_call(
            body,
            out_shape=jax.ShapeDtypeStruct(residual.shape, jnp.float32),
            in_specs=[
                pl.BlockSpec(memory_space=pltpu.VMEM),
            ],
            out_specs=pl.BlockSpec(memory_space=pltpu.VMEM),
            scratch_shapes=[
                vmem(512),
                vmem(512),
                vmem(343),
                vmem(343),
                vmem(343),
                vmem(343),
                vmem(343),
                vmem(512),
                vmem(196),
                vmem(112),
                vmem(49),
                vmem(16),
                vmem(BUF_VREGS),
                vmem(BUF_VREGS),
                pltpu.SemaphoreType.DMA((MESSAGES,)),
                pltpu.SemaphoreType.DMA((MESSAGES,)),
            ],
            compiler_params=pltpu.CompilerParams(
                collective_id=0, has_side_effects=True, vmem_limit_bytes=40 * 1024 * 1024
            ),
        )(residual)

    return jax.shard_map(
        local,
        mesh=mesh,
        in_specs=(P("gy", "gz", "gx"),),
        out_specs=P("gy", "gz", "gx"),
        check_vma=False,
    )
```

```python
import itertools

import jax
import jax.numpy as jnp
import numpy as np
from jax import lax
from jax.experimental import pallas as pl
from jax.experimental.pallas import tpu as pltpu
from jax.sharding import PartitionSpec as P

ORDER = 7
MID_ORDER = 3
COARSE_STEPS = 4


def legendre_pair(degree, points):
    previous = np.ones(points.shape)
    current = points.copy()
    for level in range(1, degree):
        following = ((2 * level + 1) * points * current - level * previous) / (level + 1)
        previous = current
        current = following
    return (current, previous)


def gll_table(degree):
    points = np.cos(np.pi * np.arange(degree + 1) / degree)
    for sweep in range(100):
        current, previous = legendre_pair(degree, points)
        points = points - (points * current - previous) / ((degree + 1) * current)
    points = points[::-1].copy()
    current, previous = legendre_pair(degree, points)
    weights = 2.0 / (degree * (degree + 1) * current**2)
    return (points, weights)


def lagrange_matrix(targets, points):
    point_count = len(points)
    matrix = np.ones((len(targets), point_count))
    for column in range(point_count):
        for partner in range(point_count):
            if partner != column:
                matrix[:, column] *= (targets - points[partner]) / (
                    points[column] - points[partner]
                )
    return matrix


def line_stiffness(degree):
    points, weights = gll_table(degree)
    point_count = len(points)
    barycentric = np.array(
        [
            1.0
            / np.prod(
                [
                    points[column] - points[partner]
                    for partner in range(point_count)
                    if partner != column
                ]
            )
            for column in range(point_count)
        ]
    )
    derivative = np.zeros((point_count, point_count))
    for target in range(point_count):
        for column in range(point_count):
            if target != column:
                derivative[target, column] = (
                    barycentric[column] / barycentric[target] / (points[target] - points[column])
                )
        derivative[target, target] = -np.sum(derivative[target])
    return (derivative.T @ (weights[:, None] * derivative), weights)


def assembled_patterns(degree):
    stiffness, weights = line_stiffness(degree)
    indices = np.arange(len(weights))
    diag_pat = stiffness[indices, indices].copy()
    weight_pat = weights.copy()
    row_pat = np.abs(stiffness).sum(axis=1)
    for pattern in (diag_pat, weight_pat, row_pat):
        shared = pattern[0] + pattern[-1]
        pattern[0] = shared
        pattern[-1] = shared
    return (diag_pat, weight_pat, row_pat)


def three_terms(special, weight_pat):
    return (
        special[:, None, None] * weight_pat[None, :, None] * weight_pat[None, None, :]
        + weight_pat[:, None, None] * special[None, :, None] * weight_pat[None, None, :]
        + weight_pat[:, None, None] * weight_pat[None, :, None] * special[None, None, :]
    )


def chebyshev_bound(degree):
    diag_pat, weight_pat, row_pat = assembled_patterns(degree)
    return float(np.max(three_terms(row_pat, weight_pat) / three_terms(diag_pat, weight_pat)))


class Level:
    def __init__(self, q):
        stiffness, weights = line_stiffness(q)
        diag_pat, weight_pat, row_pat = assembled_patterns(q)
        self.q = self.n = q
        self.half = half = (q + 1) // 2
        self.mass = weight_pat
        self.gain = gain = stiffness / weight_pat[:, None]
        self.even = 0.5 * (gain[:half, :half] + gain[:half, ::-1][:, :half])
        self.odd = 0.5 * (gain[:half, :half] - gain[:half, ::-1][:, :half])
        self.alpha = diag_pat / weight_pat
        upper = chebyshev_bound(q)
        lower = upper / 10.0
        self.center = 0.5 * (upper + lower)
        self.halfwidth = 0.5 * (upper - lower)

    def inverse(self, a, b, c):
        return 1.0 / (self.alpha[a] + self.alpha[b] + self.alpha[c])

    def factors(self, steps):
        scaled = self.center / self.halfwidth
        ratio = 1.0 / scaled
        found = []
        for step in range(1, steps):
            following = 1.0 / (2.0 * scaled - ratio)
            found.append((following * ratio, 2.0 * following / self.halfwidth))
            ratio = following
        return found


FINE, MID, LOW = Level(ORDER), Level(MID_ORDER), Level(1)
ALL_DIMS = "abc"
SUBSETS = ("a", "b", "c", "ab", "ac", "bc", "abc")
BLOCKS = [o for o in itertools.product((-1, 0, 1), repeat=3) if any(o)]


def node(dim, m, i, k):
    return {"a": (m, i, k), "b": (i, m, k), "c": (i, k, m)}[dim]


def face_vregs(n, dim):
    return 1 if dim == "c" else n * -(-n // 4)


def plan():
    slots, size, count = {}, 0, 0

    def add(key, length):
        nonlocal size, count
        slots[key] = (size, length, count)
        size += length
        count += 1

    for name, n in (
        ("f1", 7), ("f2", 7), ("f3", 7), ("f4", 7),
        ("m1", 3), ("m2", 3), ("m4", 3),
    ):
        for dim in ALL_DIMS:
            for way in (1, -1):
                add((name, dim, way), face_vregs(n, dim))
    for name, n, way in (("S7", 7, 1), ("S3", 3, 1), ("S1", 1, 1), ("C3", 3, -1), ("C7", 7, -1)):
        for dims in SUBSETS:
            add((name, dims, way), face_vregs(n, dims) if len(dims) == 1 else 1)
    for offset in BLOCKS:
        add(offset, 1)
    return slots, -(-size // 8) * 8, count


SLOTS, BUF_VREGS, MESSAGES = plan()


def total(terms):
    out = None
    for term in terms:
        if term is not None:
            out = term if out is None else out + term
    return out


def mix(coefs, values):
    return total(
        None if abs(coef) < 1e-13 else float(coef) * value for coef, value in zip(coefs, values)
    )


def kernel(sizes, x_hbm, out, x, tr, u, rho, d, ya, yb, yc, xs, w1, w2, ha, pk, sbuf, rbuf, ssem, rsem, xsem):
    nx, ny, nz = sizes
    gx, gy, gz = lax.axis_index("gx"), lax.axis_index("gy"), lax.axis_index("gz")
    rows = lax.broadcasted_iota(jnp.int32, (8, 128), 0)
    lanes = lax.broadcasted_iota(jnp.int32, (8, 128), 1)
    odd_row, odd_lane = rows % 2 == 1, lanes % 2 == 1
    first = {"a": rows < 2, "b": (rows % 2 == 0) & (lanes % 2 == 0), "c": lanes < 2}
    last = {"a": rows >= 6, "b": odd_row & odd_lane, "c": lanes >= 126}
    wall_a = jnp.where(first["a"] & (gy == 0), 0.0, 1.0).astype(jnp.float32)
    wall_b = jnp.where(first["b"] & (gz == 0), 0.0, 1.0).astype(jnp.float32)

    def spin(v, row, lane):
        if row % 8:
            v = pltpu.roll(v, row % 8, 0)
        if lane % 128:
            v = pltpu.roll(v, lane % 128, 1)
        return v

    def up(dim, v):
        if dim == "a":
            return jnp.where(rows >= 2, spin(v, 2, 0), 0.0)
        if dim == "b":
            w = jnp.where(odd_lane, jnp.where(odd_row, spin(v, 1, 0), 0.0), v)
            return jnp.where(odd_lane, spin(w, 0, 1), spin(w, 0, -1))
        t = jnp.where(lanes < 8, spin(v, 0, 10), spin(v, 0, 8))
        return jnp.where(lanes < 2, 0.0, t)

    def down(dim, v):
        if dim == "a":
            return jnp.where(rows < 6, spin(v, -2, 0), 0.0)
        if dim == "b":
            w = jnp.where(odd_lane, v, jnp.where(odd_row, 0.0, spin(v, -1, 0)))
            return jnp.where(odd_lane, spin(w, 0, 1), spin(w, 0, -1))
        t = jnp.where(lanes >= 120, spin(v, 0, -10), spin(v, 0, -8))
        return jnp.where(lanes >= 126, 0.0, t)

    def pack(dim, way, vs):
        acc = None
        for j, v in enumerate(vs):
            if dim == "a":
                v, mask = spin(v, 2 * j + (2 if way > 0 else 0), 0), rows // 2 == j
            elif dim == "b":
                js, jl = j % 2, j // 2
                back = 1 if way > 0 else 0
                v, mask = spin(v, js - back, jl - back), (rows % 2 == js) & (lanes % 2 == jl)
            else:
                v, mask = spin(v, 0, 2 * j + (2 if way > 0 else 0)), lanes // 2 == j
            acc = v if acc is None else jnp.where(mask, v, acc)
        return acc

    def unpack(dim, way, w, j):
        if dim == "a":
            w = spin(w, -2 * j if way > 0 else 6 - 2 * j, 0)
        elif dim == "b":
            js, jl = j % 2, j // 2
            w = spin(w, -js, -jl) if way > 0 else spin(w, 1 - js, 1 - jl)
        else:
            w = spin(w, 0, -2 * j if way > 0 else 126 - 2 * j)
        return jnp.where((first if way > 0 else last)[dim], w, 0.0)

    def move(dims, way, v):
        row = (2 if "a" in dims else 0) - (1 if "b" in dims else 0)
        lane = (2 if "c" in dims else 0) - (1 if "b" in dims else 0)
        mask = None
        for dim in dims:
            part = (first if way > 0 else last)[dim]
            mask = part if mask is None else mask & part
        return jnp.where(mask, spin(v, way * row, way * lane), 0.0)

    def guarded(key, way, run):
        if "a" in key[1]:
            pl.when(gy < ny - 1 if way > 0 else gy > 0)(run)
        else:
            run()

    def edge_spin(dims, way, v, j):
        return spin(v, way * j, 0) if dims == "ab" else spin(v, 0, way * 2 * j)

    def send_edge(name, dims, way, vs):
        acc = total(edge_spin(dims, way, move(dims, way, v), j) for j, v in enumerate(vs))
        put(sbuf, SLOTS[(name, dims, way)][0], acc)
        send((name, dims, way))

    def load_edge(name, dims, way, count):
        w = tile(rbuf, SLOTS[(name, dims, way)][0])
        mask = None
        for dim in dims:
            part = (first if way > 0 else last)[dim]
            mask = part if mask is None else mask & part
        return [jnp.where(mask, edge_spin(dims, -way, w, j), 0.0) for j in range(count)]

    def device_at(da, db, dc):
        return {
            "gx": lax.rem(gx + dc + nx, nx) if dc else gx,
            "gy": lax.rem(gy + da + ny, ny) if da else gy,
            "gz": lax.rem(gz + db + nz, nz) if db else gz,
        }

    def remote(src, dst, index, device):
        return pltpu.make_async_remote_copy(
            src_ref=src,
            dst_ref=dst,
            send_sem=ssem.at[index],
            recv_sem=rsem.at[index],
            device_id=device,
            device_id_type=pl.DeviceIdType.MESH,
        )

    def copy_of(key):
        name, dims, way = key
        offset, length, index = SLOTS[key]
        part = pl.ds(offset * 8, length * 8)
        device = device_at(*(way if dim in dims else 0 for dim in ALL_DIMS))
        return remote(sbuf.at[part], rbuf.at[part], index, device)

    pending = []

    def send(key):
        guarded(key, key[2], lambda: copy_of(key).start())
        pending.append(key)

    def receive(key):
        guarded(key, -key[2], lambda: copy_of(key).wait_recv())

    def drain(keep=None):
        for key in list(pending):
            if key[0] != keep:
                guarded(key, key[2], lambda: copy_of(key).wait_send())
                pending.remove(key)

    def tile(ref, index):
        start = index * 8
        if not isinstance(index, int):
            start = pl.multiple_of(start, 8)
        return ref[pl.ds(start, 8), :]

    def put(ref, index, value):
        start = index * 8
        if not isinstance(index, int):
            start = pl.multiple_of(start, 8)
        ref[pl.ds(start, 8), :] = value

    def sub(ref, base, length):
        start = base * 8
        if not isinstance(base, int):
            start = pl.multiple_of(start, 8)
        return ref.at[pl.ds(start, length * 8)]

    def line_view(ref, dim, i):
        if dim == "a":
            return sub(ref, i * 7, 301), lambda m, k: m * 49 + k
        return sub(ref, i * 49, 49), (lambda m, k: m * 7 + k) if dim == "b" else (
            lambda m, k: k * 7 + m
        )

    def by_class(i, values):
        picked = jnp.where((i == 2) | (i == 5), values[2], values[3])
        picked = jnp.where((i == 1) | (i == 6), values[1], picked)
        return jnp.where(i == 0, values[0], picked)

    def splat(value):
        return jnp.full((8, 128), value, jnp.float32)

    def inverse_slab(a):
        alpha = splat(by_class(a, [float(v) for v in FINE.alpha[:4]]))
        found = {}
        for b in range(4):
            for c in range(b, 4):
                found[(b, c)] = 1.0 / (alpha + float(FINE.alpha[b] + FINE.alpha[c]))
        return lambda b, c: found[tuple(sorted((min(b, 7 - b), min(c, 7 - c))))]

    def at7(t):
        return (t[0] * 7 + t[1]) * 7 + t[2]

    def at8(t):
        return (t[0] * 8 + t[1]) * 8 + t[2]

    def loop(count, body):
        def step(i, carry):
            body(i)
            return carry

        lax.fori_loop(0, count, step, 0)

    def line(lv, dim, v):
        q, half = lv.q, lv.half
        full = list(v) + [down(dim, v[0])]
        e = [full[j] + full[q - j] for j in range(half)]
        o = [full[j] - full[q - j] for j in range(half)]
        y = [None] * (q + 1)
        for i in range(half):
            ev, od = mix(lv.even[i], e), mix(lv.odd[i], o)
            y[i] = od if ev is None else ev + od
            y[q - i] = -od if ev is None else ev - od
        own = jnp.where(first[dim], float(lv.gain[q, q]), 0.0)
        y[0] = y[0] + up(dim, y[q]) + own * v[0]
        return y[:q]

    def partial_end(lv, v):
        return mix(lv.gain[lv.q, : lv.q], v)

    def lower_line(hi, lo, v):
        jmat = lagrange_matrix(gll_table(hi.q)[0], gll_table(lo.q)[0])
        r = jmat.T * hi.mass[None, :] / lo.mass[:, None]
        inner = range(1, hi.half)
        e = [v[n] + v[hi.q - n] for n in inner]
        o = [v[n] - v[hi.q - n] for n in inner]
        y = [None] * (lo.q + 1)
        for m in range(lo.half):
            ev = mix([0.5 * (r[m, n] + r[m, hi.q - n]) for n in inner], e)
            od = mix([0.5 * (r[m, n] - r[m, hi.q - n]) for n in inner], o)
            y[m], y[lo.q - m] = ev + od, ev - od
        y[0] = y[0] + float(r[0, 0]) * v[0]
        return y

    def raise_line(hi, lo, v):
        jmat = lagrange_matrix(gll_table(hi.q)[0], gll_table(lo.q)[0])
        e = [v[m] + v[lo.q - m] for m in range(lo.half)]
        o = [v[m] - v[lo.q - m] for m in range(lo.half)]
        y = [None] * (hi.q + 1)
        y[0] = v[0]
        for n in range(1, hi.half):
            ev = mix([0.5 * (jmat[n, m] + jmat[n, lo.q - m]) for m in range(lo.half)], e)
            od = mix([0.5 * (jmat[n, m] - jmat[n, lo.q - m]) for m in range(lo.half)], o)
            y[n], y[hi.q - n] = ev + od, ev - od
        return y[: hi.q]


    def store_face(name, dim, way, n, get):
        offset = SLOTS[(name, dim, way)][0]
        if dim == "c":
            acc = None
            for i in range(n):
                w = pack(dim, way, [get(i, k) for k in range(n)])
                acc = w if acc is None else jnp.where(lanes // 8 == i, spin(w, 0, 8 * i), acc)
            put(sbuf, offset, acc)
        else:
            for i in range(n):
                put(sbuf, offset + i, pack(dim, way, [get(i, k) for k in range(n)]))
        send((name, dim, way))

    def load_face(name, dim, way, n):
        offset = SLOTS[(name, dim, way)][0]
        receive((name, dim, way))
        if dim == "c":
            w = tile(rbuf, offset)
            return [[unpack(dim, way, spin(w, 0, -8 * i), k) for k in range(n)] for i in range(n)]
        return [
            [unpack(dim, way, tile(rbuf, offset + i), k) for k in range(n)] for i in range(n)
        ]

    def small_apply(lv, name, dv):
        n = lv.n
        for dim in ALL_DIMS:
            store_face(name, dim, -1, n, lambda i, k: dv[node(dim, 0, i, k)])
            store_face(
                name, dim, 1, n,
                lambda i, k: partial_end(lv, [dv[node(dim, m, i, k)] for m in range(n)]),
            )
        y = {}
        for dim in ALL_DIMS:
            for i in range(n):
                for k in range(n):
                    got = line(lv, dim, [dv[node(dim, m, i, k)] for m in range(n)])
                    for m in range(n):
                        t = node(dim, m, i, k)
                        y[t] = got[m] if t not in y else y[t] + got[m]
        drain(name)
        for dim in ALL_DIMS:
            before = load_face(name, dim, -1, n)
            after = load_face(name, dim, 1, n)
            for i in range(n):
                for k in range(n):
                    for m in range(n):
                        t = node(dim, m, i, k)
                        y[t] = y[t] + float(lv.gain[m, lv.q]) * before[i][k]
                    t = node(dim, 0, i, k)
                    y[t] = y[t] + after[i][k]
        return y

    def masked(t, v):
        if t[0] == 0:
            v = v * wall_a
        if t[1] == 0:
            v = v * wall_b
        return v

    def small_sum(lv, name, closed):
        n, q = lv.n, lv.q
        for dim in ALL_DIMS:
            for i in range(q + 1):
                for k in range(q + 1):
                    low, high = node(dim, 0, i, k), node(dim, q, i, k)
                    closed[low] = closed[low] + up(dim, closed[high])
        for dim in ALL_DIMS:
            store_face(name, dim, 1, n, lambda i, k: closed[node(dim, q, i, k)])
        for dims in SUBSETS[3:]:
            send_edge(name, dims, 1, [closed[t] for t in plane(dims, n, q)])
        drain(name)
        r = {t: closed[t] for t in itertools.product(range(n), repeat=3)}
        for dim in ALL_DIMS:
            got = load_face(name, dim, 1, n)
            for i in range(n):
                for k in range(n):
                    t = node(dim, 0, i, k)
                    r[t] = r[t] + got[i][k]
        for dims in SUBSETS[3:]:
            receive((name, dims, 1))
            places = plane(dims, n, 0)
            for t, v in zip(places, load_edge(name, dims, 1, len(places))):
                r[t] = r[t] + v
        return {t: masked(t, v) for t, v in r.items()}

    def plane(dims, n, end):
        ranges = [[end] if dim in dims else range(n) for dim in ALL_DIMS]
        return list(itertools.product(*ranges))

    def small_close(lv, name, v):
        n, q = lv.n, lv.q
        for dim in ALL_DIMS:
            store_face(name, dim, -1, n, lambda i, k: v[node(dim, 0, i, k)])
        for dims in SUBSETS[3:]:
            send_edge(name, dims, -1, [v[t] for t in plane(dims, n, 0)])
        drain(name)
        halo = {}
        for dim in ALL_DIMS:
            got = load_face(name, dim, -1, n)
            for i in range(n):
                for k in range(n):
                    halo[(dim, node(dim, q, i, k))] = got[i][k]
        for dims in SUBSETS[3:]:
            receive((name, dims, -1))
            places = plane(dims, n, q)
            for t, got in zip(places, load_edge(name, dims, -1, len(places))):
                halo[(dims, t)] = got
        return closure(lv, dict(v), halo)

    def closure(lv, field, halo):
        n, q = lv.n, lv.q

        def value(have, t):
            ends = "".join(dim for dim, i in zip(ALL_DIMS, t) if i == q and dim not in have)
            if not ends:
                return halo[(have, t)] if have else field[t]
            dim = ends[0]
            low = tuple(0 if d == dim else i for d, i in zip(ALL_DIMS, t))
            with_dim = "".join(d for d in ALL_DIMS if d in have or d == dim)
            return down(dim, value(have, low)) + value(with_dim, t)

        return {t: value("", t) for t in itertools.product(range(q + 1), repeat=3)}

    def first_step(lv, r):
        return {t: float(lv.inverse(*t) / lv.center) * v for t, v in r.items()}

    def next_step(lv, factor, dv, r):
        keep, gain = factor
        return {t: float(keep) * dv[t] + float(gain * lv.inverse(*t)) * r[t] for t in r}

    def subtract(r, y):
        return {t: masked(t, r[t] - y[t]) for t in r}

    def add(*fields):
        return {t: total(f[t] for f in fields) for t in fields[0]}

    for an in (7, 0, 1, 2, 3, 4, 5, 6):
        pltpu.make_async_copy(x_hbm.at[:, an], x.at[:, an], xsem.at[an]).start()

    def zero_block(i):
        rbuf[pl.ds(pl.multiple_of(i * 64, 64), 64), :] = jnp.zeros((64, 128), jnp.float32)

    loop(BUF_VREGS // 8, zero_block)

    for offset in BLOCKS:
        pl.semaphore_signal(
            pltpu.get_barrier_semaphore(),
            inc=1,
            device_id=device_at(*offset),
            device_id_type=pl.DeviceIdType.MESH,
        )

    def butterfly(vs):
        for bit in (1, 2, 4):
            new = list(vs)
            low = (lanes // bit) % 2 == 0
            for i in range(8):
                if not i & bit:
                    lo, hi = vs[i], vs[i + bit]
                    new[i] = jnp.where(low, lo, spin(hi, 0, bit))
                    new[i + bit] = jnp.where(low, spin(lo, 0, -bit), hi)
            vs = new
        return vs

    def enter(an):
        to = sub(tr, an * 64, 64)
        for ael in range(4):
            for b_hi in range(2):
                vs = [
                    x[ael, an, pl.ds((2 * b_hi + g % 2) * 8, 8), pl.ds((g // 2) * 128, 128)]
                    for g in range(8)
                ]
                for cn, v in enumerate(butterfly(vs)):
                    put(to, cn * 8 + ael * 2 + b_hi, v)

    def by_nodes(bn, cn):
        return pl.ds(cn * 64 + bn, 8, stride=8)

    def slab(a):
        at = sub(tr, a * 64, 64)
        to = sub(u, a * 64, 64)
        v = {(b, c): at[by_nodes(b, c), :] for b in range(8) for c in range(8)}
        for c in range(8):
            v[(0, c)] = v[(0, c)] + up("b", v[(7, c)])
        for b in range(8):
            v[(b, 0)] = v[(b, 0)] + up("c", v[(b, 7)])
        for (b, c), value in v.items():
            put(to, b * 8 + c, value)

    fetch = [
        pltpu.make_async_copy(x_hbm.at[:, an], x.at[:, an], xsem.at[an]) for an in range(8)
    ]

    def face_row(name, dim, way, i, vs):
        offset = SLOTS[(name, dim, way)][0]
        if dim == "c":
            put(pk, i if way > 0 else i + 7, pack(dim, way, vs))
        else:
            to = sub(sbuf, offset + 2 * i, 2)
            put(to, 0, pack(dim, way, vs[:4]))
            put(to, 1, pack(dim, way, vs[4:]))

    def send_face(name, dim, way):
        if dim == "c":
            base = 0 if way > 0 else 7
            acc = tile(pk, base)
            for i in range(1, 7):
                acc = jnp.where(lanes // 16 == i, spin(tile(pk, base + i), 0, 16 * i), acc)
            put(sbuf, SLOTS[(name, dim, way)][0], acc)
        send((name, dim, way))

    def spread_c(name, way, base):
        w = tile(rbuf, SLOTS[(name, "c", way)][0])
        for i in range(7):
            put(pk, base + i, spin(w, 0, -16 * i))

    def fine_row(name, dim, way, i, base):
        if dim == "c":
            w = tile(pk, base + i)
            return [unpack(dim, way, w, k) for k in range(7)]
        offset = SLOTS[(name, dim, way)][0]
        at = sub(rbuf, offset + 2 * i, 2)
        lo, hi = tile(at, 0), tile(at, 1)
        return [unpack(dim, way, lo if k < 4 else hi, k % 4) for k in range(7)]

    def start_sum(dims):
        if len(dims) > 1:
            send_edge("S7", dims, 1, [tile(u, at8(t)) for t in plane(dims, 7, 7)])
            return
        for i in range(7):
            face_row("S7", dims, 1, i, [tile(u, at8(node(dims, 7, i, k))) for k in range(7)])
        send_face("S7", dims, 1)

    fetch[7].wait()
    enter(7)
    slab(7)
    pl.semaphore_wait(pltpu.get_barrier_semaphore(), len(BLOCKS))
    for dims in ("a", "ab", "ac", "abc"):
        start_sum(dims)
    for an in range(7):
        fetch[an].wait()
    loop(7, enter)
    loop(7, slab)
    for b in range(8):
        for c in range(8):
            t = at8((0, b, c))
            put(u, t, tile(u, t) + up("a", tile(u, at8((7, b, c)))))
    for dims in ("c", "b", "bc"):
        start_sum(dims)

    for dims in ("c", "b", "a", "bc", "ac", "ab", "abc"):
        key = ("S7", dims, 1)
        receive(key)
        if dims == "c":
            spread_c("S7", 1, 0)
        elif dims == "a":
            for i in range(7):
                got = fine_row("S7", "a", 1, i, 0)
                for k in range(7):
                    t = at8((0, i, k))
                    put(u, t, tile(u, t) + got[k])
        elif len(dims) > 1:
            places = plane(dims, 7, 0)
            for t, v in zip(places, load_edge("S7", dims, 1, len(places))):
                put(u, at8(t), tile(u, at8(t)) + v)

    def first_fine(a):
        wall = jnp.where(a == 0, wall_a, 1.0)
        from_u, to_rho, to_d = sub(u, a * 64, 64), sub(rho, a * 49, 49), sub(d, a * 49, 49)
        mass_a = by_class(a, [float(1.0 / v) for v in FINE.mass[:4]])
        inverse = inverse_slab(a)
        b_after = fine_row("S7", "b", 1, a, 0)
        c_after = fine_row("S7", "c", 1, a, 0)
        for b in range(7):
            for c in range(7):
                r = tile(from_u, b * 8 + c)
                if b == 0:
                    r = r + b_after[c]
                if c == 0:
                    r = r + c_after[b]
                r = r * (float(1.0 / (FINE.mass[b] * FINE.mass[c])) * mass_a) * wall
                if b == 0:
                    r = r * wall_b
                put(to_rho, b * 7 + c, r)
                put(to_d, b * 7 + c, (inverse(b, c) * float(1.0 / FINE.center)) * r)

    loop(7, first_fine)

    def fine_apply(name, after):
        for dims in ("a", "bc"):

            def faces(i):
                for dim in dims:
                    at, place = line_view(d, dim, i)
                    vs = [[tile(at, place(m, k)) for m in range(7)] for k in range(7)]
                    face_row(name, dim, -1, i, [v[0] for v in vs])
                    face_row(name, dim, 1, i, [partial_end(FINE, v) for v in vs])

            loop(7, faces)
            for dim in dims:
                send_face(name, dim, -1)
                send_face(name, dim, 1)

        def lines(i):
            for dim, y in zip(ALL_DIMS, (ya, yb, yc)):
                at, place = line_view(d, dim, i)
                to, _ = line_view(y, dim, i)
                for k in range(7):
                    got = line(FINE, dim, [tile(at, place(m, k)) for m in range(7)])
                    for m in range(7):
                        put(to, place(m, k), got[m])

        loop(7, lines)

        drain(name)
        for dim in "cba":
            for way in (1, -1):
                receive((name, dim, way))
        spread_c(name, 1, 0)
        spread_c(name, -1, 7)
        for i in range(7):
            got = fine_row(name, "a", -1, i, 0)
            add0 = fine_row(name, "a", 1, i, 0)
            for k in range(7):
                put(ha, i * 7 + k, got[k])
                t = at7((0, i, k))
                put(ya, t, tile(ya, t) + add0[k])

        def finish(a):
            wall = jnp.where(a == 0, wall_a, 1.0)
            gain_a = float(FINE.gain[6, 7])
            for m in range(6):
                gain_a = jnp.where(a == m, float(FINE.gain[m, 7]), gain_a)
            gain_a = splat(gain_a)
            inverse = inverse_slab(a)
            b_before = fine_row(name, "b", -1, a, 0)
            b_after = fine_row(name, "b", 1, a, 0)
            c_before = fine_row(name, "c", -1, a, 7)
            c_after = fine_row(name, "c", 1, a, 0)
            at_rho, at_d, at_x = sub(rho, a * 49, 49), sub(d, a * 49, 49), sub(xs, a * 64, 64)
            at_y = [sub(y, a * 49, 49) for y in (ya, yb, yc)]
            for b in range(7):
                for c in range(7):
                    t, t8 = b * 7 + c, b * 8 + c
                    y = total(tile(part, t) for part in at_y) + gain_a * tile(ha, t)
                    y = y + float(FINE.gain[b, 7]) * b_before[c]
                    y = y + float(FINE.gain[c, 7]) * c_before[b]
                    if b == 0:
                        y = y + b_after[c]
                    if c == 0:
                        y = y + c_after[b]
                    r = (tile(at_rho, t) - y) * wall
                    if b == 0:
                        r = r * wall_b
                    put(at_rho, t, r)
                    if after is None:
                        continue
                    old = tile(at_d, t)
                    if after == "lift":
                        put(at_x, t8, tile(at_x, t8) + old)
                        put(at_d, t, (inverse(b, c) * float(1.0 / FINE.center)) * r)
                        continue
                    new = float(fine_keep) * old + (inverse(b, c) * float(fine_gain)) * r
                    if after == "first":
                        put(at_x, t8, old + new)
                        put(at_d, t, new)
                    else:
                        put(at_x, t8, tile(at_x, t8) + old + new)

        finish(0)
        if after == "post":
            for dims in ("a", "ab", "ac", "abc"):
                start_close(dims)
        loop(6, lambda a: finish(a + 1))

    def start_close(dims):
        if len(dims) > 1:
            send_edge("C7", dims, -1, [tile(xs, at8(t)) for t in plane(dims, 7, 0)])
            return
        for i in range(7):
            face_row("C7", dims, -1, i, [tile(xs, at8(node(dims, 0, i, k))) for k in range(7)])
        send_face("C7", dims, -1)

    fine_keep, fine_gain = FINE.factors(2)[0]
    fine_apply("f1", "first")
    fine_apply("f2", None)

    def lower_a(b):
        at, place = line_view(rho, "a", b)
        to = sub(w1, b * 7, 154)
        for c in range(7):
            got = lower_line(FINE, MID, [tile(at, place(m, c)) for m in range(7)])
            for m in range(4):
                put(to, m * 49 + c, got[m])

    loop(7, lower_a)

    def lower_b(a):
        at, to = sub(w1, a * 49, 49), sub(w2, a * 28, 28)
        for c in range(7):
            got = lower_line(FINE, MID, [tile(at, m * 7 + c) for m in range(7)])
            for m in range(4):
                put(to, m * 7 + c, got[m])

    loop(4, lower_b)
    closed = {}
    for a in range(4):
        for b in range(4):
            got = lower_line(FINE, MID, [tile(w2, (a * 4 + b) * 7 + m) for m in range(7)])
            for m in range(4):
                closed[(a, b, m)] = got[m]
    r3 = small_sum(MID, "S3", closed)

    mid_factor = MID.factors(2)[0]
    d3 = first_step(MID, r3)
    r3 = subtract(r3, small_apply(MID, "m1", d3))
    e3 = next_step(MID, mid_factor, d3, r3)
    x3 = add(d3, e3)
    r3 = subtract(r3, small_apply(MID, "m2", e3))

    closed = r3
    for dim in ALL_DIMS:
        new = {}
        others = sorted({tuple(i for dd, i in zip(ALL_DIMS, t) if dd != dim) for t in closed})
        for i, k in others:
            got = lower_line(MID, LOW, [closed[node(dim, m, i, k)] for m in range(3)])
            for m in range(2):
                new[node(dim, m, i, k)] = got[m]
        closed = new
    r1 = small_sum(LOW, "S1", closed)
    here = (0, 0, 0)
    origin = SLOTS[BLOCKS[0]][0]
    put(sbuf, origin, r1[here])

    def block_copy(offset):
        place, _, index = SLOTS[offset]
        src, dst = sbuf.at[pl.ds(origin * 8, 8)], rbuf.at[pl.ds(place * 8, 8)]
        return remote(src, dst, index, device_at(*offset))

    def block_copies(way, act):
        for step in (1, 0, -1):
            group = [o for o in BLOCKS if o[0] == step]

            def run():
                for offset in group:
                    act(block_copy(offset))

            if step:
                pl.when(gy < ny - 1 if step * way > 0 else gy > 0)(run)
            else:
                run()

    block_copies(1, lambda copy: copy.start())
    drain()
    block_copies(-1, lambda copy: copy.wait_recv())
    r = {here: r1[here]}
    for offset in BLOCKS:
        r[tuple(-o for o in offset)] = tile(rbuf, SLOTS[offset][0])

    def up_full(dim, v, before):
        if dim == "a":
            return spin(jnp.where(last["a"], before, v), 2, 0)
        if dim == "b":
            w = jnp.where(odd_lane, jnp.where(odd_row, spin(v, 1, 0), spin(before, -1, 0)), v)
            return jnp.where(odd_lane, spin(w, 0, 1), spin(w, 0, -1))
        t = jnp.where(lanes < 8, spin(v, 0, 10), spin(v, 0, 8))
        return jnp.where(lanes < 2, spin(before, 0, 2), t)

    def down_full(dim, v, after):
        if dim == "a":
            return spin(jnp.where(first["a"], after, v), -2, 0)
        if dim == "b":
            w = jnp.where(odd_lane, v, jnp.where(odd_row, spin(after, 1, 0), spin(v, -1, 0)))
            return jnp.where(odd_lane, spin(w, 0, 1), spin(w, 0, -1))
        t = jnp.where(lanes >= 120, spin(v, 0, -10), spin(v, 0, -8))
        return jnp.where(lanes >= 126, spin(after, 0, -2), t)

    def beside(dim, o, step):
        return tuple(i + step if d == dim else i for d, i in zip(ALL_DIMS, o))

    def both_sides(dim, f, o):
        before, after = f.get(beside(dim, o, -1), f[o]), f.get(beside(dim, o, 1), f[o])
        return up_full(dim, f[o], before) + down_full(dim, f[o], after)

    walls_a, walls_b = {}, {}
    for step in (-1, 0, 1):
        at_a, at_b = lax.rem(gy + step + ny, ny) == 0, lax.rem(gz + step + nz, nz) == 0
        walls_a[step] = jnp.where(first["a"] & at_a, 0.0, 1.0).astype(jnp.float32)
        walls_b[step] = jnp.where(first["b"] & at_b, 0.0, 1.0).astype(jnp.float32)

    own_low = 3.0 * float(LOW.gain[0, 0] + LOW.gain[1, 1])
    side_low = float(LOW.gain[0, 1])
    inverse_low = float(LOW.inverse(0, 0, 0))
    dl = {o: (inverse_low / LOW.center) * v for o, v in r.items()}
    x1 = dict(dl)
    for keep, gain in LOW.factors(COARSE_STEPS):
        new = {}
        for o in r:
            sides = total(both_sides(dim, dl, o) for dim in ALL_DIMS)
            left = r[o] - (own_low * dl[o] + side_low * sides)
            new[o] = left * (walls_a[o[0]] * walls_b[o[1]])
        r = new
        dl = {o: float(keep) * dl[o] + float(gain * inverse_low) * r[o] for o in r}
        x1 = add(x1, dl)

    def corners(f, dims):
        for dim in dims:
            new = {}
            for o, v in f.items():
                new[o] = v if o[ALL_DIMS.index(dim)] == 0 else None
            for o in f:
                if new[o] is None:
                    low = beside(dim, o, -1)
                    new[o] = down_full(dim, f[low], f[o])
            f = new
        return f

    def lift_low(f, dims):
        for dim in dims:
            new = {}
            rest = sorted({tuple(i for d, i in zip(ALL_DIMS, t) if d != dim) for t in f})
            for i, k in rest:
                got = raise_line(MID, LOW, [f[node(dim, m, i, k)] for m in range(2)])
                for m in range(3):
                    new[node(dim, m, i, k)] = got[m]
            f = new
        return f

    ends = list(itertools.product((0, 1), repeat=3))
    c3 = lift_low(corners({o: x1[o] for o in ends}, ALL_DIMS), "cba")
    y = {t: None for t in c3}
    for dim in ALL_DIMS:
        at = ALL_DIMS.index(dim)
        rest = ALL_DIMS.replace(dim, "")
        f = {}
        for o in ends:
            if o[at] == 0:
                f[o] = (x1[o] - 0.5 * both_sides(dim, x1, o)) * float(1.0 / MID.mass[0])
        for t, v in lift_low(corners(f, rest), rest).items():
            y[t] = v if y[t] is None else y[t] + v
    r3 = {t: masked(t, v if y[t] is None else v - y[t]) for t, v in r3.items()}
    d3 = first_step(MID, r3)
    r3 = subtract(r3, small_apply(MID, "m4", d3))
    e3 = next_step(MID, mid_factor, d3, r3)
    t3 = small_close(MID, "C3", add(x3, c3, d3, e3))

    for a in range(4):
        for b in range(4):
            got = raise_line(FINE, MID, [t3[(a, b, m)] for m in range(4)])
            for m in range(7):
                put(w2, (a * 4 + b) * 7 + m, got[m])

    def raise_b(a):
        at, to = sub(w2, a * 28, 28), sub(w1, a * 49, 49)
        for c in range(7):
            got = raise_line(FINE, MID, [tile(at, m * 7 + c) for m in range(4)])
            for m in range(7):
                put(to, m * 7 + c, got[m])

    loop(4, raise_b)

    def raise_a(b):
        at = sub(w1, b * 7, 154)
        to, place = line_view(d, "a", b)
        for c in range(7):
            got = raise_line(FINE, MID, [tile(at, m * 49 + c) for m in range(4)])
            for m in range(7):
                put(to, place(m, c), got[m])

    loop(7, raise_a)
    fine_apply("f3", "lift")
    fine_apply("f4", "post")

    for dims in ("b", "c", "bc"):
        start_close(dims)

    def leave_nodes(a):
        at, to = sub(xs, a * 64, 64), sub(tr, a * 64, 64)
        for b in range(8):
            for c in range(8):
                to[by_nodes(b, c), :] = tile(at, b * 8 + c)

    def leave(an):
        at = sub(tr, an * 64, 64)
        for ael in range(4):
            for b_hi in range(2):
                vs = butterfly([tile(at, cn * 8 + ael * 2 + b_hi) for cn in range(8)])
                for g, v in enumerate(vs):
                    b_at, c_at = pl.ds((2 * b_hi + g % 2) * 8, 8), pl.ds((g // 2) * 128, 128)
                    out[ael * 8 + an, b_at, c_at] = v

    def end_face(dim):
        for i in range(7):
            got = fine_row("C7", dim, -1, i, 0)
            for k in range(7):
                value = down(dim, tile(xs, at8(node(dim, 0, i, k)))) + got[k]
                put(xs, at8(node(dim, 7, i, k)), value)

    for dims in ("b", "c", "bc"):
        receive(("C7", dims, -1))
    spread_c("C7", -1, 0)
    end_face("b")
    end_face("c")
    hb = fine_row("C7", "b", -1, 0, 0)
    hc_a = fine_row("C7", "c", -1, 0, 0)
    hc_b = [fine_row("C7", "c", -1, i, 0)[0] for i in range(7)]
    edge_bc = load_edge("C7", "bc", -1, 7)
    for k in range(7):
        value = down("c", tile(xs, at8((k, 7, 0)))) + down("b", hc_b[k]) + edge_bc[k]
        put(xs, at8((k, 7, 7)), value)
    loop(7, leave_nodes)
    loop(7, leave)

    for dims in ("a", "ab", "ac", "abc"):
        receive(("C7", dims, -1))
    end_face("a")
    edge_ab, edge_ac = load_edge("C7", "ab", -1, 7), load_edge("C7", "ac", -1, 7)
    for k in range(7):
        value = down("b", tile(xs, at8((7, 0, k)))) + down("a", hb[k]) + edge_ab[k]
        put(xs, at8((7, 7, k)), value)
        value = down("c", tile(xs, at8((7, k, 0)))) + down("a", hc_a[k]) + edge_ac[k]
        put(xs, at8((7, k, 7)), value)
    value = down("c", tile(xs, at8((7, 7, 0)))) + down("b", down("a", hc_a[0]))
    value = value + down("b", edge_ac[0]) + down("a", edge_bc[0])
    put(xs, at8((7, 7, 7)), value + load_edge("C7", "abc", -1, 1)[0])
    leave_nodes(7)
    leave(7)
    drain()
    block_copies(1, lambda copy: copy.wait_send())


def solution(mesh):
    sizes = tuple(mesh.shape[axis] for axis in ("gx", "gy", "gz"))

    def body(*refs):
        kernel(sizes, *refs)

    def local(residual):
        vmem = lambda count: pltpu.VMEM((count * 8, 128), jnp.float32)
        return pl.pallas_call(
            body,
            out_shape=jax.ShapeDtypeStruct(residual.shape, jnp.float32),
            in_specs=[
                pl.BlockSpec(memory_space=pl.ANY),
            ],
            out_specs=pl.BlockSpec(memory_space=pltpu.VMEM),
            scratch_shapes=[
                pltpu.VMEM((4, 8, 32, 512), jnp.float32),
                vmem(512),
                vmem(512),
                vmem(343),
                vmem(343),
                vmem(343),
                vmem(343),
                vmem(343),
                vmem(512),
                vmem(196),
                vmem(112),
                vmem(49),
                vmem(16),
                vmem(BUF_VREGS),
                vmem(BUF_VREGS),
                pltpu.SemaphoreType.DMA((MESSAGES,)),
                pltpu.SemaphoreType.DMA((MESSAGES,)),
                pltpu.SemaphoreType.DMA((8,)),
            ],
            compiler_params=pltpu.CompilerParams(
                collective_id=0, has_side_effects=True, vmem_limit_bytes=40 * 1024 * 1024
            ),
        )(residual.reshape(4, 8, 32, 512))

    return jax.shard_map(
        local,
        mesh=mesh,
        in_specs=(P("gy", "gz", "gx"),),
        out_specs=P("gy", "gz", "gx"),
        check_vma=False,
    )
```

```python
import itertools

import jax
import jax.numpy as jnp
import numpy as np
from jax import lax
from jax.experimental import pallas as pl
from jax.experimental.pallas import tpu as pltpu
from jax.sharding import PartitionSpec as P

ORDER = 7
MID_ORDER = 3
COARSE_STEPS = 4


def legendre_pair(degree, points):
    previous = np.ones(points.shape)
    current = points.copy()
    for level in range(1, degree):
        following = ((2 * level + 1) * points * current - level * previous) / (level + 1)
        previous = current
        current = following
    return (current, previous)


def gll_table(degree):
    points = np.cos(np.pi * np.arange(degree + 1) / degree)
    for sweep in range(100):
        current, previous = legendre_pair(degree, points)
        points = points - (points * current - previous) / ((degree + 1) * current)
    points = points[::-1].copy()
    current, previous = legendre_pair(degree, points)
    weights = 2.0 / (degree * (degree + 1) * current**2)
    return (points, weights)


def lagrange_matrix(targets, points):
    point_count = len(points)
    matrix = np.ones((len(targets), point_count))
    for column in range(point_count):
        for partner in range(point_count):
            if partner != column:
                matrix[:, column] *= (targets - points[partner]) / (
                    points[column] - points[partner]
                )
    return matrix


def line_stiffness(degree):
    points, weights = gll_table(degree)
    point_count = len(points)
    barycentric = np.array(
        [
            1.0
            / np.prod(
                [
                    points[column] - points[partner]
                    for partner in range(point_count)
                    if partner != column
                ]
            )
            for column in range(point_count)
        ]
    )
    derivative = np.zeros((point_count, point_count))
    for target in range(point_count):
        for column in range(point_count):
            if target != column:
                derivative[target, column] = (
                    barycentric[column] / barycentric[target] / (points[target] - points[column])
                )
        derivative[target, target] = -np.sum(derivative[target])
    return (derivative.T @ (weights[:, None] * derivative), weights)


def assembled_patterns(degree):
    stiffness, weights = line_stiffness(degree)
    indices = np.arange(len(weights))
    diag_pat = stiffness[indices, indices].copy()
    weight_pat = weights.copy()
    row_pat = np.abs(stiffness).sum(axis=1)
    for pattern in (diag_pat, weight_pat, row_pat):
        shared = pattern[0] + pattern[-1]
        pattern[0] = shared
        pattern[-1] = shared
    return (diag_pat, weight_pat, row_pat)


def three_terms(special, weight_pat):
    return (
        special[:, None, None] * weight_pat[None, :, None] * weight_pat[None, None, :]
        + weight_pat[:, None, None] * special[None, :, None] * weight_pat[None, None, :]
        + weight_pat[:, None, None] * weight_pat[None, :, None] * special[None, None, :]
    )


def chebyshev_bound(degree):
    diag_pat, weight_pat, row_pat = assembled_patterns(degree)
    return float(np.max(three_terms(row_pat, weight_pat) / three_terms(diag_pat, weight_pat)))


class Level:
    def __init__(self, q):
        stiffness, weights = line_stiffness(q)
        diag_pat, weight_pat, row_pat = assembled_patterns(q)
        self.q = self.n = q
        self.half = half = (q + 1) // 2
        self.mass = weight_pat
        self.gain = gain = stiffness / weight_pat[:, None]
        self.even = 0.5 * (gain[:half, :half] + gain[:half, ::-1][:, :half])
        self.odd = 0.5 * (gain[:half, :half] - gain[:half, ::-1][:, :half])
        self.alpha = diag_pat / weight_pat
        upper = chebyshev_bound(q)
        lower = upper / 10.0
        self.center = 0.5 * (upper + lower)
        self.halfwidth = 0.5 * (upper - lower)

    def inverse(self, a, b, c):
        return 1.0 / (self.alpha[a] + self.alpha[b] + self.alpha[c])

    def factors(self, steps):
        scaled = self.center / self.halfwidth
        ratio = 1.0 / scaled
        found = []
        for step in range(1, steps):
            following = 1.0 / (2.0 * scaled - ratio)
            found.append((following * ratio, 2.0 * following / self.halfwidth))
            ratio = following
        return found


FINE, MID, LOW = Level(ORDER), Level(MID_ORDER), Level(1)
ALL_DIMS = "abc"
SUBSETS = ("a", "b", "c", "ab", "ac", "bc", "abc")
BLOCKS = [o for o in itertools.product((-1, 0, 1), repeat=3) if any(o)]


def node(dim, m, i, k):
    return {"a": (m, i, k), "b": (i, m, k), "c": (i, k, m)}[dim]


def face_vregs(n, dim):
    return 1 if dim == "c" else n * -(-n // 4)


def plan():
    slots, size, count = {}, 0, 0

    def add(key, length):
        nonlocal size, count
        slots[key] = (size, length, count)
        size += length
        count += 1

    for name, n in (
        ("f1", 7), ("f2", 7), ("f3", 7), ("f4", 7),
        ("m1", 3), ("m2", 3), ("m4", 3),
    ):
        for dim in ALL_DIMS:
            for way in (1, -1):
                add((name, dim, way), face_vregs(n, dim))
    for name, n, way in (("S7", 7, 1), ("S3", 3, 1), ("S1", 1, 1), ("C3", 3, -1), ("C7", 7, -1)):
        for dims in SUBSETS:
            add((name, dims, way), face_vregs(n, dims) if len(dims) == 1 else 1)
    for offset in BLOCKS:
        add(offset, 1)
    return slots, -(-size // 8) * 8, count


SLOTS, BUF_VREGS, MESSAGES = plan()


def total(terms):
    out = None
    for term in terms:
        if term is not None:
            out = term if out is None else out + term
    return out


def mix(coefs, values):
    return total(
        None if abs(coef) < 1e-13 else float(coef) * value for coef, value in zip(coefs, values)
    )


def kernel(sizes, x_hbm, out, x, tr, u, rho, d, ya, yb, yc, xs, w1, w2, ha, pk, sbuf, rbuf, ssem, rsem, xsem):
    nx, ny, nz = sizes
    gx, gy, gz = lax.axis_index("gx"), lax.axis_index("gy"), lax.axis_index("gz")
    rows = lax.broadcasted_iota(jnp.int32, (8, 128), 0)
    lanes = lax.broadcasted_iota(jnp.int32, (8, 128), 1)
    odd_row, odd_lane = rows % 2 == 1, lanes % 2 == 1
    first = {"a": rows < 2, "b": (rows % 2 == 0) & (lanes % 2 == 0), "c": lanes < 2}
    last = {"a": rows >= 6, "b": odd_row & odd_lane, "c": lanes >= 126}
    wall_a = jnp.where(first["a"] & (gy == 0), 0.0, 1.0).astype(jnp.float32)
    wall_b = jnp.where(first["b"] & (gz == 0), 0.0, 1.0).astype(jnp.float32)

    def spin(v, row, lane):
        if row % 8:
            v = pltpu.roll(v, row % 8, 0)
        if lane % 128:
            v = pltpu.roll(v, lane % 128, 1)
        return v

    def up(dim, v):
        if dim == "a":
            return jnp.where(rows >= 2, spin(v, 2, 0), 0.0)
        if dim == "b":
            w = jnp.where(odd_lane, jnp.where(odd_row, spin(v, 1, 0), 0.0), v)
            return jnp.where(odd_lane, spin(w, 0, 1), spin(w, 0, -1))
        t = jnp.where(lanes < 8, spin(v, 0, 10), spin(v, 0, 8))
        return jnp.where(lanes < 2, 0.0, t)

    def down(dim, v):
        if dim == "a":
            return jnp.where(rows < 6, spin(v, -2, 0), 0.0)
        if dim == "b":
            w = jnp.where(odd_lane, v, jnp.where(odd_row, 0.0, spin(v, -1, 0)))
            return jnp.where(odd_lane, spin(w, 0, 1), spin(w, 0, -1))
        t = jnp.where(lanes >= 120, spin(v, 0, -10), spin(v, 0, -8))
        return jnp.where(lanes >= 126, 0.0, t)

    def pack(dim, way, vs):
        acc = None
        for j, v in enumerate(vs):
            if dim == "a":
                v, mask = spin(v, 2 * j + (2 if way > 0 else 0), 0), rows // 2 == j
            elif dim == "b":
                js, jl = j % 2, j // 2
                back = 1 if way > 0 else 0
                v, mask = spin(v, js - back, jl - back), (rows % 2 == js) & (lanes % 2 == jl)
            else:
                v, mask = spin(v, 0, 2 * j + (2 if way > 0 else 0)), lanes // 2 == j
            acc = v if acc is None else jnp.where(mask, v, acc)
        return acc

    def unpack(dim, way, w, j):
        if dim == "a":
            w = spin(w, -2 * j if way > 0 else 6 - 2 * j, 0)
        elif dim == "b":
            js, jl = j % 2, j // 2
            w = spin(w, -js, -jl) if way > 0 else spin(w, 1 - js, 1 - jl)
        else:
            w = spin(w, 0, -2 * j if way > 0 else 126 - 2 * j)
        return jnp.where((first if way > 0 else last)[dim], w, 0.0)

    def move(dims, way, v):
        row = (2 if "a" in dims else 0) - (1 if "b" in dims else 0)
        lane = (2 if "c" in dims else 0) - (1 if "b" in dims else 0)
        mask = None
        for dim in dims:
            part = (first if way > 0 else last)[dim]
            mask = part if mask is None else mask & part
        return jnp.where(mask, spin(v, way * row, way * lane), 0.0)

    def guarded(key, way, run):
        if "a" in key[1]:
            pl.when(gy < ny - 1 if way > 0 else gy > 0)(run)
        else:
            run()

    def edge_spin(dims, way, v, j):
        return spin(v, way * j, 0) if dims == "ab" else spin(v, 0, way * 2 * j)

    def send_edge(name, dims, way, vs):
        acc = total(edge_spin(dims, way, move(dims, way, v), j) for j, v in enumerate(vs))
        put(sbuf, SLOTS[(name, dims, way)][0], acc)
        send((name, dims, way))

    def load_edge(name, dims, way, count):
        w = tile(rbuf, SLOTS[(name, dims, way)][0])
        mask = None
        for dim in dims:
            part = (first if way > 0 else last)[dim]
            mask = part if mask is None else mask & part
        return [jnp.where(mask, edge_spin(dims, -way, w, j), 0.0) for j in range(count)]

    def device_at(da, db, dc):
        return {
            "gx": lax.rem(gx + dc + nx, nx) if dc else gx,
            "gy": lax.rem(gy + da + ny, ny) if da else gy,
            "gz": lax.rem(gz + db + nz, nz) if db else gz,
        }

    def remote(src, dst, index, device):
        return pltpu.make_async_remote_copy(
            src_ref=src,
            dst_ref=dst,
            send_sem=ssem.at[index],
            recv_sem=rsem.at[index],
            device_id=device,
            device_id_type=pl.DeviceIdType.MESH,
        )

    turn = [0]

    def slot(key):
        name, dims, way = key
        if name != "f":
            return SLOTS[key]
        offset, length, index = SLOTS[("f1", dims, way)]
        shift = [SLOTS[("f2", dims, way)][i] - SLOTS[("f1", dims, way)][i] for i in (0, 2)]
        return offset + turn[0] * shift[0], length, index + turn[0] * shift[1]

    def copy_of(key):
        name, dims, way = key
        offset, length, index = slot(key)
        start = offset * 8
        part = pl.ds(start if isinstance(start, int) else pl.multiple_of(start, 8), length * 8)
        device = device_at(*(way if dim in dims else 0 for dim in ALL_DIMS))
        return remote(sbuf.at[part], rbuf.at[part], index, device)

    pending = []

    def send(key):
        guarded(key, key[2], lambda: copy_of(key).start())
        if key[0] != "f":
            pending.append(key)

    def receive(key):
        guarded(key, -key[2], lambda: copy_of(key).wait_recv())

    def drain(keep=None):
        for key in list(pending):
            if key[0] != keep:
                guarded(key, key[2], lambda: copy_of(key).wait_send())
                pending.remove(key)

    def tile(ref, index):
        start = index * 8
        if not isinstance(index, int):
            start = pl.multiple_of(start, 8)
        return ref[pl.ds(start, 8), :]

    def put(ref, index, value):
        start = index * 8
        if not isinstance(index, int):
            start = pl.multiple_of(start, 8)
        ref[pl.ds(start, 8), :] = value

    def sub(ref, base, length):
        start = base * 8
        if not isinstance(base, int):
            start = pl.multiple_of(start, 8)
        return ref.at[pl.ds(start, length * 8)]

    def line_view(ref, dim, i):
        if dim == "a":
            return sub(ref, i * 7, 301), lambda m, k: m * 49 + k
        return sub(ref, i * 49, 49), (lambda m, k: m * 7 + k) if dim == "b" else (
            lambda m, k: k * 7 + m
        )

    def by_class(i, values):
        picked = jnp.where((i == 2) | (i == 5), values[2], values[3])
        picked = jnp.where((i == 1) | (i == 6), values[1], picked)
        return jnp.where(i == 0, values[0], picked)

    def splat(value):
        return jnp.full((8, 128), value, jnp.float32)

    def inverse_slab(a):
        alpha = splat(by_class(a, [float(v) for v in FINE.alpha[:4]]))
        found = {}
        for b in range(4):
            for c in range(b, 4):
                found[(b, c)] = 1.0 / (alpha + float(FINE.alpha[b] + FINE.alpha[c]))
        return lambda b, c: found[tuple(sorted((min(b, 7 - b), min(c, 7 - c))))]

    def at7(t):
        return (t[0] * 7 + t[1]) * 7 + t[2]

    def at8(t):
        return (t[0] * 8 + t[1]) * 8 + t[2]

    def loop(count, body):
        def step(i, carry):
            body(i)
            return carry

        lax.fori_loop(0, count, step, 0)

    def line(lv, dim, v):
        q, half = lv.q, lv.half
        full = list(v) + [down(dim, v[0])]
        e = [full[j] + full[q - j] for j in range(half)]
        o = [full[j] - full[q - j] for j in range(half)]
        y = [None] * (q + 1)
        for i in range(half):
            ev, od = mix(lv.even[i], e), mix(lv.odd[i], o)
            y[i] = od if ev is None else ev + od
            y[q - i] = -od if ev is None else ev - od
        own = jnp.where(first[dim], float(lv.gain[q, q]), 0.0)
        y[0] = y[0] + up(dim, y[q]) + own * v[0]
        return y[:q]

    def partial_end(lv, v):
        return mix(lv.gain[lv.q, : lv.q], v)

    def lower_line(hi, lo, v):
        jmat = lagrange_matrix(gll_table(hi.q)[0], gll_table(lo.q)[0])
        r = jmat.T * hi.mass[None, :] / lo.mass[:, None]
        inner = range(1, hi.half)
        e = [v[n] + v[hi.q - n] for n in inner]
        o = [v[n] - v[hi.q - n] for n in inner]
        y = [None] * (lo.q + 1)
        for m in range(lo.half):
            ev = mix([0.5 * (r[m, n] + r[m, hi.q - n]) for n in inner], e)
            od = mix([0.5 * (r[m, n] - r[m, hi.q - n]) for n in inner], o)
            y[m], y[lo.q - m] = ev + od, ev - od
        y[0] = y[0] + float(r[0, 0]) * v[0]
        return y

    def raise_line(hi, lo, v):
        jmat = lagrange_matrix(gll_table(hi.q)[0], gll_table(lo.q)[0])
        e = [v[m] + v[lo.q - m] for m in range(lo.half)]
        o = [v[m] - v[lo.q - m] for m in range(lo.half)]
        y = [None] * (hi.q + 1)
        y[0] = v[0]
        for n in range(1, hi.half):
            ev = mix([0.5 * (jmat[n, m] + jmat[n, lo.q - m]) for m in range(lo.half)], e)
            od = mix([0.5 * (jmat[n, m] - jmat[n, lo.q - m]) for m in range(lo.half)], o)
            y[n], y[hi.q - n] = ev + od, ev - od
        return y[: hi.q]


    def store_face(name, dim, way, n, get):
        offset = SLOTS[(name, dim, way)][0]
        if dim == "c":
            acc = None
            for i in range(n):
                w = pack(dim, way, [get(i, k) for k in range(n)])
                acc = w if acc is None else jnp.where(lanes // 8 == i, spin(w, 0, 8 * i), acc)
            put(sbuf, offset, acc)
        else:
            for i in range(n):
                put(sbuf, offset + i, pack(dim, way, [get(i, k) for k in range(n)]))
        send((name, dim, way))

    def load_face(name, dim, way, n):
        offset = SLOTS[(name, dim, way)][0]
        receive((name, dim, way))
        if dim == "c":
            w = tile(rbuf, offset)
            return [[unpack(dim, way, spin(w, 0, -8 * i), k) for k in range(n)] for i in range(n)]
        return [
            [unpack(dim, way, tile(rbuf, offset + i), k) for k in range(n)] for i in range(n)
        ]

    def small_apply(lv, name, dv):
        n = lv.n
        for dim in ALL_DIMS:
            store_face(name, dim, -1, n, lambda i, k: dv[node(dim, 0, i, k)])
            store_face(
                name, dim, 1, n,
                lambda i, k: partial_end(lv, [dv[node(dim, m, i, k)] for m in range(n)]),
            )
        y = {}
        for dim in ALL_DIMS:
            for i in range(n):
                for k in range(n):
                    got = line(lv, dim, [dv[node(dim, m, i, k)] for m in range(n)])
                    for m in range(n):
                        t = node(dim, m, i, k)
                        y[t] = got[m] if t not in y else y[t] + got[m]
        drain(name)
        for dim in "cba":
            before = load_face(name, dim, -1, n)
            after = load_face(name, dim, 1, n)
            for i in range(n):
                for k in range(n):
                    for m in range(n):
                        t = node(dim, m, i, k)
                        y[t] = y[t] + float(lv.gain[m, lv.q]) * before[i][k]
                    t = node(dim, 0, i, k)
                    y[t] = y[t] + after[i][k]
        return y

    def masked(t, v):
        if t[0] == 0:
            v = v * wall_a
        if t[1] == 0:
            v = v * wall_b
        return v

    def small_sum(lv, name, closed):
        n, q = lv.n, lv.q
        for dim in ALL_DIMS:
            for i in range(q + 1):
                for k in range(q + 1):
                    low, high = node(dim, 0, i, k), node(dim, q, i, k)
                    closed[low] = closed[low] + up(dim, closed[high])
        for dim in ALL_DIMS:
            store_face(name, dim, 1, n, lambda i, k: closed[node(dim, q, i, k)])
        for dims in SUBSETS[3:]:
            send_edge(name, dims, 1, [closed[t] for t in plane(dims, n, q)])
        drain(name)
        r = {t: closed[t] for t in itertools.product(range(n), repeat=3)}
        for dim in "cba":
            got = load_face(name, dim, 1, n)
            for i in range(n):
                for k in range(n):
                    t = node(dim, 0, i, k)
                    r[t] = r[t] + got[i][k]
        for dims in ("bc", "ab", "ac", "abc"):
            receive((name, dims, 1))
            places = plane(dims, n, 0)
            for t, v in zip(places, load_edge(name, dims, 1, len(places))):
                r[t] = r[t] + v
        return {t: masked(t, v) for t, v in r.items()}

    def plane(dims, n, end):
        ranges = [[end] if dim in dims else range(n) for dim in ALL_DIMS]
        return list(itertools.product(*ranges))

    def small_close(lv, name, v):
        n, q = lv.n, lv.q
        for dim in ALL_DIMS:
            store_face(name, dim, -1, n, lambda i, k: v[node(dim, 0, i, k)])
        for dims in SUBSETS[3:]:
            send_edge(name, dims, -1, [v[t] for t in plane(dims, n, 0)])
        drain(name)
        halo = {}
        for dim in "cba":
            got = load_face(name, dim, -1, n)
            for i in range(n):
                for k in range(n):
                    halo[(dim, node(dim, q, i, k))] = got[i][k]
        for dims in SUBSETS[3:]:
            receive((name, dims, -1))
            places = plane(dims, n, q)
            for t, got in zip(places, load_edge(name, dims, -1, len(places))):
                halo[(dims, t)] = got
        return closure(lv, dict(v), halo)

    def closure(lv, field, halo):
        n, q = lv.n, lv.q

        def value(have, t):
            ends = "".join(dim for dim, i in zip(ALL_DIMS, t) if i == q and dim not in have)
            if not ends:
                return halo[(have, t)] if have else field[t]
            dim = ends[0]
            low = tuple(0 if d == dim else i for d, i in zip(ALL_DIMS, t))
            with_dim = "".join(d for d in ALL_DIMS if d in have or d == dim)
            return down(dim, value(have, low)) + value(with_dim, t)

        return {t: value("", t) for t in itertools.product(range(q + 1), repeat=3)}

    def first_step(lv, r):
        return {t: float(lv.inverse(*t) / lv.center) * v for t, v in r.items()}

    def next_step(lv, factor, dv, r):
        keep, gain = factor
        return {t: float(keep) * dv[t] + float(gain * lv.inverse(*t)) * r[t] for t in r}

    def subtract(r, y):
        return {t: masked(t, r[t] - y[t]) for t in r}

    def add(*fields):
        return {t: total(f[t] for f in fields) for t in fields[0]}

    for an in (7, 0, 1, 2, 3, 4, 5, 6):
        pltpu.make_async_copy(x_hbm.at[:, an], x.at[:, an], xsem.at[an]).start()

    def zero_block(i):
        rbuf[pl.ds(pl.multiple_of(i * 64, 64), 64), :] = jnp.zeros((64, 128), jnp.float32)

    loop(BUF_VREGS // 8, zero_block)

    for offset in BLOCKS:
        pl.semaphore_signal(
            pltpu.get_barrier_semaphore(),
            inc=1,
            device_id=device_at(*offset),
            device_id_type=pl.DeviceIdType.MESH,
        )

    def butterfly(vs):
        for bit in (1, 2, 4):
            new = list(vs)
            low = (lanes // bit) % 2 == 0
            for i in range(8):
                if not i & bit:
                    lo, hi = vs[i], vs[i + bit]
                    new[i] = jnp.where(low, lo, spin(hi, 0, bit))
                    new[i + bit] = jnp.where(low, spin(lo, 0, -bit), hi)
            vs = new
        return vs

    def enter(an):
        to = sub(tr, an * 64, 64)
        for ael in range(4):
            for b_hi in range(2):
                vs = [
                    x[ael, an, pl.ds((2 * b_hi + g % 2) * 8, 8), pl.ds((g // 2) * 128, 128)]
                    for g in range(8)
                ]
                for cn, v in enumerate(butterfly(vs)):
                    put(to, cn * 8 + ael * 2 + b_hi, v)

    def by_nodes(bn, cn):
        return pl.ds(cn * 64 + bn, 8, stride=8)

    def slab(a):
        at = sub(tr, a * 64, 64)
        to = sub(u, a * 64, 64)
        v = {(b, c): at[by_nodes(b, c), :] for b in range(8) for c in range(8)}
        for c in range(8):
            v[(0, c)] = v[(0, c)] + up("b", v[(7, c)])
        for b in range(8):
            v[(b, 0)] = v[(b, 0)] + up("c", v[(b, 7)])
        for (b, c), value in v.items():
            put(to, b * 8 + c, value)

    fetch = [
        pltpu.make_async_copy(x_hbm.at[:, an], x.at[:, an], xsem.at[an]) for an in range(8)
    ]

    def face_row(name, dim, way, i, vs):
        offset = slot((name, dim, way))[0]
        if dim == "c":
            put(pk, i if way > 0 else i + 7, pack(dim, way, vs))
        else:
            to = sub(sbuf, offset + 2 * i, 2)
            put(to, 0, pack(dim, way, vs[:4]))
            put(to, 1, pack(dim, way, vs[4:]))

    def send_face(name, dim, way):
        if dim == "c":
            base = 0 if way > 0 else 7
            acc = tile(pk, base)
            for i in range(1, 7):
                acc = jnp.where(lanes // 16 == i, spin(tile(pk, base + i), 0, 16 * i), acc)
            put(sbuf, slot((name, dim, way))[0], acc)
        send((name, dim, way))

    def spread_c(name, way, base):
        w = tile(rbuf, slot((name, "c", way))[0])
        for i in range(7):
            put(pk, base + i, spin(w, 0, -16 * i))

    def fine_row(name, dim, way, i, base):
        if dim == "c":
            w = tile(pk, base + i)
            return [unpack(dim, way, w, k) for k in range(7)]
        offset = slot((name, dim, way))[0]
        at = sub(rbuf, offset + 2 * i, 2)
        lo, hi = tile(at, 0), tile(at, 1)
        return [unpack(dim, way, lo if k < 4 else hi, k % 4) for k in range(7)]

    def start_sum(dims):
        if len(dims) > 1:
            send_edge("S7", dims, 1, [tile(u, at8(t)) for t in plane(dims, 7, 7)])
            return
        for i in range(7):
            face_row("S7", dims, 1, i, [tile(u, at8(node(dims, 7, i, k))) for k in range(7)])
        send_face("S7", dims, 1)

    fetch[7].wait()
    enter(7)
    slab(7)
    pl.semaphore_wait(pltpu.get_barrier_semaphore(), len(BLOCKS))
    for dims in ("a", "ab", "ac", "abc"):
        start_sum(dims)
    for an in range(7):
        fetch[an].wait()
    loop(7, enter)
    loop(7, slab)
    for b in range(8):
        for c in range(8):
            t = at8((0, b, c))
            put(u, t, tile(u, t) + up("a", tile(u, at8((7, b, c)))))
    for dims in ("c", "b", "bc"):
        start_sum(dims)

    for dims in ("c", "b", "a", "bc", "ac", "ab", "abc"):
        key = ("S7", dims, 1)
        receive(key)
        if dims == "c":
            spread_c("S7", 1, 0)
        elif dims == "a":
            for i in range(7):
                got = fine_row("S7", "a", 1, i, 0)
                for k in range(7):
                    t = at8((0, i, k))
                    put(u, t, tile(u, t) + got[k])
        elif len(dims) > 1:
            places = plane(dims, 7, 0)
            for t, v in zip(places, load_edge("S7", dims, 1, len(places))):
                put(u, at8(t), tile(u, at8(t)) + v)

    def first_fine(a):
        wall = jnp.where(a == 0, wall_a, 1.0)
        from_u, to_rho, to_d = sub(u, a * 64, 64), sub(rho, a * 49, 49), sub(d, a * 49, 49)
        to_x = sub(xs, a * 64, 64)
        mass_a = by_class(a, [float(1.0 / v) for v in FINE.mass[:4]])
        inverse = inverse_slab(a)
        b_after = fine_row("S7", "b", 1, a, 0)
        c_after = fine_row("S7", "c", 1, a, 0)
        for b in range(7):
            for c in range(7):
                r = tile(from_u, b * 8 + c)
                if b == 0:
                    r = r + b_after[c]
                if c == 0:
                    r = r + c_after[b]
                r = r * (float(1.0 / (FINE.mass[b] * FINE.mass[c])) * mass_a) * wall
                if b == 0:
                    r = r * wall_b
                put(to_rho, b * 7 + c, r)
                put(to_x, b * 8 + c, jnp.zeros((8, 128), jnp.float32))
                put(to_d, b * 7 + c, (inverse(b, c) * float(1.0 / FINE.center)) * r)

    loop(7, first_fine)
    drain()

    def fine_apply(it):
        name = "f"
        turn[0] = it
        ends = (it == 0) | (it == 3)
        for dims in ("a", "bc"):

            def faces(i):
                for dim in dims:
                    at, place = line_view(d, dim, i)
                    vs = [[tile(at, place(m, k)) for m in range(7)] for k in range(7)]
                    face_row(name, dim, -1, i, [v[0] for v in vs])
                    face_row(name, dim, 1, i, [partial_end(FINE, v) for v in vs])

            loop(7, faces)
            for dim in dims:
                send_face(name, dim, -1)
                send_face(name, dim, 1)

        def lines(i):
            for dim, y in zip(ALL_DIMS, (ya, yb, yc)):
                at, place = line_view(d, dim, i)
                to, _ = line_view(y, dim, i)
                for k in range(7):
                    got = line(FINE, dim, [tile(at, place(m, k)) for m in range(7)])
                    for m in range(7):
                        put(to, place(m, k), got[m])

        loop(7, lines)

        for dim in "cba":
            for way in (1, -1):
                receive((name, dim, way))
        spread_c(name, 1, 0)
        spread_c(name, -1, 7)
        for i in range(7):
            got = fine_row(name, "a", -1, i, 0)
            add0 = fine_row(name, "a", 1, i, 0)
            for k in range(7):
                put(ha, i * 7 + k, got[k])
                t = at7((0, i, k))
                put(ya, t, tile(ya, t) + add0[k])

        def finish(a):
            wall = jnp.where(a == 0, wall_a, 1.0)
            gain_a = float(FINE.gain[6, 7])
            for m in range(6):
                gain_a = jnp.where(a == m, float(FINE.gain[m, 7]), gain_a)
            gain_a = splat(gain_a)
            inverse = inverse_slab(a)
            keep = splat(jnp.where(ends, float(fine_keep), 0.0))
            gain = splat(jnp.where(it == 2, float(1.0 / FINE.center), float(fine_gain)))
            old_part = splat(jnp.where(it == 1, 0.0, 1.0))
            new_part = splat(jnp.where(ends, 1.0, 0.0))
            b_before = fine_row(name, "b", -1, a, 0)
            b_after = fine_row(name, "b", 1, a, 0)
            c_before = fine_row(name, "c", -1, a, 7)
            c_after = fine_row(name, "c", 1, a, 0)
            at_rho, at_d, at_x = sub(rho, a * 49, 49), sub(d, a * 49, 49), sub(xs, a * 64, 64)
            at_y = [sub(y, a * 49, 49) for y in (ya, yb, yc)]
            for b in range(7):
                for c in range(7):
                    t, t8 = b * 7 + c, b * 8 + c
                    y = total(tile(part, t) for part in at_y) + gain_a * tile(ha, t)
                    y = y + float(FINE.gain[b, 7]) * b_before[c]
                    y = y + float(FINE.gain[c, 7]) * c_before[b]
                    if b == 0:
                        y = y + b_after[c]
                    if c == 0:
                        y = y + c_after[b]
                    r = (tile(at_rho, t) - y) * wall
                    if b == 0:
                        r = r * wall_b
                    put(at_rho, t, r)
                    old = tile(at_d, t)
                    new = keep * old + (inverse(b, c) * gain) * r
                    put(at_x, t8, tile(at_x, t8) + (old_part * old + new_part * new))
                    put(at_d, t, new)

        def slab_end(a):
            finish(a)

            @pl.when((a == 0) & (it == 3))
            def _():
                for dims in ("a", "ab", "ac", "abc"):
                    start_close(dims)

        loop(7, slab_end)
        for dim in ALL_DIMS:
            for way in (1, -1):
                key = (name, dim, way)
                guarded(key, way, lambda: copy_of(key).wait_send())

    def start_close(dims):
        if len(dims) > 1:
            send_edge("C7", dims, -1, [tile(xs, at8(t)) for t in plane(dims, 7, 0)])
            return
        for i in range(7):
            face_row("C7", dims, -1, i, [tile(xs, at8(node(dims, 0, i, k))) for k in range(7)])
        send_face("C7", dims, -1)

    fine_keep, fine_gain = FINE.factors(2)[0]
    def coarse():
        def lower_a(b):
            at, place = line_view(rho, "a", b)
            to = sub(w1, b * 7, 154)
            for c in range(7):
                got = lower_line(FINE, MID, [tile(at, place(m, c)) for m in range(7)])
                for m in range(4):
                    put(to, m * 49 + c, got[m])

        loop(7, lower_a)

        def lower_b(a):
            at, to = sub(w1, a * 49, 49), sub(w2, a * 28, 28)
            for c in range(7):
                got = lower_line(FINE, MID, [tile(at, m * 7 + c) for m in range(7)])
                for m in range(4):
                    put(to, m * 7 + c, got[m])

        loop(4, lower_b)
        closed = {}
        for a in range(4):
            for b in range(4):
                got = lower_line(FINE, MID, [tile(w2, (a * 4 + b) * 7 + m) for m in range(7)])
                for m in range(4):
                    closed[(a, b, m)] = got[m]
        r3 = small_sum(MID, "S3", closed)

        mid_factor = MID.factors(2)[0]
        d3 = first_step(MID, r3)
        r3 = subtract(r3, small_apply(MID, "m1", d3))
        e3 = next_step(MID, mid_factor, d3, r3)
        x3 = add(d3, e3)
        r3 = subtract(r3, small_apply(MID, "m2", e3))

        closed = r3
        for dim in ALL_DIMS:
            new = {}
            others = sorted({tuple(i for dd, i in zip(ALL_DIMS, t) if dd != dim) for t in closed})
            for i, k in others:
                got = lower_line(MID, LOW, [closed[node(dim, m, i, k)] for m in range(3)])
                for m in range(2):
                    new[node(dim, m, i, k)] = got[m]
            closed = new
        r1 = small_sum(LOW, "S1", closed)
        here = (0, 0, 0)
        origin = SLOTS[BLOCKS[0]][0]
        put(sbuf, origin, r1[here])

        def block_copy(offset):
            place, _, index = SLOTS[offset]
            src, dst = sbuf.at[pl.ds(origin * 8, 8)], rbuf.at[pl.ds(place * 8, 8)]
            return remote(src, dst, index, device_at(*offset))

        def block_copies(way, act):
            for step in (1, 0, -1):
                group = [o for o in BLOCKS if o[0] == step]

                def run():
                    for offset in group:
                        act(block_copy(offset))

                if step:
                    pl.when(gy < ny - 1 if step * way > 0 else gy > 0)(run)
                else:
                    run()

        block_copies(1, lambda copy: copy.start())
        drain()
        block_copies(-1, lambda copy: copy.wait_recv())
        r = {here: r1[here]}
        for offset in BLOCKS:
            r[tuple(-o for o in offset)] = tile(rbuf, SLOTS[offset][0])

        def up_full(dim, v, before):
            if dim == "a":
                return spin(jnp.where(last["a"], before, v), 2, 0)
            if dim == "b":
                w = jnp.where(odd_lane, jnp.where(odd_row, spin(v, 1, 0), spin(before, -1, 0)), v)
                return jnp.where(odd_lane, spin(w, 0, 1), spin(w, 0, -1))
            t = jnp.where(lanes < 8, spin(v, 0, 10), spin(v, 0, 8))
            return jnp.where(lanes < 2, spin(before, 0, 2), t)

        def down_full(dim, v, after):
            if dim == "a":
                return spin(jnp.where(first["a"], after, v), -2, 0)
            if dim == "b":
                w = jnp.where(odd_lane, v, jnp.where(odd_row, spin(after, 1, 0), spin(v, -1, 0)))
                return jnp.where(odd_lane, spin(w, 0, 1), spin(w, 0, -1))
            t = jnp.where(lanes >= 120, spin(v, 0, -10), spin(v, 0, -8))
            return jnp.where(lanes >= 126, spin(after, 0, -2), t)

        def beside(dim, o, step):
            return tuple(i + step if d == dim else i for d, i in zip(ALL_DIMS, o))

        def both_sides(dim, f, o):
            before, after = f.get(beside(dim, o, -1), f[o]), f.get(beside(dim, o, 1), f[o])
            return up_full(dim, f[o], before) + down_full(dim, f[o], after)

        walls_a, walls_b = {}, {}
        for step in (-1, 0, 1):
            at_a, at_b = lax.rem(gy + step + ny, ny) == 0, lax.rem(gz + step + nz, nz) == 0
            walls_a[step] = jnp.where(first["a"] & at_a, 0.0, 1.0).astype(jnp.float32)
            walls_b[step] = jnp.where(first["b"] & at_b, 0.0, 1.0).astype(jnp.float32)

        own_low = 3.0 * float(LOW.gain[0, 0] + LOW.gain[1, 1])
        side_low = float(LOW.gain[0, 1])
        inverse_low = float(LOW.inverse(0, 0, 0))
        dl = {o: (inverse_low / LOW.center) * v for o, v in r.items()}
        x1 = dict(dl)
        for keep, gain in LOW.factors(COARSE_STEPS):
            new = {}
            for o in r:
                sides = total(both_sides(dim, dl, o) for dim in ALL_DIMS)
                left = r[o] - (own_low * dl[o] + side_low * sides)
                new[o] = left * (walls_a[o[0]] * walls_b[o[1]])
            r = new
            dl = {o: float(keep) * dl[o] + float(gain * inverse_low) * r[o] for o in r}
            x1 = add(x1, dl)

        def corners(f, dims):
            for dim in dims:
                new = {}
                for o, v in f.items():
                    new[o] = v if o[ALL_DIMS.index(dim)] == 0 else None
                for o in f:
                    if new[o] is None:
                        low = beside(dim, o, -1)
                        new[o] = down_full(dim, f[low], f[o])
                f = new
            return f

        def lift_low(f, dims):
            for dim in dims:
                new = {}
                rest = sorted({tuple(i for d, i in zip(ALL_DIMS, t) if d != dim) for t in f})
                for i, k in rest:
                    got = raise_line(MID, LOW, [f[node(dim, m, i, k)] for m in range(2)])
                    for m in range(3):
                        new[node(dim, m, i, k)] = got[m]
                f = new
            return f

        ends = list(itertools.product((0, 1), repeat=3))
        c3 = lift_low(corners({o: x1[o] for o in ends}, ALL_DIMS), "cba")
        y = {t: None for t in c3}
        for dim in ALL_DIMS:
            at = ALL_DIMS.index(dim)
            rest = ALL_DIMS.replace(dim, "")
            f = {}
            for o in ends:
                if o[at] == 0:
                    f[o] = (x1[o] - 0.5 * both_sides(dim, x1, o)) * float(1.0 / MID.mass[0])
            for t, v in lift_low(corners(f, rest), rest).items():
                y[t] = v if y[t] is None else y[t] + v
        r3 = {t: masked(t, v if y[t] is None else v - y[t]) for t, v in r3.items()}
        d3 = first_step(MID, r3)
        r3 = subtract(r3, small_apply(MID, "m4", d3))
        e3 = next_step(MID, mid_factor, d3, r3)
        t3 = small_close(MID, "C3", add(x3, c3, d3, e3))

        for a in range(4):
            for b in range(4):
                got = raise_line(FINE, MID, [t3[(a, b, m)] for m in range(4)])
                for m in range(7):
                    put(w2, (a * 4 + b) * 7 + m, got[m])

        def raise_b(a):
            at, to = sub(w2, a * 28, 28), sub(w1, a * 49, 49)
            for c in range(7):
                got = raise_line(FINE, MID, [tile(at, m * 7 + c) for m in range(4)])
                for m in range(7):
                    put(to, m * 7 + c, got[m])

        loop(4, raise_b)

        def raise_a(b):
            at = sub(w1, b * 7, 154)
            to, place = line_view(d, "a", b)
            for c in range(7):
                got = raise_line(FINE, MID, [tile(at, m * 49 + c) for m in range(4)])
                for m in range(7):
                    put(to, place(m, c), got[m])

        loop(7, raise_a)
        drain()
        block_copies(1, lambda copy: copy.wait_send())

    def one_turn(it):
        pl.when(it == 2)(coarse)
        fine_apply(it)

    loop(4, one_turn)

    for dims in ("b", "c", "bc"):
        start_close(dims)

    def leave_nodes(a):
        at, to = sub(xs, a * 64, 64), sub(tr, a * 64, 64)
        for b in range(8):
            for c in range(8):
                to[by_nodes(b, c), :] = tile(at, b * 8 + c)

    def leave(an):
        at = sub(tr, an * 64, 64)
        for ael in range(4):
            for b_hi in range(2):
                vs = butterfly([tile(at, cn * 8 + ael * 2 + b_hi) for cn in range(8)])
                for g, v in enumerate(vs):
                    b_at, c_at = pl.ds((2 * b_hi + g % 2) * 8, 8), pl.ds((g // 2) * 128, 128)
                    out[ael * 8 + an, b_at, c_at] = v

    def end_face(dim):
        for i in range(7):
            got = fine_row("C7", dim, -1, i, 0)
            for k in range(7):
                value = down(dim, tile(xs, at8(node(dim, 0, i, k)))) + got[k]
                put(xs, at8(node(dim, 7, i, k)), value)

    for dims in ("b", "c", "bc"):
        receive(("C7", dims, -1))
    spread_c("C7", -1, 0)
    end_face("b")
    end_face("c")
    hb = fine_row("C7", "b", -1, 0, 0)
    hc_a = fine_row("C7", "c", -1, 0, 0)
    hc_b = [fine_row("C7", "c", -1, i, 0)[0] for i in range(7)]
    edge_bc = load_edge("C7", "bc", -1, 7)
    for k in range(7):
        value = down("c", tile(xs, at8((k, 7, 0)))) + down("b", hc_b[k]) + edge_bc[k]
        put(xs, at8((k, 7, 7)), value)
    loop(7, leave_nodes)
    loop(7, leave)

    for dims in ("a", "ab", "ac", "abc"):
        receive(("C7", dims, -1))
    end_face("a")
    edge_ab, edge_ac = load_edge("C7", "ab", -1, 7), load_edge("C7", "ac", -1, 7)
    for k in range(7):
        value = down("b", tile(xs, at8((7, 0, k)))) + down("a", hb[k]) + edge_ab[k]
        put(xs, at8((7, 7, k)), value)
        value = down("c", tile(xs, at8((7, k, 0)))) + down("a", hc_a[k]) + edge_ac[k]
        put(xs, at8((7, k, 7)), value)
    value = down("c", tile(xs, at8((7, 7, 0)))) + down("b", down("a", hc_a[0]))
    value = value + down("b", edge_ac[0]) + down("a", edge_bc[0])
    put(xs, at8((7, 7, 7)), value + load_edge("C7", "abc", -1, 1)[0])
    leave_nodes(7)
    leave(7)
    drain()

def solution(mesh):
    sizes = tuple(mesh.shape[axis] for axis in ("gx", "gy", "gz"))

    def body(*refs):
        kernel(sizes, *refs)

    def local(residual):
        vmem = lambda count: pltpu.VMEM((count * 8, 128), jnp.float32)
        return pl.pallas_call(
            body,
            out_shape=jax.ShapeDtypeStruct(residual.shape, jnp.float32),
            in_specs=[
                pl.BlockSpec(memory_space=pl.ANY),
            ],
            out_specs=pl.BlockSpec(memory_space=pltpu.VMEM),
            scratch_shapes=[
                pltpu.VMEM((4, 8, 32, 512), jnp.float32),
                vmem(512),
                vmem(512),
                vmem(343),
                vmem(343),
                vmem(343),
                vmem(343),
                vmem(343),
                vmem(512),
                vmem(196),
                vmem(112),
                vmem(49),
                vmem(16),
                vmem(BUF_VREGS),
                vmem(BUF_VREGS),
                pltpu.SemaphoreType.DMA((MESSAGES,)),
                pltpu.SemaphoreType.DMA((MESSAGES,)),
                pltpu.SemaphoreType.DMA((8,)),
            ],
            compiler_params=pltpu.CompilerParams(
                collective_id=0, has_side_effects=True, vmem_limit_bytes=40 * 1024 * 1024
            ),
        )(residual.reshape(4, 8, 32, 512))

    return jax.shard_map(
        local,
        mesh=mesh,
        in_specs=(P("gy", "gz", "gx"),),
        out_specs=P("gy", "gz", "gx"),
        check_vma=False,
    )
```

```python
import itertools

import jax
import jax.numpy as jnp
import numpy as np
from jax import lax
from jax.experimental import pallas as pl
from jax.experimental.pallas import tpu as pltpu
from jax.sharding import PartitionSpec as P

ORDER = 7
MID_ORDER = 3
COARSE_STEPS = 4


def legendre_pair(degree, points):
    previous = np.ones(points.shape)
    current = points.copy()
    for level in range(1, degree):
        following = ((2 * level + 1) * points * current - level * previous) / (level + 1)
        previous = current
        current = following
    return (current, previous)


def gll_table(degree):
    points = np.cos(np.pi * np.arange(degree + 1) / degree)
    for sweep in range(100):
        current, previous = legendre_pair(degree, points)
        points = points - (points * current - previous) / ((degree + 1) * current)
    points = points[::-1].copy()
    current, previous = legendre_pair(degree, points)
    weights = 2.0 / (degree * (degree + 1) * current**2)
    return (points, weights)


def lagrange_matrix(targets, points):
    point_count = len(points)
    matrix = np.ones((len(targets), point_count))
    for column in range(point_count):
        for partner in range(point_count):
            if partner != column:
                matrix[:, column] *= (targets - points[partner]) / (
                    points[column] - points[partner]
                )
    return matrix


def line_stiffness(degree):
    points, weights = gll_table(degree)
    point_count = len(points)
    barycentric = np.array(
        [
            1.0
            / np.prod(
                [
                    points[column] - points[partner]
                    for partner in range(point_count)
                    if partner != column
                ]
            )
            for column in range(point_count)
        ]
    )
    derivative = np.zeros((point_count, point_count))
    for target in range(point_count):
        for column in range(point_count):
            if target != column:
                derivative[target, column] = (
                    barycentric[column] / barycentric[target] / (points[target] - points[column])
                )
        derivative[target, target] = -np.sum(derivative[target])
    return (derivative.T @ (weights[:, None] * derivative), weights)


def assembled_patterns(degree):
    stiffness, weights = line_stiffness(degree)
    indices = np.arange(len(weights))
    diag_pat = stiffness[indices, indices].copy()
    weight_pat = weights.copy()
    row_pat = np.abs(stiffness).sum(axis=1)
    for pattern in (diag_pat, weight_pat, row_pat):
        shared = pattern[0] + pattern[-1]
        pattern[0] = shared
        pattern[-1] = shared
    return (diag_pat, weight_pat, row_pat)


def three_terms(special, weight_pat):
    return (
        special[:, None, None] * weight_pat[None, :, None] * weight_pat[None, None, :]
        + weight_pat[:, None, None] * special[None, :, None] * weight_pat[None, None, :]
        + weight_pat[:, None, None] * weight_pat[None, :, None] * special[None, None, :]
    )


def chebyshev_bound(degree):
    diag_pat, weight_pat, row_pat = assembled_patterns(degree)
    return float(np.max(three_terms(row_pat, weight_pat) / three_terms(diag_pat, weight_pat)))


class Level:
    def __init__(self, q):
        stiffness, weights = line_stiffness(q)
        diag_pat, weight_pat, row_pat = assembled_patterns(q)
        self.q = self.n = q
        self.half = half = (q + 1) // 2
        self.mass = weight_pat
        self.gain = gain = stiffness / weight_pat[:, None]
        self.even = 0.5 * (gain[:half, :half] + gain[:half, ::-1][:, :half])
        self.odd = 0.5 * (gain[:half, :half] - gain[:half, ::-1][:, :half])
        self.alpha = diag_pat / weight_pat
        upper = chebyshev_bound(q)
        lower = upper / 10.0
        self.center = 0.5 * (upper + lower)
        self.halfwidth = 0.5 * (upper - lower)

    def inverse(self, a, b, c):
        return 1.0 / (self.alpha[a] + self.alpha[b] + self.alpha[c])

    def factors(self, steps):
        scaled = self.center / self.halfwidth
        ratio = 1.0 / scaled
        found = []
        for step in range(1, steps):
            following = 1.0 / (2.0 * scaled - ratio)
            found.append((following * ratio, 2.0 * following / self.halfwidth))
            ratio = following
        return found


FINE, MID, LOW = Level(ORDER), Level(MID_ORDER), Level(1)
ALL_DIMS = "abc"
SUBSETS = ("a", "b", "c", "ab", "ac", "bc", "abc")
BLOCKS = [o for o in itertools.product((-1, 0, 1), repeat=3) if any(o)]


def node(dim, m, i, k):
    return {"a": (m, i, k), "b": (i, m, k), "c": (i, k, m)}[dim]


def face_vregs(n, dim):
    return 1 if dim == "c" else n * -(-n // 4)


def plan():
    slots, size, count = {}, 0, 0

    def add(key, length):
        nonlocal size, count
        slots[key] = (size, length, count)
        size += length
        count += 1

    for name, n in (
        ("f1", 7), ("f2", 7), ("f3", 7), ("f4", 7),
        ("m1", 3), ("m2", 3), ("m4", 3),
    ):
        for dim in ALL_DIMS:
            for way in (1, -1):
                add((name, dim, way), face_vregs(n, dim))
    for name, n, way in (("S7", 7, 1), ("S3", 3, 1), ("S1", 1, 1), ("C3", 3, -1), ("C7", 7, -1)):
        for dims in SUBSETS:
            add((name, dims, way), face_vregs(n, dims) if len(dims) == 1 else 1)
    for offset in BLOCKS:
        add(offset, 1)
    return slots, -(-size // 8) * 8, count


SLOTS, BUF_VREGS, MESSAGES = plan()


def total(terms):
    out = None
    for term in terms:
        if term is not None:
            out = term if out is None else out + term
    return out


def mix(coefs, values):
    return total(
        None if abs(coef) < 1e-13 else float(coef) * value for coef, value in zip(coefs, values)
    )


def kernel(sizes, x_hbm, out_hbm, x, out, tr, u, rho, d, ya, yb, yc, xs, w1, w2, ha, pk, sbuf, rbuf, ssem, rsem, xsem, osem):
    nx, ny, nz = sizes
    gx, gy, gz = lax.axis_index("gx"), lax.axis_index("gy"), lax.axis_index("gz")
    rows = lax.broadcasted_iota(jnp.int32, (8, 128), 0)
    lanes = lax.broadcasted_iota(jnp.int32, (8, 128), 1)
    odd_row, odd_lane = rows % 2 == 1, lanes % 2 == 1
    first = {"a": rows < 2, "b": (rows % 2 == 0) & (lanes % 2 == 0), "c": lanes < 2}
    last = {"a": rows >= 6, "b": odd_row & odd_lane, "c": lanes >= 126}
    wall_a = jnp.where(first["a"] & (gy == 0), 0.0, 1.0).astype(jnp.float32)
    wall_b = jnp.where(first["b"] & (gz == 0), 0.0, 1.0).astype(jnp.float32)

    def spin(v, row, lane):
        if row % 8:
            v = pltpu.roll(v, row % 8, 0)
        if lane % 128:
            v = pltpu.roll(v, lane % 128, 1)
        return v

    def up(dim, v):
        if dim == "a":
            return jnp.where(rows >= 2, spin(v, 2, 0), 0.0)
        if dim == "b":
            w = jnp.where(odd_lane, jnp.where(odd_row, spin(v, 1, 0), 0.0), v)
            return jnp.where(odd_lane, spin(w, 0, 1), spin(w, 0, -1))
        t = jnp.where(lanes < 8, spin(v, 0, 10), spin(v, 0, 8))
        return jnp.where(lanes < 2, 0.0, t)

    def down(dim, v):
        if dim == "a":
            return jnp.where(rows < 6, spin(v, -2, 0), 0.0)
        if dim == "b":
            w = jnp.where(odd_lane, v, jnp.where(odd_row, 0.0, spin(v, -1, 0)))
            return jnp.where(odd_lane, spin(w, 0, 1), spin(w, 0, -1))
        t = jnp.where(lanes >= 120, spin(v, 0, -10), spin(v, 0, -8))
        return jnp.where(lanes >= 126, 0.0, t)

    def pack(dim, way, vs):
        acc = None
        for j, v in enumerate(vs):
            if dim == "a":
                v, mask = spin(v, 2 * j + (2 if way > 0 else 0), 0), rows // 2 == j
            elif dim == "b":
                js, jl = j % 2, j // 2
                back = 1 if way > 0 else 0
                v, mask = spin(v, js - back, jl - back), (rows % 2 == js) & (lanes % 2 == jl)
            else:
                v, mask = spin(v, 0, 2 * j + (2 if way > 0 else 0)), lanes // 2 == j
            acc = v if acc is None else jnp.where(mask, v, acc)
        return acc

    def unpack(dim, way, w, j):
        if dim == "a":
            w = spin(w, -2 * j if way > 0 else 6 - 2 * j, 0)
        elif dim == "b":
            js, jl = j % 2, j // 2
            w = spin(w, -js, -jl) if way > 0 else spin(w, 1 - js, 1 - jl)
        else:
            w = spin(w, 0, -2 * j if way > 0 else 126 - 2 * j)
        return jnp.where((first if way > 0 else last)[dim], w, 0.0)

    def move(dims, way, v):
        row = (2 if "a" in dims else 0) - (1 if "b" in dims else 0)
        lane = (2 if "c" in dims else 0) - (1 if "b" in dims else 0)
        mask = None
        for dim in dims:
            part = (first if way > 0 else last)[dim]
            mask = part if mask is None else mask & part
        return jnp.where(mask, spin(v, way * row, way * lane), 0.0)

    def guarded(key, way, run):
        if "a" in key[1]:
            pl.when(gy < ny - 1 if way > 0 else gy > 0)(run)
        else:
            run()

    def edge_spin(dims, way, v, j):
        return spin(v, way * j, 0) if dims == "ab" else spin(v, 0, way * 2 * j)

    def send_edge(name, dims, way, vs):
        acc = total(edge_spin(dims, way, move(dims, way, v), j) for j, v in enumerate(vs))
        put(sbuf, SLOTS[(name, dims, way)][0], acc)
        send((name, dims, way))

    def load_edge(name, dims, way, count):
        w = tile(rbuf, SLOTS[(name, dims, way)][0])
        mask = None
        for dim in dims:
            part = (first if way > 0 else last)[dim]
            mask = part if mask is None else mask & part
        return [jnp.where(mask, edge_spin(dims, -way, w, j), 0.0) for j in range(count)]

    def device_at(da, db, dc):
        return {
            "gx": lax.rem(gx + dc + nx, nx) if dc else gx,
            "gy": lax.rem(gy + da + ny, ny) if da else gy,
            "gz": lax.rem(gz + db + nz, nz) if db else gz,
        }

    def remote(src, dst, index, device):
        return pltpu.make_async_remote_copy(
            src_ref=src,
            dst_ref=dst,
            send_sem=ssem.at[index],
            recv_sem=rsem.at[index],
            device_id=device,
            device_id_type=pl.DeviceIdType.MESH,
        )

    def copy_of(key):
        name, dims, way = key
        offset, length, index = SLOTS[key]
        part = pl.ds(offset * 8, length * 8)
        device = device_at(*(way if dim in dims else 0 for dim in ALL_DIMS))
        return remote(sbuf.at[part], rbuf.at[part], index, device)

    pending = []

    def send(key):
        guarded(key, key[2], lambda: copy_of(key).start())
        pending.append(key)

    def receive(key):
        guarded(key, -key[2], lambda: copy_of(key).wait_recv())

    def drain(keep=None):
        for key in list(pending):
            if key[0] != keep:
                guarded(key, key[2], lambda: copy_of(key).wait_send())
                pending.remove(key)

    def tile(ref, index):
        start = index * 8
        if not isinstance(index, int):
            start = pl.multiple_of(start, 8)
        return ref[pl.ds(start, 8), :]

    def put(ref, index, value):
        start = index * 8
        if not isinstance(index, int):
            start = pl.multiple_of(start, 8)
        ref[pl.ds(start, 8), :] = value

    def sub(ref, base, length):
        start = base * 8
        if not isinstance(base, int):
            start = pl.multiple_of(start, 8)
        return ref.at[pl.ds(start, length * 8)]

    def line_view(ref, dim, i):
        if dim == "a":
            return sub(ref, i * 7, 301), lambda m, k: m * 49 + k
        return sub(ref, i * 49, 49), (lambda m, k: m * 7 + k) if dim == "b" else (
            lambda m, k: k * 7 + m
        )

    def by_class(i, values):
        picked = jnp.where((i == 2) | (i == 5), values[2], values[3])
        picked = jnp.where((i == 1) | (i == 6), values[1], picked)
        return jnp.where(i == 0, values[0], picked)

    def splat(value):
        return jnp.full((8, 128), value, jnp.float32)

    def inverse_slab(a):
        alpha = splat(by_class(a, [float(v) for v in FINE.alpha[:4]]))
        found = {}
        for b in range(4):
            for c in range(b, 4):
                found[(b, c)] = 1.0 / (alpha + float(FINE.alpha[b] + FINE.alpha[c]))
        return lambda b, c: found[tuple(sorted((min(b, 7 - b), min(c, 7 - c))))]

    def at7(t):
        return (t[0] * 7 + t[1]) * 7 + t[2]

    def at8(t):
        return (t[0] * 8 + t[1]) * 8 + t[2]

    def loop(count, body):
        def step(i, carry):
            body(i)
            return carry

        lax.fori_loop(0, count, step, 0)

    def line(lv, dim, v):
        q, half = lv.q, lv.half
        full = list(v) + [down(dim, v[0])]
        e = [full[j] + full[q - j] for j in range(half)]
        o = [full[j] - full[q - j] for j in range(half)]
        y = [None] * (q + 1)
        e = [v - e[0] for v in e[1:]]
        for i in range(half):
            ev, od = mix(lv.even[i][1:], e), mix(lv.odd[i], o)
            y[i] = od if ev is None else ev + od
            y[q - i] = -od if ev is None else ev - od
        own = jnp.where(first[dim], float(lv.gain[q, q]), 0.0)
        y[0] = y[0] + up(dim, y[q]) + own * v[0]
        return y[:q]

    def partial_end(lv, v):
        return mix(lv.gain[lv.q, : lv.q], v)

    def lower_line(hi, lo, v):
        jmat = lagrange_matrix(gll_table(hi.q)[0], gll_table(lo.q)[0])
        r = jmat.T * hi.mass[None, :] / lo.mass[:, None]
        inner = range(1, hi.half)
        e = [v[n] + v[hi.q - n] for n in inner]
        o = [v[n] - v[hi.q - n] for n in inner]
        y = [None] * (lo.q + 1)
        for m in range(lo.half):
            ev = mix([0.5 * (r[m, n] + r[m, hi.q - n]) for n in inner], e)
            od = mix([0.5 * (r[m, n] - r[m, hi.q - n]) for n in inner], o)
            y[m], y[lo.q - m] = ev + od, ev - od
        y[0] = y[0] + float(r[0, 0]) * v[0]
        return y

    def raise_line(hi, lo, v):
        jmat = lagrange_matrix(gll_table(hi.q)[0], gll_table(lo.q)[0])
        e = [v[m] + v[lo.q - m] for m in range(lo.half)]
        o = [v[m] - v[lo.q - m] for m in range(lo.half)]
        y = [None] * (hi.q + 1)
        y[0] = v[0]
        for n in range(1, hi.half):
            ev = mix([0.5 * (jmat[n, m] + jmat[n, lo.q - m]) for m in range(lo.half)], e)
            od = mix([0.5 * (jmat[n, m] - jmat[n, lo.q - m]) for m in range(lo.half)], o)
            y[n], y[hi.q - n] = ev + od, ev - od
        return y[: hi.q]


    def store_face(name, dim, way, n, get):
        offset = SLOTS[(name, dim, way)][0]
        if dim == "c":
            acc = None
            for i in range(n):
                w = pack(dim, way, [get(i, k) for k in range(n)])
                acc = w if acc is None else jnp.where(lanes // 8 == i, spin(w, 0, 8 * i), acc)
            put(sbuf, offset, acc)
        else:
            for i in range(n):
                put(sbuf, offset + i, pack(dim, way, [get(i, k) for k in range(n)]))
        send((name, dim, way))

    def load_face(name, dim, way, n):
        offset = SLOTS[(name, dim, way)][0]
        receive((name, dim, way))
        if dim == "c":
            w = tile(rbuf, offset)
            return [[unpack(dim, way, spin(w, 0, -8 * i), k) for k in range(n)] for i in range(n)]
        return [
            [unpack(dim, way, tile(rbuf, offset + i), k) for k in range(n)] for i in range(n)
        ]

    def small_apply(lv, name, dv):
        n = lv.n
        for dim in ALL_DIMS:
            store_face(name, dim, -1, n, lambda i, k: dv[node(dim, 0, i, k)])
            store_face(
                name, dim, 1, n,
                lambda i, k: partial_end(lv, [dv[node(dim, m, i, k)] for m in range(n)]),
            )
        y = {}
        for dim in ALL_DIMS:
            for i in range(n):
                for k in range(n):
                    got = line(lv, dim, [dv[node(dim, m, i, k)] for m in range(n)])
                    for m in range(n):
                        t = node(dim, m, i, k)
                        y[t] = got[m] if t not in y else y[t] + got[m]
        drain(name)
        for dim in "cba":
            before = load_face(name, dim, -1, n)
            after = load_face(name, dim, 1, n)
            for i in range(n):
                for k in range(n):
                    for m in range(n):
                        t = node(dim, m, i, k)
                        y[t] = y[t] + float(lv.gain[m, lv.q]) * before[i][k]
                    t = node(dim, 0, i, k)
                    y[t] = y[t] + after[i][k]
        return y

    def masked(t, v):
        if t[0] == 0:
            v = v * wall_a
        if t[1] == 0:
            v = v * wall_b
        return v

    def small_sum(lv, name, closed):
        n, q = lv.n, lv.q
        for dim in ALL_DIMS:
            for i in range(q + 1):
                for k in range(q + 1):
                    low, high = node(dim, 0, i, k), node(dim, q, i, k)
                    closed[low] = closed[low] + up(dim, closed[high])
        for dim in ALL_DIMS:
            store_face(name, dim, 1, n, lambda i, k: closed[node(dim, q, i, k)])
        for dims in SUBSETS[3:]:
            send_edge(name, dims, 1, [closed[t] for t in plane(dims, n, q)])
        drain(name)
        r = {t: closed[t] for t in itertools.product(range(n), repeat=3)}
        for dim in "cba":
            got = load_face(name, dim, 1, n)
            for i in range(n):
                for k in range(n):
                    t = node(dim, 0, i, k)
                    r[t] = r[t] + got[i][k]
        for dims in ("bc", "ab", "ac", "abc"):
            receive((name, dims, 1))
            places = plane(dims, n, 0)
            for t, v in zip(places, load_edge(name, dims, 1, len(places))):
                r[t] = r[t] + v
        return {t: masked(t, v) for t, v in r.items()}

    def plane(dims, n, end):
        ranges = [[end] if dim in dims else range(n) for dim in ALL_DIMS]
        return list(itertools.product(*ranges))

    def small_close(lv, name, v):
        n, q = lv.n, lv.q
        for dim in ALL_DIMS:
            store_face(name, dim, -1, n, lambda i, k: v[node(dim, 0, i, k)])
        for dims in SUBSETS[3:]:
            send_edge(name, dims, -1, [v[t] for t in plane(dims, n, 0)])
        drain(name)
        halo = {}
        for dim in "cba":
            got = load_face(name, dim, -1, n)
            for i in range(n):
                for k in range(n):
                    halo[(dim, node(dim, q, i, k))] = got[i][k]
        for dims in SUBSETS[3:]:
            receive((name, dims, -1))
            places = plane(dims, n, q)
            for t, got in zip(places, load_edge(name, dims, -1, len(places))):
                halo[(dims, t)] = got
        return closure(lv, dict(v), halo)

    def closure(lv, field, halo):
        n, q = lv.n, lv.q

        def value(have, t):
            ends = "".join(dim for dim, i in zip(ALL_DIMS, t) if i == q and dim not in have)
            if not ends:
                return halo[(have, t)] if have else field[t]
            dim = ends[0]
            low = tuple(0 if d == dim else i for d, i in zip(ALL_DIMS, t))
            with_dim = "".join(d for d in ALL_DIMS if d in have or d == dim)
            return down(dim, value(have, low)) + value(with_dim, t)

        return {t: value("", t) for t in itertools.product(range(q + 1), repeat=3)}

    def first_step(lv, r):
        return {t: float(lv.inverse(*t) / lv.center) * v for t, v in r.items()}

    def next_step(lv, factor, dv, r):
        keep, gain = factor
        return {t: float(keep) * dv[t] + float(gain * lv.inverse(*t)) * r[t] for t in r}

    def subtract(r, y):
        return {t: masked(t, r[t] - y[t]) for t in r}

    def add(*fields):
        return {t: total(f[t] for f in fields) for t in fields[0]}

    for an in (7, 0, 1, 2, 3, 4, 5, 6):
        pltpu.make_async_copy(x_hbm.at[:, an], x.at[:, an], xsem.at[an]).start()

    def zero_block(i):
        rbuf[pl.ds(pl.multiple_of(i * 64, 64), 64), :] = jnp.zeros((64, 128), jnp.float32)

    loop(BUF_VREGS // 8, zero_block)

    for offset in BLOCKS:
        pl.semaphore_signal(
            pltpu.get_barrier_semaphore(),
            inc=1,
            device_id=device_at(*offset),
            device_id_type=pl.DeviceIdType.MESH,
        )

    def butterfly(vs):
        for bit in (1, 2, 4):
            new = list(vs)
            low = (lanes // bit) % 2 == 0
            for i in range(8):
                if not i & bit:
                    lo, hi = vs[i], vs[i + bit]
                    new[i] = jnp.where(low, lo, spin(hi, 0, bit))
                    new[i + bit] = jnp.where(low, spin(lo, 0, -bit), hi)
            vs = new
        return vs

    def enter(an):
        to = sub(tr, an * 64, 64)
        for ael in range(4):
            for b_hi in range(2):
                vs = [
                    x[ael, an, pl.ds((2 * b_hi + g % 2) * 8, 8), pl.ds((g // 2) * 128, 128)]
                    for g in range(8)
                ]
                for cn, v in enumerate(butterfly(vs)):
                    put(to, cn * 8 + ael * 2 + b_hi, v)

    def by_nodes(bn, cn):
        return pl.ds(cn * 64 + bn, 8, stride=8)

    def slab(a):
        at = sub(tr, a * 64, 64)
        to = sub(u, a * 64, 64)
        v = {(b, c): at[by_nodes(b, c), :] for b in range(8) for c in range(8)}
        for c in range(8):
            v[(0, c)] = v[(0, c)] + up("b", v[(7, c)])
        for b in range(8):
            v[(b, 0)] = v[(b, 0)] + up("c", v[(b, 7)])
        for (b, c), value in v.items():
            put(to, b * 8 + c, value)

    fetch = [
        pltpu.make_async_copy(x_hbm.at[:, an], x.at[:, an], xsem.at[an]) for an in range(8)
    ]

    def face_row(name, dim, way, i, vs):
        offset = SLOTS[(name, dim, way)][0]
        if dim == "c":
            put(pk, i if way > 0 else i + 7, pack(dim, way, vs))
        else:
            to = sub(sbuf, offset + 2 * i, 2)
            put(to, 0, pack(dim, way, vs[:4]))
            put(to, 1, pack(dim, way, vs[4:]))

    def send_face(name, dim, way):
        if dim == "c":
            base = 0 if way > 0 else 7
            acc = tile(pk, base)
            for i in range(1, 7):
                acc = jnp.where(lanes // 16 == i, spin(tile(pk, base + i), 0, 16 * i), acc)
            put(sbuf, SLOTS[(name, dim, way)][0], acc)
        send((name, dim, way))

    def spread_c(name, way, base):
        w = tile(rbuf, SLOTS[(name, "c", way)][0])
        for i in range(7):
            put(pk, base + i, spin(w, 0, -16 * i))

    def fine_row(name, dim, way, i, base):
        if dim == "c":
            w = tile(pk, base + i)
            return [unpack(dim, way, w, k) for k in range(7)]
        offset = SLOTS[(name, dim, way)][0]
        at = sub(rbuf, offset + 2 * i, 2)
        lo, hi = tile(at, 0), tile(at, 1)
        return [unpack(dim, way, lo if k < 4 else hi, k % 4) for k in range(7)]

    def start_sum(dims):
        if len(dims) > 1:
            send_edge("S7", dims, 1, [tile(u, at8(t)) for t in plane(dims, 7, 7)])
            return
        for i in range(7):
            face_row("S7", dims, 1, i, [tile(u, at8(node(dims, 7, i, k))) for k in range(7)])
        send_face("S7", dims, 1)

    fetch[7].wait()
    enter(7)
    slab(7)
    pl.semaphore_wait(pltpu.get_barrier_semaphore(), len(BLOCKS))
    for dims in ("a", "ab", "ac", "abc"):
        start_sum(dims)
    for an in range(7):
        fetch[an].wait()
    loop(7, enter)
    loop(7, slab)
    for b in range(8):
        for c in range(8):
            t = at8((0, b, c))
            put(u, t, tile(u, t) + up("a", tile(u, at8((7, b, c)))))
    for dims in ("c", "b", "bc"):
        start_sum(dims)

    for dims in ("c", "b", "a", "bc", "ac", "ab", "abc"):
        key = ("S7", dims, 1)
        receive(key)
        if dims == "c":
            spread_c("S7", 1, 0)
        elif dims == "a":
            for i in range(7):
                got = fine_row("S7", "a", 1, i, 0)
                for k in range(7):
                    t = at8((0, i, k))
                    put(u, t, tile(u, t) + got[k])
        elif len(dims) > 1:
            places = plane(dims, 7, 0)
            for t, v in zip(places, load_edge("S7", dims, 1, len(places))):
                put(u, at8(t), tile(u, at8(t)) + v)

    def first_fine(a):
        wall = jnp.where(a == 0, wall_a, 1.0)
        from_u, to_rho, to_d = sub(u, a * 64, 64), sub(rho, a * 49, 49), sub(d, a * 49, 49)
        mass_a = by_class(a, [float(1.0 / v) for v in FINE.mass[:4]])
        inverse = inverse_slab(a)
        b_after = fine_row("S7", "b", 1, a, 0)
        c_after = fine_row("S7", "c", 1, a, 0)
        for b in range(7):
            for c in range(7):
                r = tile(from_u, b * 8 + c)
                if b == 0:
                    r = r + b_after[c]
                if c == 0:
                    r = r + c_after[b]
                r = r * (float(1.0 / (FINE.mass[b] * FINE.mass[c])) * mass_a) * wall
                if b == 0:
                    r = r * wall_b
                put(to_rho, b * 7 + c, r)
                put(to_d, b * 7 + c, (inverse(b, c) * float(1.0 / FINE.center)) * r)

    loop(7, first_fine)

    def fine_apply(name, after):
        for dims in ("a", "bc"):

            def faces(i):
                for dim in dims:
                    at, place = line_view(d, dim, i)
                    vs = [[tile(at, place(m, k)) for m in range(7)] for k in range(7)]
                    face_row(name, dim, -1, i, [v[0] for v in vs])
                    face_row(name, dim, 1, i, [partial_end(FINE, v) for v in vs])

            loop(7, faces)
            for dim in dims:
                send_face(name, dim, -1)
                send_face(name, dim, 1)

        def lines(i):
            for dim, y in zip(ALL_DIMS, (ya, yb, yc)):
                at, place = line_view(d, dim, i)
                to, _ = line_view(y, dim, i)
                for k in range(7):
                    got = line(FINE, dim, [tile(at, place(m, k)) for m in range(7)])
                    for m in range(7):
                        put(to, place(m, k), got[m])

        loop(7, lines)

        drain(name)
        for dim in "cba":
            for way in (1, -1):
                receive((name, dim, way))
        spread_c(name, 1, 0)
        spread_c(name, -1, 7)
        for i in range(7):
            got = fine_row(name, "a", -1, i, 0)
            add0 = fine_row(name, "a", 1, i, 0)
            for k in range(7):
                put(ha, i * 7 + k, got[k])
                t = at7((0, i, k))
                put(ya, t, tile(ya, t) + add0[k])

        def finish(a):
            wall = jnp.where(a == 0, wall_a, 1.0)
            gain_a = float(FINE.gain[6, 7])
            for m in range(6):
                gain_a = jnp.where(a == m, float(FINE.gain[m, 7]), gain_a)
            gain_a = splat(gain_a)
            inverse = inverse_slab(a)
            b_before = fine_row(name, "b", -1, a, 0)
            b_after = fine_row(name, "b", 1, a, 0)
            c_before = fine_row(name, "c", -1, a, 7)
            c_after = fine_row(name, "c", 1, a, 0)
            at_rho, at_d, at_x = sub(rho, a * 49, 49), sub(d, a * 49, 49), sub(xs, a * 64, 64)
            at_y = [sub(y, a * 49, 49) for y in (ya, yb, yc)]
            for b in range(7):
                for c in range(7):
                    t, t8 = b * 7 + c, b * 8 + c
                    y = total(tile(part, t) for part in at_y) + gain_a * tile(ha, t)
                    y = y + float(FINE.gain[b, 7]) * b_before[c]
                    y = y + float(FINE.gain[c, 7]) * c_before[b]
                    if b == 0:
                        y = y + b_after[c]
                    if c == 0:
                        y = y + c_after[b]
                    r = (tile(at_rho, t) - y) * wall
                    if b == 0:
                        r = r * wall_b
                    put(at_rho, t, r)
                    if after is None:
                        continue
                    old = tile(at_d, t)
                    if after == "lift":
                        put(at_x, t8, tile(at_x, t8) + old)
                        put(at_d, t, (inverse(b, c) * float(1.0 / FINE.center)) * r)
                        continue
                    new = float(fine_keep) * old + (inverse(b, c) * float(fine_gain)) * r
                    if after == "first":
                        put(at_x, t8, old + new)
                        put(at_d, t, new)
                    else:
                        put(at_x, t8, tile(at_x, t8) + old + new)

        finish(0)
        if after == "post":
            for dims in ("a", "ab", "ac", "abc"):
                start_close(dims)
        loop(6, lambda a: finish(a + 1))

    def start_close(dims):
        if len(dims) > 1:
            send_edge("C7", dims, -1, [tile(xs, at8(t)) for t in plane(dims, 7, 0)])
            return
        for i in range(7):
            face_row("C7", dims, -1, i, [tile(xs, at8(node(dims, 0, i, k))) for k in range(7)])
        send_face("C7", dims, -1)

    fine_keep, fine_gain = FINE.factors(2)[0]
    fine_apply("f1", "first")
    fine_apply("f2", None)

    def lower_a(b):
        at, place = line_view(rho, "a", b)
        to = sub(w1, b * 7, 154)
        for c in range(7):
            got = lower_line(FINE, MID, [tile(at, place(m, c)) for m in range(7)])
            for m in range(4):
                put(to, m * 49 + c, got[m])

    loop(7, lower_a)

    def lower_b(a):
        at, to = sub(w1, a * 49, 49), sub(w2, a * 28, 28)
        for c in range(7):
            got = lower_line(FINE, MID, [tile(at, m * 7 + c) for m in range(7)])
            for m in range(4):
                put(to, m * 7 + c, got[m])

    loop(4, lower_b)
    closed = {}
    for a in range(4):
        for b in range(4):
            got = lower_line(FINE, MID, [tile(w2, (a * 4 + b) * 7 + m) for m in range(7)])
            for m in range(4):
                closed[(a, b, m)] = got[m]
    r3 = small_sum(MID, "S3", closed)

    mid_factor = MID.factors(2)[0]
    d3 = first_step(MID, r3)
    r3 = subtract(r3, small_apply(MID, "m1", d3))
    e3 = next_step(MID, mid_factor, d3, r3)
    x3 = add(d3, e3)
    r3 = subtract(r3, small_apply(MID, "m2", e3))

    closed = r3
    for dim in ALL_DIMS:
        new = {}
        others = sorted({tuple(i for dd, i in zip(ALL_DIMS, t) if dd != dim) for t in closed})
        for i, k in others:
            got = lower_line(MID, LOW, [closed[node(dim, m, i, k)] for m in range(3)])
            for m in range(2):
                new[node(dim, m, i, k)] = got[m]
        closed = new
    r1 = small_sum(LOW, "S1", closed)
    here = (0, 0, 0)
    origin = SLOTS[BLOCKS[0]][0]
    put(sbuf, origin, r1[here])

    def block_copy(offset):
        place, _, index = SLOTS[offset]
        src, dst = sbuf.at[pl.ds(origin * 8, 8)], rbuf.at[pl.ds(place * 8, 8)]
        return remote(src, dst, index, device_at(*offset))

    def block_copies(way, act):
        for step in (1, 0, -1):
            group = [o for o in BLOCKS if o[0] == step]

            def run():
                for offset in group:
                    act(block_copy(offset))

            if step:
                pl.when(gy < ny - 1 if step * way > 0 else gy > 0)(run)
            else:
                run()

    block_copies(1, lambda copy: copy.start())
    drain()
    block_copies(-1, lambda copy: copy.wait_recv())
    r = {here: r1[here]}
    for offset in BLOCKS:
        r[tuple(-o for o in offset)] = tile(rbuf, SLOTS[offset][0])

    def up_full(dim, v, before):
        if dim == "a":
            return spin(jnp.where(last["a"], before, v), 2, 0)
        if dim == "b":
            w = jnp.where(odd_lane, jnp.where(odd_row, spin(v, 1, 0), spin(before, -1, 0)), v)
            return jnp.where(odd_lane, spin(w, 0, 1), spin(w, 0, -1))
        t = jnp.where(lanes < 8, spin(v, 0, 10), spin(v, 0, 8))
        return jnp.where(lanes < 2, spin(before, 0, 2), t)

    def down_full(dim, v, after):
        if dim == "a":
            return spin(jnp.where(first["a"], after, v), -2, 0)
        if dim == "b":
            w = jnp.where(odd_lane, v, jnp.where(odd_row, spin(after, 1, 0), spin(v, -1, 0)))
            return jnp.where(odd_lane, spin(w, 0, 1), spin(w, 0, -1))
        t = jnp.where(lanes >= 120, spin(v, 0, -10), spin(v, 0, -8))
        return jnp.where(lanes >= 126, spin(after, 0, -2), t)

    def beside(dim, o, step):
        return tuple(i + step if d == dim else i for d, i in zip(ALL_DIMS, o))

    def both_sides(dim, f, o):
        before, after = f.get(beside(dim, o, -1), f[o]), f.get(beside(dim, o, 1), f[o])
        return up_full(dim, f[o], before) + down_full(dim, f[o], after)

    walls_a, walls_b = {}, {}
    for step in (-1, 0, 1):
        at_a, at_b = lax.rem(gy + step + ny, ny) == 0, lax.rem(gz + step + nz, nz) == 0
        walls_a[step] = jnp.where(first["a"] & at_a, 0.0, 1.0).astype(jnp.float32)
        walls_b[step] = jnp.where(first["b"] & at_b, 0.0, 1.0).astype(jnp.float32)

    own_low = 3.0 * float(LOW.gain[0, 0] + LOW.gain[1, 1])
    side_low = float(LOW.gain[0, 1])
    inverse_low = float(LOW.inverse(0, 0, 0))
    dl = {o: (inverse_low / LOW.center) * v for o, v in r.items()}
    x1 = dict(dl)
    for keep, gain in LOW.factors(COARSE_STEPS):
        new = {}
        for o in r:
            sides = total(both_sides(dim, dl, o) for dim in ALL_DIMS)
            left = r[o] - (own_low * dl[o] + side_low * sides)
            new[o] = left * (walls_a[o[0]] * walls_b[o[1]])
        r = new
        dl = {o: float(keep) * dl[o] + float(gain * inverse_low) * r[o] for o in r}
        x1 = add(x1, dl)

    def corners(f, dims):
        for dim in dims:
            new = {}
            for o, v in f.items():
                new[o] = v if o[ALL_DIMS.index(dim)] == 0 else None
            for o in f:
                if new[o] is None:
                    low = beside(dim, o, -1)
                    new[o] = down_full(dim, f[low], f[o])
            f = new
        return f

    def lift_low(f, dims):
        for dim in dims:
            new = {}
            rest = sorted({tuple(i for d, i in zip(ALL_DIMS, t) if d != dim) for t in f})
            for i, k in rest:
                got = raise_line(MID, LOW, [f[node(dim, m, i, k)] for m in range(2)])
                for m in range(3):
                    new[node(dim, m, i, k)] = got[m]
            f = new
        return f

    ends = list(itertools.product((0, 1), repeat=3))
    c3 = lift_low(corners({o: x1[o] for o in ends}, ALL_DIMS), "cba")
    y = {t: None for t in c3}
    for dim in ALL_DIMS:
        at = ALL_DIMS.index(dim)
        rest = ALL_DIMS.replace(dim, "")
        f = {}
        for o in ends:
            if o[at] == 0:
                f[o] = (x1[o] - 0.5 * both_sides(dim, x1, o)) * float(1.0 / MID.mass[0])
        for t, v in lift_low(corners(f, rest), rest).items():
            y[t] = v if y[t] is None else y[t] + v
    r3 = {t: masked(t, v if y[t] is None else v - y[t]) for t, v in r3.items()}
    d3 = first_step(MID, r3)
    r3 = subtract(r3, small_apply(MID, "m4", d3))
    e3 = next_step(MID, mid_factor, d3, r3)
    t3 = small_close(MID, "C3", add(x3, c3, d3, e3))

    for a in range(4):
        for b in range(4):
            got = raise_line(FINE, MID, [t3[(a, b, m)] for m in range(4)])
            for m in range(7):
                put(w2, (a * 4 + b) * 7 + m, got[m])

    def raise_b(a):
        at, to = sub(w2, a * 28, 28), sub(w1, a * 49, 49)
        for c in range(7):
            got = raise_line(FINE, MID, [tile(at, m * 7 + c) for m in range(4)])
            for m in range(7):
                put(to, m * 7 + c, got[m])

    loop(4, raise_b)

    def raise_a(b):
        at = sub(w1, b * 7, 154)
        to, place = line_view(d, "a", b)
        for c in range(7):
            got = raise_line(FINE, MID, [tile(at, m * 49 + c) for m in range(4)])
            for m in range(7):
                put(to, place(m, c), got[m])

    loop(7, raise_a)
    fine_apply("f3", "lift")
    fine_apply("f4", "post")

    for dims in ("b", "c", "bc"):
        start_close(dims)

    def leave_nodes(a):
        at, to = sub(xs, a * 64, 64), sub(tr, a * 64, 64)
        for b in range(8):
            for c in range(8):
                to[by_nodes(b, c), :] = tile(at, b * 8 + c)

    def leave(an):
        at = sub(tr, an * 64, 64)
        for ael in range(4):
            for b_hi in range(2):
                vs = butterfly([tile(at, cn * 8 + ael * 2 + b_hi) for cn in range(8)])
                for g, v in enumerate(vs):
                    b_at, c_at = pl.ds((2 * b_hi + g % 2) * 8, 8), pl.ds((g // 2) * 128, 128)
                    out[ael, an, b_at, c_at] = v

    def end_face(dim):
        for i in range(7):
            got = fine_row("C7", dim, -1, i, 0)
            for k in range(7):
                value = down(dim, tile(xs, at8(node(dim, 0, i, k)))) + got[k]
                put(xs, at8(node(dim, 7, i, k)), value)

    for dims in ("b", "c", "bc"):
        receive(("C7", dims, -1))
    spread_c("C7", -1, 0)
    end_face("b")
    end_face("c")
    hb = fine_row("C7", "b", -1, 0, 0)
    hc_a = fine_row("C7", "c", -1, 0, 0)
    hc_b = [fine_row("C7", "c", -1, i, 0)[0] for i in range(7)]
    edge_bc = load_edge("C7", "bc", -1, 7)
    for k in range(7):
        value = down("c", tile(xs, at8((k, 7, 0)))) + down("b", hc_b[k]) + edge_bc[k]
        put(xs, at8((k, 7, 7)), value)
    loop(7, leave_nodes)
    loop(7, leave)
    store = [
        pltpu.make_async_copy(out.at[:, an], out_hbm.at[:, an], osem.at[an]) for an in range(8)
    ]
    for an in range(7):
        store[an].start()

    for dims in ("a", "ab", "ac", "abc"):
        receive(("C7", dims, -1))
    end_face("a")
    edge_ab, edge_ac = load_edge("C7", "ab", -1, 7), load_edge("C7", "ac", -1, 7)
    for k in range(7):
        value = down("b", tile(xs, at8((7, 0, k)))) + down("a", hb[k]) + edge_ab[k]
        put(xs, at8((7, 7, k)), value)
        value = down("c", tile(xs, at8((7, k, 0)))) + down("a", hc_a[k]) + edge_ac[k]
        put(xs, at8((7, k, 7)), value)
    value = down("c", tile(xs, at8((7, 7, 0)))) + down("b", down("a", hc_a[0]))
    value = value + down("b", edge_ac[0]) + down("a", edge_bc[0])
    put(xs, at8((7, 7, 7)), value + load_edge("C7", "abc", -1, 1)[0])
    leave_nodes(7)
    leave(7)
    store[7].start()
    for copy in store:
        copy.wait()
    drain()
    block_copies(1, lambda copy: copy.wait_send())


def solution(mesh):
    sizes = tuple(mesh.shape[axis] for axis in ("gx", "gy", "gz"))

    def body(*refs):
        kernel(sizes, *refs)

    def local(residual):
        vmem = lambda count: pltpu.VMEM((count * 8, 128), jnp.float32)
        return pl.pallas_call(
            body,
            out_shape=jax.ShapeDtypeStruct((4, 8, 32, 512), jnp.float32),
            in_specs=[
                pl.BlockSpec(memory_space=pl.ANY),
            ],
            out_specs=pl.BlockSpec(memory_space=pl.ANY),
            scratch_shapes=[
                pltpu.VMEM((4, 8, 32, 512), jnp.float32),
                pltpu.VMEM((4, 8, 32, 512), jnp.float32),
                vmem(512),
                vmem(512),
                vmem(343),
                vmem(343),
                vmem(343),
                vmem(343),
                vmem(343),
                vmem(512),
                vmem(196),
                vmem(112),
                vmem(49),
                vmem(16),
                vmem(BUF_VREGS),
                vmem(BUF_VREGS),
                pltpu.SemaphoreType.DMA((MESSAGES,)),
                pltpu.SemaphoreType.DMA((MESSAGES,)),
                pltpu.SemaphoreType.DMA((8,)),
                pltpu.SemaphoreType.DMA((8,)),
            ],
            compiler_params=pltpu.CompilerParams(
                collective_id=0, has_side_effects=True, vmem_limit_bytes=60 * 1024 * 1024
            ),
        )(residual.reshape(4, 8, 32, 512)).reshape(residual.shape)

    return jax.shard_map(
        local,
        mesh=mesh,
        in_specs=(P("gy", "gz", "gx"),),
        out_specs=P("gy", "gz", "gx"),
        check_vma=False,
    )
```

```python
import itertools

import jax
import jax.numpy as jnp
import numpy as np
from jax import lax
from jax.experimental import pallas as pl
from jax.experimental.pallas import tpu as pltpu
from jax.sharding import PartitionSpec as P

ORDER = 7
MID_ORDER = 3
COARSE_STEPS = 4


def legendre_pair(degree, points):
    previous = np.ones(points.shape)
    current = points.copy()
    for level in range(1, degree):
        following = ((2 * level + 1) * points * current - level * previous) / (level + 1)
        previous = current
        current = following
    return (current, previous)


def gll_table(degree):
    points = np.cos(np.pi * np.arange(degree + 1) / degree)
    for sweep in range(100):
        current, previous = legendre_pair(degree, points)
        points = points - (points * current - previous) / ((degree + 1) * current)
    points = points[::-1].copy()
    current, previous = legendre_pair(degree, points)
    weights = 2.0 / (degree * (degree + 1) * current**2)
    return (points, weights)


def lagrange_matrix(targets, points):
    point_count = len(points)
    matrix = np.ones((len(targets), point_count))
    for column in range(point_count):
        for partner in range(point_count):
            if partner != column:
                matrix[:, column] *= (targets - points[partner]) / (
                    points[column] - points[partner]
                )
    return matrix


def line_stiffness(degree):
    points, weights = gll_table(degree)
    point_count = len(points)
    barycentric = np.array(
        [
            1.0
            / np.prod(
                [
                    points[column] - points[partner]
                    for partner in range(point_count)
                    if partner != column
                ]
            )
            for column in range(point_count)
        ]
    )
    derivative = np.zeros((point_count, point_count))
    for target in range(point_count):
        for column in range(point_count):
            if target != column:
                derivative[target, column] = (
                    barycentric[column] / barycentric[target] / (points[target] - points[column])
                )
        derivative[target, target] = -np.sum(derivative[target])
    return (derivative.T @ (weights[:, None] * derivative), weights)


def assembled_patterns(degree):
    stiffness, weights = line_stiffness(degree)
    indices = np.arange(len(weights))
    diag_pat = stiffness[indices, indices].copy()
    weight_pat = weights.copy()
    row_pat = np.abs(stiffness).sum(axis=1)
    for pattern in (diag_pat, weight_pat, row_pat):
        shared = pattern[0] + pattern[-1]
        pattern[0] = shared
        pattern[-1] = shared
    return (diag_pat, weight_pat, row_pat)


def three_terms(special, weight_pat):
    return (
        special[:, None, None] * weight_pat[None, :, None] * weight_pat[None, None, :]
        + weight_pat[:, None, None] * special[None, :, None] * weight_pat[None, None, :]
        + weight_pat[:, None, None] * weight_pat[None, :, None] * special[None, None, :]
    )


def chebyshev_bound(degree):
    diag_pat, weight_pat, row_pat = assembled_patterns(degree)
    return float(np.max(three_terms(row_pat, weight_pat) / three_terms(diag_pat, weight_pat)))


class Level:
    def __init__(self, q):
        stiffness, weights = line_stiffness(q)
        diag_pat, weight_pat, row_pat = assembled_patterns(q)
        self.q = self.n = q
        self.half = half = (q + 1) // 2
        self.mass = weight_pat
        self.gain = gain = stiffness / weight_pat[:, None]
        self.even = 0.5 * (gain[:half, :half] + gain[:half, ::-1][:, :half])
        self.odd = 0.5 * (gain[:half, :half] - gain[:half, ::-1][:, :half])
        self.alpha = diag_pat / weight_pat
        upper = chebyshev_bound(q)
        lower = upper / 10.0
        self.center = 0.5 * (upper + lower)
        self.halfwidth = 0.5 * (upper - lower)

    def inverse(self, a, b, c):
        return 1.0 / (self.alpha[a] + self.alpha[b] + self.alpha[c])

    def factors(self, steps):
        scaled = self.center / self.halfwidth
        ratio = 1.0 / scaled
        found = []
        for step in range(1, steps):
            following = 1.0 / (2.0 * scaled - ratio)
            found.append((following * ratio, 2.0 * following / self.halfwidth))
            ratio = following
        return found


FINE, MID, LOW = Level(ORDER), Level(MID_ORDER), Level(1)
ALL_DIMS = "abc"
SUBSETS = ("a", "b", "c", "ab", "ac", "bc", "abc")
BLOCKS = [o for o in itertools.product((-1, 0, 1), repeat=3) if any(o)]


def node(dim, m, i, k):
    return {"a": (m, i, k), "b": (i, m, k), "c": (i, k, m)}[dim]


def face_vregs(n, dim):
    return 1 if dim == "c" else n * -(-n // 4)


def plan():
    slots, size, count = {}, 0, 0

    def add(key, length):
        nonlocal size, count
        slots[key] = (size, length, count)
        size += length
        count += 1

    for name, n in (
        ("f1", 7), ("f2", 7), ("f3", 7), ("f4", 7),
        ("m1", 3), ("m2", 3), ("m4", 3),
    ):
        for dim in ALL_DIMS:
            for way in (1, -1):
                add((name, dim, way), face_vregs(n, dim))
    for name, n, way in (("S7", 7, 1), ("S3", 3, 1), ("S1", 1, 1), ("C3", 3, -1), ("C7", 7, -1)):
        for dims in SUBSETS:
            add((name, dims, way), face_vregs(n, dims) if len(dims) == 1 else 1)
    for offset in BLOCKS:
        add(offset, 1)
    return slots, -(-size // 8) * 8, count


SLOTS, BUF_VREGS, MESSAGES = plan()


def total(terms):
    out = None
    for term in terms:
        if term is not None:
            out = term if out is None else out + term
    return out


def mix(coefs, values):
    return total(
        None if abs(coef) < 1e-13 else float(coef) * value for coef, value in zip(coefs, values)
    )


def kernel(sizes, x_hbm, out, x, tr, u, rho, d, ya, yb, yc, xs, w1, w2, ha, pk, sbuf, rbuf, ssem, rsem, xsem):
    nx, ny, nz = sizes
    gx, gy, gz = lax.axis_index("gx"), lax.axis_index("gy"), lax.axis_index("gz")
    rows = lax.broadcasted_iota(jnp.int32, (8, 128), 0)
    lanes = lax.broadcasted_iota(jnp.int32, (8, 128), 1)
    odd_row, odd_lane = rows % 2 == 1, lanes % 2 == 1
    first = {"a": rows < 2, "b": (rows % 2 == 0) & (lanes % 2 == 0), "c": lanes < 2}
    last = {"a": rows >= 6, "b": odd_row & odd_lane, "c": lanes >= 126}
    wall_a = jnp.where(first["a"] & (gy == 0), 0.0, 1.0).astype(jnp.float32)
    wall_b = jnp.where(first["b"] & (gz == 0), 0.0, 1.0).astype(jnp.float32)

    def spin(v, row, lane):
        if row % 8:
            v = pltpu.roll(v, row % 8, 0)
        if lane % 128:
            v = pltpu.roll(v, lane % 128, 1)
        return v

    def up(dim, v):
        if dim == "a":
            return jnp.where(rows >= 2, spin(v, 2, 0), 0.0)
        if dim == "b":
            w = jnp.where(odd_lane, jnp.where(odd_row, spin(v, 1, 0), 0.0), v)
            return jnp.where(odd_lane, spin(w, 0, 1), spin(w, 0, -1))
        t = jnp.where(lanes < 8, spin(v, 0, 10), spin(v, 0, 8))
        return jnp.where(lanes < 2, 0.0, t)

    def down(dim, v):
        if dim == "a":
            return jnp.where(rows < 6, spin(v, -2, 0), 0.0)
        if dim == "b":
            w = jnp.where(odd_lane, v, jnp.where(odd_row, 0.0, spin(v, -1, 0)))
            return jnp.where(odd_lane, spin(w, 0, 1), spin(w, 0, -1))
        t = jnp.where(lanes >= 120, spin(v, 0, -10), spin(v, 0, -8))
        return jnp.where(lanes >= 126, 0.0, t)

    def pack(dim, way, vs):
        acc = None
        for j, v in enumerate(vs):
            if dim == "a":
                v, mask = spin(v, 2 * j + (2 if way > 0 else 0), 0), rows // 2 == j
            elif dim == "b":
                js, jl = j % 2, j // 2
                back = 1 if way > 0 else 0
                v, mask = spin(v, js - back, jl - back), (rows % 2 == js) & (lanes % 2 == jl)
            else:
                v, mask = spin(v, 0, 2 * j + (2 if way > 0 else 0)), lanes // 2 == j
            acc = v if acc is None else jnp.where(mask, v, acc)
        return acc

    def unpack(dim, way, w, j):
        if dim == "a":
            w = spin(w, -2 * j if way > 0 else 6 - 2 * j, 0)
        elif dim == "b":
            js, jl = j % 2, j // 2
            w = spin(w, -js, -jl) if way > 0 else spin(w, 1 - js, 1 - jl)
        else:
            w = spin(w, 0, -2 * j if way > 0 else 126 - 2 * j)
        return jnp.where((first if way > 0 else last)[dim], w, 0.0)

    def move(dims, way, v):
        row = (2 if "a" in dims else 0) - (1 if "b" in dims else 0)
        lane = (2 if "c" in dims else 0) - (1 if "b" in dims else 0)
        mask = None
        for dim in dims:
            part = (first if way > 0 else last)[dim]
            mask = part if mask is None else mask & part
        return jnp.where(mask, spin(v, way * row, way * lane), 0.0)

    def guarded(key, way, run):
        if "a" in key[1]:
            pl.when(gy < ny - 1 if way > 0 else gy > 0)(run)
        else:
            run()

    def edge_spin(dims, way, v, j):
        return spin(v, way * j, 0) if dims == "ab" else spin(v, 0, way * 2 * j)

    def send_edge(name, dims, way, vs):
        acc = total(edge_spin(dims, way, move(dims, way, v), j) for j, v in enumerate(vs))
        put(sbuf, SLOTS[(name, dims, way)][0], acc)
        send((name, dims, way))

    def load_edge(name, dims, way, count):
        w = tile(rbuf, SLOTS[(name, dims, way)][0])
        mask = None
        for dim in dims:
            part = (first if way > 0 else last)[dim]
            mask = part if mask is None else mask & part
        return [jnp.where(mask, edge_spin(dims, -way, w, j), 0.0) for j in range(count)]

    def device_at(da, db, dc):
        return {
            "gx": lax.rem(gx + dc + nx, nx) if dc else gx,
            "gy": lax.rem(gy + da + ny, ny) if da else gy,
            "gz": lax.rem(gz + db + nz, nz) if db else gz,
        }

    def remote(src, dst, index, device):
        return pltpu.make_async_remote_copy(
            src_ref=src,
            dst_ref=dst,
            send_sem=ssem.at[index],
            recv_sem=rsem.at[index],
            device_id=device,
            device_id_type=pl.DeviceIdType.MESH,
        )

    def copy_of(key):
        name, dims, way = key
        offset, length, index = SLOTS[key]
        part = pl.ds(offset * 8, length * 8)
        device = device_at(*(way if dim in dims else 0 for dim in ALL_DIMS))
        return remote(sbuf.at[part], rbuf.at[part], index, device)

    pending = []

    def send(key):
        guarded(key, key[2], lambda: copy_of(key).start())
        pending.append(key)

    def receive(key):
        guarded(key, -key[2], lambda: copy_of(key).wait_recv())

    def drain(keep=None):
        for key in list(pending):
            if key[0] != keep:
                guarded(key, key[2], lambda: copy_of(key).wait_send())
                pending.remove(key)

    def tile(ref, index):
        start = index * 8
        if not isinstance(index, int):
            start = pl.multiple_of(start, 8)
        return ref[pl.ds(start, 8), :]

    def put(ref, index, value):
        start = index * 8
        if not isinstance(index, int):
            start = pl.multiple_of(start, 8)
        ref[pl.ds(start, 8), :] = value

    def sub(ref, base, length):
        start = base * 8
        if not isinstance(base, int):
            start = pl.multiple_of(start, 8)
        return ref.at[pl.ds(start, length * 8)]

    def line_view(ref, dim, i):
        if dim == "a":
            return sub(ref, i * 7, 301), lambda m, k: m * 49 + k
        return sub(ref, i * 49, 49), (lambda m, k: m * 7 + k) if dim == "b" else (
            lambda m, k: k * 7 + m
        )

    def by_class(i, values):
        picked = jnp.where((i == 2) | (i == 5), values[2], values[3])
        picked = jnp.where((i == 1) | (i == 6), values[1], picked)
        return jnp.where(i == 0, values[0], picked)

    def splat(value):
        return jnp.full((8, 128), value, jnp.float32)

    def inverse_slab(a):
        alpha = splat(by_class(a, [float(v) for v in FINE.alpha[:4]]))
        found = {}
        for b in range(4):
            for c in range(b, 4):
                found[(b, c)] = 1.0 / (alpha + float(FINE.alpha[b] + FINE.alpha[c]))
        return lambda b, c: found[tuple(sorted((min(b, 7 - b), min(c, 7 - c))))]

    def at7(t):
        return (t[0] * 7 + t[1]) * 7 + t[2]

    def at8(t):
        return (t[0] * 8 + t[1]) * 8 + t[2]

    def loop(count, body):
        def step(i, carry):
            body(i)
            return carry

        lax.fori_loop(0, count, step, 0)

    def line(lv, dim, v):
        q, half = lv.q, lv.half
        full = list(v) + [down(dim, v[0])]
        e = [full[j] + full[q - j] for j in range(half)]
        o = [full[j] - full[q - j] for j in range(half)]
        y = [None] * (q + 1)
        e = [v - e[0] for v in e[1:]]
        for i in range(half):
            ev, od = mix(lv.even[i][1:], e), mix(lv.odd[i], o)
            y[i] = od if ev is None else ev + od
            y[q - i] = -od if ev is None else ev - od
        own = jnp.where(first[dim], float(lv.gain[q, q]), 0.0)
        y[0] = y[0] + up(dim, y[q]) + own * v[0]
        return y[:q]

    def partial_end(lv, v):
        return mix(lv.gain[lv.q, : lv.q], v)

    def lower_line(hi, lo, v):
        jmat = lagrange_matrix(gll_table(hi.q)[0], gll_table(lo.q)[0])
        r = jmat.T * hi.mass[None, :] / lo.mass[:, None]
        inner = range(1, hi.half)
        e = [v[n] + v[hi.q - n] for n in inner]
        o = [v[n] - v[hi.q - n] for n in inner]
        y = [None] * (lo.q + 1)
        for m in range(lo.half):
            ev = mix([0.5 * (r[m, n] + r[m, hi.q - n]) for n in inner], e)
            od = mix([0.5 * (r[m, n] - r[m, hi.q - n]) for n in inner], o)
            y[m], y[lo.q - m] = ev + od, ev - od
        y[0] = y[0] + float(r[0, 0]) * v[0]
        return y

    def raise_line(hi, lo, v):
        jmat = lagrange_matrix(gll_table(hi.q)[0], gll_table(lo.q)[0])
        e = [v[m] + v[lo.q - m] for m in range(lo.half)]
        o = [v[m] - v[lo.q - m] for m in range(lo.half)]
        y = [None] * (hi.q + 1)
        y[0] = v[0]
        for n in range(1, hi.half):
            ev = mix([0.5 * (jmat[n, m] + jmat[n, lo.q - m]) for m in range(lo.half)], e)
            od = mix([0.5 * (jmat[n, m] - jmat[n, lo.q - m]) for m in range(lo.half)], o)
            y[n], y[hi.q - n] = ev + od, ev - od
        return y[: hi.q]


    def store_face(name, dim, way, n, get):
        offset = SLOTS[(name, dim, way)][0]
        if dim == "c":
            acc = None
            for i in range(n):
                w = pack(dim, way, [get(i, k) for k in range(n)])
                acc = w if acc is None else jnp.where(lanes // 8 == i, spin(w, 0, 8 * i), acc)
            put(sbuf, offset, acc)
        else:
            for i in range(n):
                put(sbuf, offset + i, pack(dim, way, [get(i, k) for k in range(n)]))
        send((name, dim, way))

    def load_face(name, dim, way, n):
        offset = SLOTS[(name, dim, way)][0]
        receive((name, dim, way))
        if dim == "c":
            w = tile(rbuf, offset)
            return [[unpack(dim, way, spin(w, 0, -8 * i), k) for k in range(n)] for i in range(n)]
        return [
            [unpack(dim, way, tile(rbuf, offset + i), k) for k in range(n)] for i in range(n)
        ]

    def small_apply(lv, name, dv):
        n = lv.n
        for dim in ALL_DIMS:
            store_face(name, dim, -1, n, lambda i, k: dv[node(dim, 0, i, k)])
            store_face(
                name, dim, 1, n,
                lambda i, k: partial_end(lv, [dv[node(dim, m, i, k)] for m in range(n)]),
            )
        y = {}
        for dim in ALL_DIMS:
            for i in range(n):
                for k in range(n):
                    got = line(lv, dim, [dv[node(dim, m, i, k)] for m in range(n)])
                    for m in range(n):
                        t = node(dim, m, i, k)
                        y[t] = got[m] if t not in y else y[t] + got[m]
        drain(name)
        for dim in "cba":
            before = load_face(name, dim, -1, n)
            after = load_face(name, dim, 1, n)
            for i in range(n):
                for k in range(n):
                    for m in range(n):
                        t = node(dim, m, i, k)
                        y[t] = y[t] + float(lv.gain[m, lv.q]) * before[i][k]
                    t = node(dim, 0, i, k)
                    y[t] = y[t] + after[i][k]
        return y

    def masked(t, v):
        if t[0] == 0:
            v = v * wall_a
        if t[1] == 0:
            v = v * wall_b
        return v

    def small_sum(lv, name, closed):
        n, q = lv.n, lv.q
        for dim in ALL_DIMS:
            for i in range(q + 1):
                for k in range(q + 1):
                    low, high = node(dim, 0, i, k), node(dim, q, i, k)
                    closed[low] = closed[low] + up(dim, closed[high])
        for dim in ALL_DIMS:
            store_face(name, dim, 1, n, lambda i, k: closed[node(dim, q, i, k)])
        for dims in SUBSETS[3:]:
            send_edge(name, dims, 1, [closed[t] for t in plane(dims, n, q)])
        drain(name)
        r = {t: closed[t] for t in itertools.product(range(n), repeat=3)}
        for dim in "cba":
            got = load_face(name, dim, 1, n)
            for i in range(n):
                for k in range(n):
                    t = node(dim, 0, i, k)
                    r[t] = r[t] + got[i][k]
        for dims in ("bc", "ab", "ac", "abc"):
            receive((name, dims, 1))
            places = plane(dims, n, 0)
            for t, v in zip(places, load_edge(name, dims, 1, len(places))):
                r[t] = r[t] + v
        return {t: masked(t, v) for t, v in r.items()}

    def plane(dims, n, end):
        ranges = [[end] if dim in dims else range(n) for dim in ALL_DIMS]
        return list(itertools.product(*ranges))

    def small_close(lv, name, v):
        n, q = lv.n, lv.q
        for dim in ALL_DIMS:
            store_face(name, dim, -1, n, lambda i, k: v[node(dim, 0, i, k)])
        for dims in SUBSETS[3:]:
            send_edge(name, dims, -1, [v[t] for t in plane(dims, n, 0)])
        drain(name)
        halo = {}
        for dim in "cba":
            got = load_face(name, dim, -1, n)
            for i in range(n):
                for k in range(n):
                    halo[(dim, node(dim, q, i, k))] = got[i][k]
        for dims in SUBSETS[3:]:
            receive((name, dims, -1))
            places = plane(dims, n, q)
            for t, got in zip(places, load_edge(name, dims, -1, len(places))):
                halo[(dims, t)] = got
        return closure(lv, dict(v), halo)

    def closure(lv, field, halo):
        n, q = lv.n, lv.q

        def value(have, t):
            ends = "".join(dim for dim, i in zip(ALL_DIMS, t) if i == q and dim not in have)
            if not ends:
                return halo[(have, t)] if have else field[t]
            dim = ends[0]
            low = tuple(0 if d == dim else i for d, i in zip(ALL_DIMS, t))
            with_dim = "".join(d for d in ALL_DIMS if d in have or d == dim)
            return down(dim, value(have, low)) + value(with_dim, t)

        return {t: value("", t) for t in itertools.product(range(q + 1), repeat=3)}

    def first_step(lv, r):
        return {t: float(lv.inverse(*t) / lv.center) * v for t, v in r.items()}

    def next_step(lv, factor, dv, r):
        keep, gain = factor
        return {t: float(keep) * dv[t] + float(gain * lv.inverse(*t)) * r[t] for t in r}

    def subtract(r, y):
        return {t: masked(t, r[t] - y[t]) for t in r}

    def add(*fields):
        return {t: total(f[t] for f in fields) for t in fields[0]}

    for an in (7, 0, 1, 2, 3, 4, 5, 6):
        pltpu.make_async_copy(x_hbm.at[:, an], x.at[:, an], xsem.at[an]).start()

    def zero_block(i):
        rbuf[pl.ds(pl.multiple_of(i * 64, 64), 64), :] = jnp.zeros((64, 128), jnp.float32)

    loop(BUF_VREGS // 8, zero_block)

    for offset in BLOCKS:
        pl.semaphore_signal(
            pltpu.get_barrier_semaphore(),
            inc=1,
            device_id=device_at(*offset),
            device_id_type=pl.DeviceIdType.MESH,
        )

    def butterfly(vs):
        for bit in (1, 2, 4):
            new = list(vs)
            low = (lanes // bit) % 2 == 0
            for i in range(8):
                if not i & bit:
                    lo, hi = vs[i], vs[i + bit]
                    new[i] = jnp.where(low, lo, spin(hi, 0, bit))
                    new[i + bit] = jnp.where(low, spin(lo, 0, -bit), hi)
            vs = new
        return vs

    def enter(an):
        to = sub(tr, an * 64, 64)
        for ael in range(4):
            for b_hi in range(2):
                vs = [
                    x[ael, an, pl.ds((2 * b_hi + g % 2) * 8, 8), pl.ds((g // 2) * 128, 128)]
                    for g in range(8)
                ]
                for cn, v in enumerate(butterfly(vs)):
                    put(to, cn * 8 + ael * 2 + b_hi, v)

    def by_nodes(bn, cn):
        return pl.ds(cn * 64 + bn, 8, stride=8)

    def slab(a):
        at = sub(tr, a * 64, 64)
        to = sub(u, a * 64, 64)
        v = {(b, c): at[by_nodes(b, c), :] for b in range(8) for c in range(8)}
        for c in range(8):
            v[(0, c)] = v[(0, c)] + up("b", v[(7, c)])
        for b in range(8):
            v[(b, 0)] = v[(b, 0)] + up("c", v[(b, 7)])
        for (b, c), value in v.items():
            put(to, b * 8 + c, value)

    fetch = [
        pltpu.make_async_copy(x_hbm.at[:, an], x.at[:, an], xsem.at[an]) for an in range(8)
    ]

    def face_row(name, dim, way, i, vs):
        offset = SLOTS[(name, dim, way)][0]
        if dim == "c":
            put(pk, i if way > 0 else i + 7, pack(dim, way, vs))
        else:
            to = sub(sbuf, offset + 2 * i, 2)
            put(to, 0, pack(dim, way, vs[:4]))
            put(to, 1, pack(dim, way, vs[4:]))

    def send_face(name, dim, way):
        if dim == "c":
            base = 0 if way > 0 else 7
            acc = tile(pk, base)
            for i in range(1, 7):
                acc = jnp.where(lanes // 16 == i, spin(tile(pk, base + i), 0, 16 * i), acc)
            put(sbuf, SLOTS[(name, dim, way)][0], acc)
        send((name, dim, way))

    def spread_c(name, way, base):
        w = tile(rbuf, SLOTS[(name, "c", way)][0])
        for i in range(7):
            put(pk, base + i, spin(w, 0, -16 * i))

    def fine_row(name, dim, way, i, base):
        if dim == "c":
            w = tile(pk, base + i)
            return [unpack(dim, way, w, k) for k in range(7)]
        offset = SLOTS[(name, dim, way)][0]
        at = sub(rbuf, offset + 2 * i, 2)
        lo, hi = tile(at, 0), tile(at, 1)
        return [unpack(dim, way, lo if k < 4 else hi, k % 4) for k in range(7)]

    def start_sum(dims):
        if len(dims) > 1:
            send_edge("S7", dims, 1, [tile(u, at8(t)) for t in plane(dims, 7, 7)])
            return
        for i in range(7):
            face_row("S7", dims, 1, i, [tile(u, at8(node(dims, 7, i, k))) for k in range(7)])
        send_face("S7", dims, 1)

    fetch[7].wait()
    enter(7)
    slab(7)
    pl.semaphore_wait(pltpu.get_barrier_semaphore(), len(BLOCKS))
    for dims in ("a", "ab", "ac", "abc"):
        start_sum(dims)
    for an in range(7):
        fetch[an].wait()
    loop(7, enter)
    loop(7, slab)
    for b in range(8):
        for c in range(8):
            t = at8((0, b, c))
            put(u, t, tile(u, t) + up("a", tile(u, at8((7, b, c)))))
    for dims in ("c", "b", "bc"):
        start_sum(dims)

    for dims in ("c", "b", "a", "bc", "ac", "ab", "abc"):
        key = ("S7", dims, 1)
        receive(key)
        if dims == "c":
            spread_c("S7", 1, 0)
        elif dims == "a":
            for i in range(7):
                got = fine_row("S7", "a", 1, i, 0)
                for k in range(7):
                    t = at8((0, i, k))
                    put(u, t, tile(u, t) + got[k])
        elif len(dims) > 1:
            places = plane(dims, 7, 0)
            for t, v in zip(places, load_edge("S7", dims, 1, len(places))):
                put(u, at8(t), tile(u, at8(t)) + v)

    def first_fine(a):
        wall = jnp.where(a == 0, wall_a, 1.0)
        from_u, to_rho, to_d = sub(u, a * 64, 64), sub(rho, a * 49, 49), sub(d, a * 49, 49)
        mass_a = by_class(a, [float(1.0 / v) for v in FINE.mass[:4]])
        inverse = inverse_slab(a)
        b_after = fine_row("S7", "b", 1, a, 0)
        c_after = fine_row("S7", "c", 1, a, 0)
        for b in range(7):
            for c in range(7):
                r = tile(from_u, b * 8 + c)
                if b == 0:
                    r = r + b_after[c]
                if c == 0:
                    r = r + c_after[b]
                r = r * (float(1.0 / (FINE.mass[b] * FINE.mass[c])) * mass_a) * wall
                if b == 0:
                    r = r * wall_b
                put(to_rho, b * 7 + c, r)
                put(to_d, b * 7 + c, (inverse(b, c) * float(1.0 / FINE.center)) * r)

    loop(7, first_fine)

    def fine_apply(name, after):
        for dims in ("a", "bc"):

            def faces(i):
                for dim in dims:
                    at, place = line_view(d, dim, i)
                    vs = [[tile(at, place(m, k)) for m in range(7)] for k in range(7)]
                    face_row(name, dim, -1, i, [v[0] for v in vs])
                    face_row(name, dim, 1, i, [partial_end(FINE, v) for v in vs])

            loop(7, faces)
            for dim in dims:
                send_face(name, dim, -1)
                send_face(name, dim, 1)

        def lines(i):
            for dim, y in zip(ALL_DIMS, (ya, yb, yc)):
                at, place = line_view(d, dim, i)
                to, _ = line_view(y, dim, i)
                for k in range(7):
                    got = line(FINE, dim, [tile(at, place(m, k)) for m in range(7)])
                    for m in range(7):
                        put(to, place(m, k), got[m])

        loop(7, lines)

        drain(name)
        for dim in "cba":
            for way in (1, -1):
                receive((name, dim, way))
        spread_c(name, 1, 0)
        spread_c(name, -1, 7)
        for i in range(7):
            got = fine_row(name, "a", -1, i, 0)
            add0 = fine_row(name, "a", 1, i, 0)
            for k in range(7):
                put(ha, i * 7 + k, got[k])
                t = at7((0, i, k))
                put(ya, t, tile(ya, t) + add0[k])

        def finish(a):
            wall = jnp.where(a == 0, wall_a, 1.0)
            gain_a = float(FINE.gain[6, 7])
            for m in range(6):
                gain_a = jnp.where(a == m, float(FINE.gain[m, 7]), gain_a)
            gain_a = splat(gain_a)
            inverse = inverse_slab(a)
            b_before = fine_row(name, "b", -1, a, 0)
            b_after = fine_row(name, "b", 1, a, 0)
            c_before = fine_row(name, "c", -1, a, 7)
            c_after = fine_row(name, "c", 1, a, 0)
            at_rho, at_d, at_x = sub(rho, a * 49, 49), sub(d, a * 49, 49), sub(xs, a * 64, 64)
            at_y = [sub(y, a * 49, 49) for y in (ya, yb, yc)]
            for b in range(7):
                for c in range(7):
                    t, t8 = b * 7 + c, b * 8 + c
                    y = total(tile(part, t) for part in at_y) + gain_a * tile(ha, t)
                    y = y + float(FINE.gain[b, 7]) * b_before[c]
                    y = y + float(FINE.gain[c, 7]) * c_before[b]
                    if b == 0:
                        y = y + b_after[c]
                    if c == 0:
                        y = y + c_after[b]
                    r = (tile(at_rho, t) - y) * wall
                    if b == 0:
                        r = r * wall_b
                    put(at_rho, t, r)
                    if after is None:
                        continue
                    old = tile(at_d, t)
                    if after == "lift":
                        put(at_x, t8, tile(at_x, t8) + old)
                        put(at_d, t, (inverse(b, c) * float(1.0 / FINE.center)) * r)
                        continue
                    new = float(fine_keep) * old + (inverse(b, c) * float(fine_gain)) * r
                    if after == "first":
                        put(at_x, t8, old + new)
                        put(at_d, t, new)
                    else:
                        put(at_x, t8, tile(at_x, t8) + old + new)

        finish(0)
        if after == "post":
            for dims in ("a", "ab", "ac", "abc"):
                start_close(dims)
        loop(6, lambda a: finish(a + 1))

    def start_close(dims):
        if len(dims) > 1:
            send_edge("C7", dims, -1, [tile(xs, at8(t)) for t in plane(dims, 7, 0)])
            return
        for i in range(7):
            face_row("C7", dims, -1, i, [tile(xs, at8(node(dims, 0, i, k))) for k in range(7)])
        send_face("C7", dims, -1)

    fine_keep, fine_gain = FINE.factors(2)[0]
    fine_apply("f1", "first")
    fine_apply("f2", None)

    def lower_a(b):
        at, place = line_view(rho, "a", b)
        to = sub(w1, b * 7, 154)
        for c in range(7):
            got = lower_line(FINE, MID, [tile(at, place(m, c)) for m in range(7)])
            for m in range(4):
                put(to, m * 49 + c, got[m])

    loop(7, lower_a)

    def lower_b(a):
        at, to = sub(w1, a * 49, 49), sub(w2, a * 28, 28)
        for c in range(7):
            got = lower_line(FINE, MID, [tile(at, m * 7 + c) for m in range(7)])
            for m in range(4):
                put(to, m * 7 + c, got[m])

    loop(4, lower_b)
    closed = {}
    for a in range(4):
        for b in range(4):
            got = lower_line(FINE, MID, [tile(w2, (a * 4 + b) * 7 + m) for m in range(7)])
            for m in range(4):
                closed[(a, b, m)] = got[m]
    r3 = small_sum(MID, "S3", closed)

    mid_factor = MID.factors(2)[0]
    d3 = first_step(MID, r3)
    r3 = subtract(r3, small_apply(MID, "m1", d3))
    e3 = next_step(MID, mid_factor, d3, r3)
    x3 = add(d3, e3)
    r3 = subtract(r3, small_apply(MID, "m2", e3))

    closed = r3
    for dim in ALL_DIMS:
        new = {}
        others = sorted({tuple(i for dd, i in zip(ALL_DIMS, t) if dd != dim) for t in closed})
        for i, k in others:
            got = lower_line(MID, LOW, [closed[node(dim, m, i, k)] for m in range(3)])
            for m in range(2):
                new[node(dim, m, i, k)] = got[m]
        closed = new
    r1 = small_sum(LOW, "S1", closed)
    here = (0, 0, 0)
    origin = SLOTS[BLOCKS[0]][0]
    put(sbuf, origin, r1[here])

    def block_copy(offset):
        place, _, index = SLOTS[offset]
        src, dst = sbuf.at[pl.ds(origin * 8, 8)], rbuf.at[pl.ds(place * 8, 8)]
        return remote(src, dst, index, device_at(*offset))

    def block_copies(way, act):
        for step in (1, 0, -1):
            group = [o for o in BLOCKS if o[0] == step]

            def run():
                for offset in group:
                    act(block_copy(offset))

            if step:
                pl.when(gy < ny - 1 if step * way > 0 else gy > 0)(run)
            else:
                run()

    block_copies(1, lambda copy: copy.start())
    drain()
    block_copies(-1, lambda copy: copy.wait_recv())
    r = {here: r1[here]}
    for offset in BLOCKS:
        r[tuple(-o for o in offset)] = tile(rbuf, SLOTS[offset][0])

    def up_full(dim, v, before):
        if dim == "a":
            return spin(jnp.where(last["a"], before, v), 2, 0)
        if dim == "b":
            w = jnp.where(odd_lane, jnp.where(odd_row, spin(v, 1, 0), spin(before, -1, 0)), v)
            return jnp.where(odd_lane, spin(w, 0, 1), spin(w, 0, -1))
        t = jnp.where(lanes < 8, spin(v, 0, 10), spin(v, 0, 8))
        return jnp.where(lanes < 2, spin(before, 0, 2), t)

    def down_full(dim, v, after):
        if dim == "a":
            return spin(jnp.where(first["a"], after, v), -2, 0)
        if dim == "b":
            w = jnp.where(odd_lane, v, jnp.where(odd_row, spin(after, 1, 0), spin(v, -1, 0)))
            return jnp.where(odd_lane, spin(w, 0, 1), spin(w, 0, -1))
        t = jnp.where(lanes >= 120, spin(v, 0, -10), spin(v, 0, -8))
        return jnp.where(lanes >= 126, spin(after, 0, -2), t)

    def beside(dim, o, step):
        return tuple(i + step if d == dim else i for d, i in zip(ALL_DIMS, o))

    def both_sides(dim, f, o):
        before, after = f.get(beside(dim, o, -1), f[o]), f.get(beside(dim, o, 1), f[o])
        return up_full(dim, f[o], before) + down_full(dim, f[o], after)

    walls_a, walls_b = {}, {}
    for step in (-1, 0, 1):
        at_a, at_b = lax.rem(gy + step + ny, ny) == 0, lax.rem(gz + step + nz, nz) == 0
        walls_a[step] = jnp.where(first["a"] & at_a, 0.0, 1.0).astype(jnp.float32)
        walls_b[step] = jnp.where(first["b"] & at_b, 0.0, 1.0).astype(jnp.float32)

    own_low = 3.0 * float(LOW.gain[0, 0] + LOW.gain[1, 1])
    side_low = float(LOW.gain[0, 1])
    inverse_low = float(LOW.inverse(0, 0, 0))
    dl = {o: (inverse_low / LOW.center) * v for o, v in r.items()}
    x1 = dict(dl)
    for keep, gain in LOW.factors(COARSE_STEPS):
        new = {}
        for o in r:
            sides = total(both_sides(dim, dl, o) for dim in ALL_DIMS)
            left = r[o] - (own_low * dl[o] + side_low * sides)
            new[o] = left * (walls_a[o[0]] * walls_b[o[1]])
        r = new
        dl = {o: float(keep) * dl[o] + float(gain * inverse_low) * r[o] for o in r}
        x1 = add(x1, dl)

    def corners(f, dims):
        for dim in dims:
            new = {}
            for o, v in f.items():
                new[o] = v if o[ALL_DIMS.index(dim)] == 0 else None
            for o in f:
                if new[o] is None:
                    low = beside(dim, o, -1)
                    new[o] = down_full(dim, f[low], f[o])
            f = new
        return f

    def lift_low(f, dims):
        for dim in dims:
            new = {}
            rest = sorted({tuple(i for d, i in zip(ALL_DIMS, t) if d != dim) for t in f})
            for i, k in rest:
                got = raise_line(MID, LOW, [f[node(dim, m, i, k)] for m in range(2)])
                for m in range(3):
                    new[node(dim, m, i, k)] = got[m]
            f = new
        return f

    ends = list(itertools.product((0, 1), repeat=3))
    c3 = lift_low(corners({o: x1[o] for o in ends}, ALL_DIMS), "cba")
    y = {t: None for t in c3}
    for dim in ALL_DIMS:
        at = ALL_DIMS.index(dim)
        rest = ALL_DIMS.replace(dim, "")
        f = {}
        for o in ends:
            if o[at] == 0:
                f[o] = (x1[o] - 0.5 * both_sides(dim, x1, o)) * float(1.0 / MID.mass[0])
        for t, v in lift_low(corners(f, rest), rest).items():
            y[t] = v if y[t] is None else y[t] + v
    r3 = {t: masked(t, v if y[t] is None else v - y[t]) for t, v in r3.items()}
    d3 = first_step(MID, r3)
    r3 = subtract(r3, small_apply(MID, "m4", d3))
    e3 = next_step(MID, mid_factor, d3, r3)
    t3 = small_close(MID, "C3", add(x3, c3, d3, e3))

    for a in range(4):
        for b in range(4):
            got = raise_line(FINE, MID, [t3[(a, b, m)] for m in range(4)])
            for m in range(7):
                put(w2, (a * 4 + b) * 7 + m, got[m])

    def raise_b(a):
        at, to = sub(w2, a * 28, 28), sub(w1, a * 49, 49)
        for c in range(7):
            got = raise_line(FINE, MID, [tile(at, m * 7 + c) for m in range(4)])
            for m in range(7):
                put(to, m * 7 + c, got[m])

    loop(4, raise_b)

    def raise_a(b):
        at = sub(w1, b * 7, 154)
        to, place = line_view(d, "a", b)
        for c in range(7):
            got = raise_line(FINE, MID, [tile(at, m * 49 + c) for m in range(4)])
            for m in range(7):
                put(to, place(m, c), got[m])

    loop(7, raise_a)
    fine_apply("f3", "lift")
    fine_apply("f4", "post")

    for dims in ("b", "c", "bc"):
        start_close(dims)

    def leave_nodes(a):
        at, to = sub(xs, a * 64, 64), sub(tr, a * 64, 64)
        for b in range(8):
            for c in range(8):
                to[by_nodes(b, c), :] = tile(at, b * 8 + c)

    def leave(an):
        at = sub(tr, an * 64, 64)
        for ael in range(4):
            for b_hi in range(2):
                vs = butterfly([tile(at, cn * 8 + ael * 2 + b_hi) for cn in range(8)])
                for g, v in enumerate(vs):
                    b_at, c_at = pl.ds((2 * b_hi + g % 2) * 8, 8), pl.ds((g // 2) * 128, 128)
                    out[ael * 8 + an, b_at, c_at] = v

    def end_face(dim):
        for i in range(7):
            got = fine_row("C7", dim, -1, i, 0)
            for k in range(7):
                value = down(dim, tile(xs, at8(node(dim, 0, i, k)))) + got[k]
                put(xs, at8(node(dim, 7, i, k)), value)

    for dims in ("b", "c", "bc"):
        receive(("C7", dims, -1))
    spread_c("C7", -1, 0)
    end_face("b")
    end_face("c")
    hb = fine_row("C7", "b", -1, 0, 0)
    hc_a = fine_row("C7", "c", -1, 0, 0)
    hc_b = [fine_row("C7", "c", -1, i, 0)[0] for i in range(7)]
    edge_bc = load_edge("C7", "bc", -1, 7)
    for k in range(7):
        value = down("c", tile(xs, at8((k, 7, 0)))) + down("b", hc_b[k]) + edge_bc[k]
        put(xs, at8((k, 7, 7)), value)
    loop(7, leave_nodes)
    loop(7, leave)

    for dims in ("a", "ab", "ac", "abc"):
        receive(("C7", dims, -1))
    end_face("a")
    edge_ab, edge_ac = load_edge("C7", "ab", -1, 7), load_edge("C7", "ac", -1, 7)
    for k in range(7):
        value = down("b", tile(xs, at8((7, 0, k)))) + down("a", hb[k]) + edge_ab[k]
        put(xs, at8((7, 7, k)), value)
        value = down("c", tile(xs, at8((7, k, 0)))) + down("a", hc_a[k]) + edge_ac[k]
        put(xs, at8((7, k, 7)), value)
    value = down("c", tile(xs, at8((7, 7, 0)))) + down("b", down("a", hc_a[0]))
    value = value + down("b", edge_ac[0]) + down("a", edge_bc[0])
    put(xs, at8((7, 7, 7)), value + load_edge("C7", "abc", -1, 1)[0])
    leave_nodes(7)
    leave(7)
    drain()
    block_copies(1, lambda copy: copy.wait_send())


def solution(mesh):
    sizes = tuple(mesh.shape[axis] for axis in ("gx", "gy", "gz"))

    def body(*refs):
        kernel(sizes, *refs)

    def local(residual):
        vmem = lambda count: pltpu.VMEM((count * 8, 128), jnp.float32)
        return pl.pallas_call(
            body,
            out_shape=jax.ShapeDtypeStruct(residual.shape, jnp.float32),
            in_specs=[
                pl.BlockSpec(memory_space=pl.ANY),
            ],
            out_specs=pl.BlockSpec(memory_space=pltpu.VMEM),
            scratch_shapes=[
                pltpu.VMEM((4, 8, 32, 512), jnp.float32),
                vmem(512),
                vmem(512),
                vmem(343),
                vmem(343),
                vmem(343),
                vmem(343),
                vmem(343),
                vmem(512),
                vmem(196),
                vmem(112),
                vmem(49),
                vmem(16),
                vmem(BUF_VREGS),
                vmem(BUF_VREGS),
                pltpu.SemaphoreType.DMA((MESSAGES,)),
                pltpu.SemaphoreType.DMA((MESSAGES,)),
                pltpu.SemaphoreType.DMA((8,)),
            ],
            compiler_params=pltpu.CompilerParams(
                collective_id=0, has_side_effects=True, vmem_limit_bytes=40 * 1024 * 1024
            ),
        )(residual.reshape(4, 8, 32, 512))

    return jax.shard_map(
        local,
        mesh=mesh,
        in_specs=(P("gy", "gz", "gx"),),
        out_specs=P("gy", "gz", "gx"),
        check_vma=False,
    )
```
